32 devices in a mesh: dp: 8 (over y, x, core), tensor: 4 (over z).
Axes of the slice: x: 2, y: 2, z: 4, core: 2. Of those that a mesh axis runs over, the one named last changes fastest.
Arguments:
- tokens: bfloat16 [16, 1024, 1152], P('dp', 'tensor'), may hold values from -6 to 6
- conditioning: float32 [16, 1152], P('dp'), may hold values from -12 to 12
- cotangent: bfloat16 [16, 1024, 1152], P('dp', 'tensor'), may hold values from -6 to 6
- query_weight: bfloat16 [1152, 1152], P('dp', 'tensor'), may hold values from -0.20623948 to 0.20623948
- key_weight: bfloat16 [1152, 1152], P('dp', 'tensor'), may hold values from -0.1875 to 0.1875
- value_weight: bfloat16 [1152, 1152], P('dp', 'tensor'), may hold values from -0.1875 to 0.1875
- out_weight: bfloat16 [1152, 1152], P('tensor', 'dp'), may hold values from -1 to 1
- up_weight: bfloat16 [1152, 4608], P('dp', 'tensor'), may hold values from -0.1875 to 0.1875
- down_weight: bfloat16 [4608, 1152], P('tensor', 'dp'), may hold values from -0.09375 to 0.09375
- ada_weight: bfloat16 [1152, 6912], P('dp', 'tensor'), may hold values from -0.109375 to 0.109375
- query_bias: float32 [1152], P('tensor'), may hold values from -3 to 3
- value_bias: float32 [1152], P('tensor'), may hold values from -3 to 3
- out_bias: float32 [1152], replicated, may hold values from -3 to 3
- up_bias: float32 [4608], P('tensor'), may hold values from -3 to 3
- down_bias: float32 [1152], replicated, may hold values from -3 to 3
- ada_bias: float32 [6912], P('tensor'), may hold values from -1.2 to 1.2
- threshold: float32 [1], replicated, may hold values from 0.5 to 1.5
Outputs:
- block_out: bfloat16 [16, 1024, 1152], P('dp', 'tensor')
- grad_tokens: float32 [16, 1024, 1152], P('dp', 'tensor')
- grad_conditioning: float32 [16, 1152], P('dp')
- grad_query_weight: float32 [1152, 1152], P('dp', 'tensor')
- grad_key_weight: float32 [1152, 1152], P('dp', 'tensor')
- grad_value_weight: float32 [1152, 1152], P('dp', 'tensor')
- grad_out_weight: float32 [1152, 1152], P('tensor', 'dp')
- grad_up_weight: float32 [1152, 4608], P('dp', 'tensor')
- grad_down_weight: float32 [4608, 1152], P('tensor', 'dp')
- grad_ada_weight: float32 [1152, 6912], P('dp', 'tensor')
- grad_query_bias: float32 [1152], P('tensor')
- grad_value_bias: float32 [1152], P('tensor')
- grad_out_bias: float32 [1152], replicated
- grad_up_bias: float32 [4608], P('tensor')
- grad_down_bias: float32 [1152], replicated
- grad_ada_bias: float32 [6912], P('tensor')
- query_clipped: bfloat16 [1152, 1152], P('dp', 'tensor')
- key_clipped: bfloat16 [1152, 1152], P('dp', 'tensor')
- query_bias_clipped: float32 [1152], P('tensor')
The draws below stay inside these ranges and needn't reach their ends.
All inputs are finite; a program needn't handle non-finite values.
Results may differ from the reference program's by a relative error of at most 0.0131.
The reference program's roundings to bfloat16 on the way count: a program that leaves them out, or rounds other values in their place, can miss the bound.
Values may be sent and summed in bfloat16 or wider, within the bound.
A program may use at most 192 MiB of HBM per device.

```python
import jax
import jax.numpy as jnp
from jax import lax

D = 1152
HEADS = 16
HEAD_DIM = 72
FF = 4608
SEQ = 1024
IMAGES = 16


def draw_conditioning(key, part):
    key = jax.random.fold_in(key, 11)
    position = jnp.arange(IMAGES, dtype=jnp.float32)[:, None]
    rising = 1.0 + 2.0 * position / max(IMAGES - 1, 1)
    entries = jnp.clip(jax.random.normal(key, (IMAGES, D), jnp.float32), -4.0, 4.0)
    return entries * rising


def draw_query_weight(key, part):
    key = jax.random.fold_in(key, 21)
    order_key = jax.random.fold_in(key, 22)
    ranks = jax.random.permutation(order_key, HEADS).astype(jnp.float32)
    levels = 2.0 ** (1.6 * ranks / max(HEADS - 1, 1) - 0.8)
    column_scale = jnp.repeat(levels, HEAD_DIM)[None, :]
    entries = jnp.clip(jax.random.normal(key, (D, D), jnp.float32), -4.0, 4.0)
    return (entries * column_scale * D ** (-0.5)).astype(jnp.bfloat16)


def block_levels(rng, extent, shards, low, high):
    def one(axis_at, parts):
        heights = jax.random.uniform(jax.random.fold_in(jax.random.fold_in(rng, 6), axis_at), (parts,), jnp.float32, low / len(shards), high / len(shards))
        return jnp.repeat(jnp.exp(heights), extent[axis_at] // parts).reshape((-1,) + (1,) * (len(extent) - axis_at - 1))

    level = one(*shards[0])
    for cut in shards[1:]:
        level = level * one(*cut)
    return level


def scatter_about(stream_key, shape, scale, bound, split=(), held_as=jnp.bfloat16):
    values = scale * jax.random.normal(stream_key, shape, jnp.float32)
    if split:
        values = values * block_levels(stream_key, shape, split, -0.22, 0.18)
    return jnp.clip(values, -bound, bound).astype(held_as)


def setup_inputs(seed: int = 0) -> dict:
    splits = jax.random.split(jax.random.key(seed), 18)
    return {
        "tokens": scatter_about(splits[0], (IMAGES, SEQ, D), 1.0, 6.0, ((0, 8), (1, 4))),
        "conditioning": draw_conditioning(jax.random.fold_in(splits[17], 71), 0),
        "cotangent": scatter_about(splits[2], (IMAGES, SEQ, D), 1.0, 6.0, ((0, 8), (1, 4))),
        "query_weight": draw_query_weight(jax.random.fold_in(splits[17], 71), 0),
        "key_weight": scatter_about(splits[4], (D, D), D ** -0.5, 0.1875, ((0, 8), (1, 4))),
        "value_weight": scatter_about(splits[5], (D, D), D ** -0.5, 0.1875, ((0, 8), (1, 4))),
        "out_weight": scatter_about(splits[6], (D, D), (D // 32) ** -0.5, 1.0, ((0, 4), (1, 8))),
        "up_weight": scatter_about(splits[7], (D, FF), D ** -0.5, 0.1875, ((0, 8), (1, 4))),
        "down_weight": scatter_about(splits[8], (FF, D), FF ** -0.5, 0.09375, ((0, 4), (1, 8))),
        "ada_weight": scatter_about(splits[9], (D, 6 * D), (3 * D) ** -0.5, 0.109375, ((0, 8), (1, 4))),
        "query_bias": scatter_about(splits[10], (D,), 0.5, 3.0, ((0, 4),), jnp.float32),
        "value_bias": scatter_about(splits[11], (D,), 0.5, 3.0, ((0, 4),), jnp.float32),
        "out_bias": scatter_about(splits[12], (D,), 0.5, 3.0, (), jnp.float32),
        "up_bias": scatter_about(splits[13], (FF,), 0.5, 3.0, ((0, 4),), jnp.float32),
        "down_bias": scatter_about(splits[14], (D,), 0.5, 3.0, (), jnp.float32),
        "ada_bias": scatter_about(splits[15], (6 * D,), 0.2, 1.2, ((0, 4),), jnp.float32),
        "threshold": jnp.clip(jax.random.uniform(splits[16], (1,), jnp.float32, 0.5, 1.5), 0.5, 1.5),
    }


@jax.custom_vjp
def low(v):
    return lax.optimization_barrier(v.astype(jnp.bfloat16)).astype(jnp.float32)

@jax.custom_vjp
def low_back(v):
    return v

def low_keep(v):
    return (low(v), None)

def low_pass(kept, grad):
    return (grad,)

def back_keep(v):
    return (v, None)

def back_low(kept, grad):
    return (low(grad),)
low.defvjp(low_keep, low_pass)
low_back.defvjp(back_keep, back_low)
epsilon = 1e-06

def round_both(value):
    return low(low_back(value))

def matmul(left, right):
    return jnp.matmul(left, right, precision=lax.Precision.HIGHEST)

def modulate(values, shift, scale):
    average = lax.optimization_barrier(jnp.mean(values, axis=-1, keepdims=True))
    centred = values - average
    spread = lax.optimization_barrier(jnp.mean(centred * centred, axis=-1, keepdims=True))
    return centred * lax.rsqrt(spread + epsilon) * (1.0 + scale[:, None, :]) + shift[:, None, :]

def image_layer(token_img, cond_img, params):
    query_weight, key_weight, value_weight, out_weight, up_weight, down_weight, ada_weight, query_bias, value_bias, out_bias, up_bias, down_bias, ada_bias = params
    modulation = low_back(matmul(low(jax.nn.silu(cond_img)), ada_weight) + ada_bias)
    pieces = [modulation[:, piece_index * D:(piece_index + 1) * D] for piece_index in range(6)]
    shift_attn, scale_attn, gate_attn, shift_mlp, scale_mlp, gate_mlp = pieces
    normed_attn = low(modulate(token_img, shift_attn, scale_attn))
    queries = round_both(matmul(normed_attn, query_weight) + query_bias)
    key_rows = round_both(matmul(normed_attn, key_weight))
    value_rows = round_both(matmul(normed_attn, value_weight) + value_bias)
    count = token_img.shape[0]
    shape_heads = (count, SEQ, HEADS, HEAD_DIM)
    scores = low_back(jnp.einsum('gqhe,gkhe->ghqk', queries.reshape(shape_heads), key_rows.reshape(shape_heads), precision=lax.Precision.HIGHEST) * HEAD_DIM ** (-0.5))
    head_peak = lax.optimization_barrier(jnp.max(scores, axis=(0, 2, 3)))
    probs = jax.nn.softmax(scores, axis=-1)
    attended = round_both(jnp.einsum('ghqk,gkhe->gqhe', low(probs), value_rows.reshape(shape_heads), precision=lax.Precision.HIGHEST)).reshape(count, SEQ, D)
    branch_attn = low_back(matmul(attended, out_weight) + out_bias)
    after_attn = token_img + gate_attn[:, None, :] * branch_attn
    normed_mlp = low(modulate(after_attn, shift_mlp, scale_mlp))
    upward = low_back(matmul(normed_mlp, up_weight) + up_bias)
    active = low(jax.nn.gelu(upward, approximate=True))
    branch_mlp = low_back(matmul(active, down_weight) + down_bias)
    return (after_attn + gate_mlp[:, None, :] * branch_mlp, head_peak)

def forward(tokens, conditioning, *params):

    def one_image(running, bundle):
        token_img, cond_img = bundle
        out_img, peak_img = jax.checkpoint(image_layer)(token_img[None], cond_img[None], params)
        return (running, (out_img[0], peak_img))
    _, (outputs, peaks) = lax.scan(one_image, jnp.zeros((), jnp.float32), (tokens, conditioning))
    return (outputs, lax.optimization_barrier(jnp.max(peaks, axis=0)))

def reference(tokens, conditioning, cotangent, query_weight, key_weight, value_weight, out_weight, up_weight, down_weight, ada_weight, query_bias, value_bias, out_bias, up_bias, down_bias, ada_bias, threshold):
    initials = (tokens, conditioning, query_weight, key_weight, value_weight, out_weight, up_weight, down_weight, ada_weight, query_bias, value_bias, out_bias, up_bias, down_bias, ada_bias)
    floats = tuple((initial.astype(jnp.float32) for initial in initials))
    block_out, pullback, head_peak = jax.vjp(forward, *floats, has_aux=True)
    grads = pullback(cotangent.astype(jnp.float32))
    limit = threshold[0]
    factor = jnp.sqrt(limit / jnp.maximum(head_peak, limit))
    column_factor = jnp.repeat(factor, HEAD_DIM)
    query_clipped = (query_weight.astype(jnp.float32) * column_factor).astype(jnp.bfloat16)
    key_clipped = (key_weight.astype(jnp.float32) * column_factor).astype(jnp.bfloat16)
    query_bias_clipped = query_bias * column_factor
    return (block_out.astype(jnp.bfloat16), grads[0], grads[1], grads[2], grads[3], grads[4], grads[5], grads[6], grads[7], grads[8], grads[9], grads[10], grads[11], grads[12], grads[13], grads[14], query_clipped, key_clipped, query_bias_clipped)
```

```python
import functools
from functools import partial

import jax
import jax.numpy as jnp
from jax import lax
from jax.experimental import pallas as pl
from jax.experimental.pallas import tpu as pltpu
from jax.sharding import Mesh, PartitionSpec as P

HEAD_DIM = 72
epsilon = 1e-06
partial_gelu = partial(jax.nn.gelu, approximate=True)

def modulate_images(values, shift, scale):
    average = jnp.mean(values, axis=-1, keepdims=True)
    centred = values - average
    spread = jnp.mean(centred * centred, axis=-1, keepdims=True)
    return centred * lax.rsqrt(spread + epsilon) * (1.0 + scale[:, None, :]) + shift[:, None, :]


def product(left, right):
    return jnp.dot(left, right, preferred_element_type=jnp.float32)


def inner_rows(left, right):
    return lax.dot_general(
        left, right, (((0,), (0,)), ((), ())), preferred_element_type=jnp.float32
    )


def against(left, right):
    return lax.dot_general(
        left, right, (((1,), (1,)), ((), ())), preferred_element_type=jnp.float32
    )


def spread_rows(values):
    return lax.all_gather(values, "tensor", axis=1, tiled=True)


def fold_rows(values):
    return lax.psum_scatter(values, "tensor", scatter_dimension=1, tiled=True)


def spread_grads(values):
    return lax.all_gather(values, "tensor", axis=1, tiled=True)


def fold_grads(values):
    return lax.psum_scatter(values, "tensor", scatter_dimension=1, tiled=True)


def local(
    tokens,
    conditioning,
    cotangent,
    query_weight,
    key_weight,
    value_weight,
    out_weight,
    up_weight,
    down_weight,
    ada_weight,
    query_bias,
    value_bias,
    out_bias,
    up_bias,
    down_bias,
    ada_bias,
    threshold,
):
    images = tokens.shape[0]
    model_width = tokens.shape[2]
    gathered = (
        lax.all_gather(query_weight, "dp", axis=0, tiled=True),
        lax.all_gather(key_weight, "dp", axis=0, tiled=True),
        lax.all_gather(value_weight, "dp", axis=0, tiled=True),
        lax.all_gather(out_weight, "dp", axis=1, tiled=True),
        lax.all_gather(up_weight, "dp", axis=0, tiled=True),
        lax.all_gather(down_weight, "dp", axis=1, tiled=True),
        lax.all_gather(ada_weight, "dp", axis=0, tiled=True),
    )
    full_query, full_key, full_value, full_out, full_up, full_down, full_ada = gathered
    lifted_low = jax.nn.silu(conditioning).astype(jnp.bfloat16)
    own_columns = product(lifted_low, full_ada) + ada_bias
    modulation = lax.all_gather(own_columns, "tensor", axis=1, tiled=True)
    pieces = [
        modulation[:, piece_index * model_width : (piece_index + 1) * model_width]
        for piece_index in range(6)
    ]
    shift_attn, scale_attn, gate_attn, shift_mlp, scale_mlp, gate_mlp = pieces
    inputs = tokens.astype(jnp.float32)
    normed_attn = spread_rows(modulate_images(inputs, shift_attn, scale_attn).astype(jnp.bfloat16))
    length = normed_attn.shape[1]
    row_count = images * length
    flat_attn = normed_attn.reshape(row_count, model_width)
    local_width = full_query.shape[1]
    heads_here = local_width // HEAD_DIM
    queries = (product(flat_attn, full_query) + query_bias).astype(jnp.bfloat16)
    key_rows = product(flat_attn, full_key).astype(jnp.bfloat16)
    value_rows = (product(flat_attn, full_value) + value_bias).astype(jnp.bfloat16)
    block_rows = min(512, length)
    head_scale = HEAD_DIM ** (-0.5)

    def by_head(matrix):
        return matrix.reshape(images, length, heads_here, HEAD_DIM)

    def attend_image(bundle):
        queries_img, keys_img, values_img = bundle
        outputs, totals, highest = ([], [], [])
        for offset in range(0, length, block_rows):
            logits = (
                jnp.einsum(
                    "qhe,khe->hqk",
                    queries_img[offset : offset + block_rows],
                    keys_img,
                    preferred_element_type=jnp.float32,
                )
                * head_scale
            )
            row_top = jnp.max(logits, axis=2, keepdims=True)
            raised = jnp.exp(logits - row_top)
            summed = jnp.sum(raised, axis=2, keepdims=True)
            shares = (raised / summed).astype(jnp.bfloat16)
            outputs.append(
                jnp.einsum(
                    "hqk,khe->qhe", shares, values_img, preferred_element_type=jnp.float32
                ).astype(jnp.bfloat16)
            )
            totals.append(row_top[:, :, 0] + jnp.log(summed[:, :, 0]))
            highest.append(jnp.max(row_top[:, :, 0], axis=1))
        return (
            jnp.concatenate(outputs, 0),
            jnp.concatenate(totals, 1),
            jnp.max(jnp.stack(highest), axis=0),
        )

    attended, log_totals, image_peaks = lax.map(
        attend_image, (by_head(queries), by_head(key_rows), by_head(value_rows))
    )
    flat_attended = attended.reshape(row_count, local_width)
    branch_attn = (
        fold_rows(product(flat_attended, full_out).reshape(images, length, model_width)) + out_bias
    )
    after_attn = inputs + gate_attn[:, None, :] * branch_attn
    normed_mlp = spread_rows(modulate_images(after_attn, shift_mlp, scale_mlp).astype(jnp.bfloat16))
    flat_mlp = normed_mlp.reshape(row_count, model_width)
    upward = product(flat_mlp, full_up) + up_bias
    active = jax.nn.gelu(upward, approximate=True).astype(jnp.bfloat16)
    branch_mlp = (
        fold_rows(product(active, full_down).reshape(images, length, model_width)) + down_bias
    )
    block_out = (after_attn + gate_mlp[:, None, :] * branch_mlp).astype(jnp.bfloat16)
    peaks = lax.pmax(jnp.max(image_peaks, axis=0), "dp")
    again = (
        lax.all_gather(query_weight, "dp", axis=0, tiled=True),
        lax.all_gather(key_weight, "dp", axis=0, tiled=True),
        lax.all_gather(value_weight, "dp", axis=0, tiled=True),
        lax.all_gather(out_weight, "dp", axis=1, tiled=True),
        lax.all_gather(up_weight, "dp", axis=0, tiled=True),
        lax.all_gather(down_weight, "dp", axis=1, tiled=True),
        lax.all_gather(ada_weight, "dp", axis=0, tiled=True),
    )
    back_query, back_key, back_value, back_out, back_up, back_down, back_ada = again
    grad_out = cotangent.astype(jnp.float32)
    grad_branch_mlp = (gate_mlp[:, None, :] * grad_out).astype(jnp.bfloat16)
    grad_gate_mlp = jnp.sum(grad_out * branch_mlp, axis=1)
    flat_grad_mlp = spread_grads(grad_branch_mlp).reshape(row_count, model_width)
    grad_down_bias = jnp.sum(flat_grad_mlp, axis=0, dtype=jnp.float32)
    grad_down_weight = inner_rows(active, flat_grad_mlp)
    grad_active = against(flat_grad_mlp, back_down)
    _, gelu_pull = jax.vjp(partial(jax.nn.gelu, approximate=True), upward)
    grad_upward = gelu_pull(grad_active)[0].astype(jnp.bfloat16)
    grad_up_bias = jnp.sum(grad_upward, axis=0, dtype=jnp.float32)
    grad_up_weight = inner_rows(flat_mlp, grad_upward)
    grad_normed_mlp = fold_grads(against(grad_upward, back_up).reshape(images, length, model_width))
    _, mlp_pull = jax.vjp(modulate_images, after_attn, shift_mlp, scale_mlp)
    grad_after, grad_shift_mlp, grad_scale_mlp = mlp_pull(grad_normed_mlp)
    grad_after = grad_out + grad_after
    grad_branch_attn = (gate_attn[:, None, :] * grad_after).astype(jnp.bfloat16)
    grad_gate_attn = jnp.sum(grad_after * branch_attn, axis=1)
    flat_grad_attn = spread_grads(grad_branch_attn).reshape(row_count, model_width)
    grad_out_bias = jnp.sum(flat_grad_attn, axis=0, dtype=jnp.float32)
    grad_out_weight = inner_rows(flat_attended, flat_grad_attn)
    grad_attended = against(flat_grad_attn, back_out).astype(jnp.bfloat16)

    def attend_back(bundle):
        queries_img, keys_img, values_img, grads_img, totals_img = bundle
        query_parts = []
        grad_keys_img = jnp.zeros(keys_img.shape, jnp.float32)
        grad_values_img = jnp.zeros(values_img.shape, jnp.float32)
        for offset in range(0, length, block_rows):
            query_block = queries_img[offset : offset + block_rows]
            grad_block = grads_img[offset : offset + block_rows]
            logits = (
                jnp.einsum(
                    "qhe,khe->hqk", query_block, keys_img, preferred_element_type=jnp.float32
                )
                * head_scale
            )
            shares = jnp.exp(logits - totals_img[:, offset : offset + block_rows, None])
            grad_shares = jnp.einsum(
                "qhe,khe->hqk", grad_block, values_img, preferred_element_type=jnp.float32
            )
            row_inner = jnp.sum(shares * grad_shares, axis=2, keepdims=True)
            grad_logits = (shares * (grad_shares - row_inner)).astype(jnp.bfloat16)
            query_parts.append(
                (
                    jnp.einsum(
                        "hqk,khe->qhe", grad_logits, keys_img, preferred_element_type=jnp.float32
                    )
                    * head_scale
                ).astype(jnp.bfloat16)
            )
            grad_keys_img = (
                grad_keys_img
                + jnp.einsum(
                    "hqk,qhe->khe", grad_logits, query_block, preferred_element_type=jnp.float32
                )
                * head_scale
            )
            grad_values_img = grad_values_img + jnp.einsum(
                "hqk,qhe->khe",
                shares.astype(jnp.bfloat16),
                grad_block,
                preferred_element_type=jnp.float32,
            )
        return (
            jnp.concatenate(query_parts, 0),
            grad_keys_img.astype(jnp.bfloat16),
            grad_values_img.astype(jnp.bfloat16),
        )

    grad_queries, grad_keys, grad_values = lax.map(
        attend_back,
        (
            by_head(queries),
            by_head(key_rows),
            by_head(value_rows),
            by_head(grad_attended),
            log_totals,
        ),
    )
    grad_queries = grad_queries.reshape(row_count, local_width)
    grad_keys = grad_keys.reshape(row_count, local_width)
    grad_values = grad_values.reshape(row_count, local_width)
    grad_query_bias = jnp.sum(grad_queries, axis=0, dtype=jnp.float32)
    grad_value_bias = jnp.sum(grad_values, axis=0, dtype=jnp.float32)
    grad_query_weight = inner_rows(flat_attn, grad_queries)
    grad_key_weight = inner_rows(flat_attn, grad_keys)
    grad_value_weight = inner_rows(flat_attn, grad_values)
    partial_normed = (
        against(grad_queries, back_query)
        + against(grad_keys, back_key)
        + against(grad_values, back_value)
    )
    grad_normed_attn = fold_grads(partial_normed.reshape(images, length, model_width))
    _, attn_pull = jax.vjp(modulate_images, inputs, shift_attn, scale_attn)
    grad_inputs, grad_shift_attn, grad_scale_attn = attn_pull(grad_normed_attn)
    grad_tokens = grad_after + grad_inputs
    modulation_terms = jnp.concatenate(
        [
            grad_shift_attn,
            grad_scale_attn,
            grad_gate_attn,
            grad_shift_mlp,
            grad_scale_mlp,
            grad_gate_mlp,
        ],
        axis=1,
    )
    grad_modulation = lax.psum_scatter(
        modulation_terms, "tensor", scatter_dimension=1, tiled=True
    ).astype(jnp.bfloat16)
    grad_ada_bias = jnp.sum(grad_modulation, axis=0, dtype=jnp.float32)
    grad_ada_weight = inner_rows(lifted_low, grad_modulation)
    grad_lifted = lax.psum(against(grad_modulation, back_ada), "tensor")
    _, silu_pull = jax.vjp(jax.nn.silu, conditioning)
    grad_conditioning = silu_pull(grad_lifted)[0]
    weight_grads = (
        lax.psum_scatter(grad_query_weight, "dp", scatter_dimension=0, tiled=True),
        lax.psum_scatter(grad_key_weight, "dp", scatter_dimension=0, tiled=True),
        lax.psum_scatter(grad_value_weight, "dp", scatter_dimension=0, tiled=True),
        lax.psum_scatter(grad_out_weight, "dp", scatter_dimension=1, tiled=True),
        lax.psum_scatter(grad_up_weight, "dp", scatter_dimension=0, tiled=True),
        lax.psum_scatter(grad_down_weight, "dp", scatter_dimension=1, tiled=True),
        lax.psum_scatter(grad_ada_weight, "dp", scatter_dimension=0, tiled=True),
    )
    bias_grads = lax.psum(
        (
            grad_query_bias,
            grad_value_bias,
            grad_out_bias,
            grad_up_bias,
            grad_down_bias,
            grad_ada_bias,
        ),
        "dp",
    )
    limit = threshold[0]
    factor = jnp.sqrt(limit / jnp.maximum(peaks, limit))
    column_factor = jnp.repeat(factor, HEAD_DIM)
    query_clipped = (query_weight.astype(jnp.float32) * column_factor).astype(jnp.bfloat16)
    key_clipped = (key_weight.astype(jnp.float32) * column_factor).astype(jnp.bfloat16)
    query_bias_clipped = query_bias * column_factor
    return (
        block_out,
        grad_tokens,
        grad_conditioning,
        weight_grads[0],
        weight_grads[1],
        weight_grads[2],
        weight_grads[3],
        weight_grads[4],
        weight_grads[5],
        weight_grads[6],
        bias_grads[0],
        bias_grads[1],
        bias_grads[2],
        bias_grads[3],
        bias_grads[4],
        bias_grads[5],
        query_clipped,
        key_clipped,
        query_bias_clipped,
    )


MESH = pl.DeviceIdType.MESH
AXES=("y","x","core","z")

class Net:
    def __init__(self):
        self.y,self.x,self.c,self.z=(lax.axis_index(a) for a in AXES)
        y,x,c,z=self.y,self.x,self.c,self.z
        self.zp=lax.rem(z+1,4); self.zm=lax.rem(z+3,4); self.zo=lax.rem(z+2,4)
        self.xn=(y,1-x,c,z); self.yn=(1-y,x,c,z); self.cn=(y,x,1-c,z)
        self.zpn=(y,x,c,self.zp); self.zmn=(y,x,c,self.zm)

def enter(net, column):
    bar=pltpu.get_barrier_semaphore()
    y,x,c,z=net.y,net.x,net.c,net.z
    others=[net.xn,net.yn]
    if column:
        for dc in range(2):
            for dz in range(4):
                if dc or dz: others.append((y,x,lax.rem(c+dc,2),lax.rem(z+dz,4)))
    else:
        others+= [net.cn,net.zpn,net.zmn]
    for o in others: pl.semaphore_signal(bar,inc=1,device_id=o,device_id_type=MESH)
    pl.semaphore_wait(bar,len(others))

ROWS=144; COLS=1152; TOP=80

def gather_kernel(tensors, s_ref, tok_ref, cot_ref, g0, g1, g2, tok_out, cot_out, send, recv, tsend, trecv, lsem):
    g_refs=(g0,g1,g2)
    net=Net(); y,x,c,z=net.y,net.x,net.c,net.z
    enter(net, True)
    def token_copies(start):
        for a,(src,dst) in enumerate(((tok_ref,tok_out),(cot_ref,cot_out))):
            for i in range(2):
                dc=lax.div(z,2); dz=2*c+i
                here=jnp.logical_and(dc==c,dz==z)
                rows=pl.ds(pl.multiple_of(lax.rem(z,2)*256,256),256)
                cp=pltpu.make_async_remote_copy(src_ref=src.at[i],dst_ref=dst.at[rows],send_sem=tsend.at[a,i],recv_sem=trecv.at[a,lax.rem(z,2)],device_id=(y,x,dc,dz),device_id_type=MESH)
                lc=pltpu.make_async_copy(src.at[i],dst.at[rows],trecv.at[a,lax.rem(z,2)])
                @pl.when(jnp.logical_not(here))
                def _():
                    if start: cp.start()
                    else: cp.wait_send()
                @pl.when(here)
                def _():
                    if start: lc.start()
    def token_arrivals():
        for a,(src,dst) in enumerate(((tok_ref,tok_out),(cot_ref,cot_out))):
            for k in range(2):
                rows=pl.ds(k*256,256)
                pltpu.make_async_copy(src.at[0],dst.at[rows],trecv.at[a,k]).wait()
    def slot(t,yy,xx,cc,zz,part=None):
        row=(4*yy+2*xx+cc)*ROWS
        n=ROWS
        if part==0: n=TOP
        if part==1: row=row+TOP; n=ROWS-TOP
        return g_refs[t].at[pl.ds(pl.multiple_of(row,16),n),pl.ds(pl.multiple_of(zz*COLS,COLS),COLS)]
    counter=[0]
    started=[]
    def sem_of(t,yy,xx,cc,zz,part):
        return recv.at[t,4*yy+2*xx+cc,zz,part or 0]
    def put(dev,t,yy,xx,cc,zz,part=None,own=False):
        src=s_ref.at[t] if own else slot(t,yy,xx,cc,zz,part)
        cp=pltpu.make_async_remote_copy(src_ref=src,dst_ref=slot(t,yy,xx,cc,zz,part),send_sem=send.at[counter[0]],recv_sem=sem_of(t,yy,xx,cc,zz,part),device_id=dev,device_id_type=MESH)
        counter[0]+=1
        cp.start(); started.append(cp)
    def arrived(t,yy,xx,cc,zz,part=None):
        s=slot(t,yy,xx,cc,zz,part)
        pltpu.make_async_copy(s,s,sem_of(t,yy,xx,cc,zz,part)).wait()
    def finish():
        for cp in started: cp.wait_send()
        started.clear(); counter[0]=0
    def from_partner(cc):
        for t in range(tensors):
            for k in range(4):
                zz=lax.rem(z+k,4)
                for yy in range(2):
                    for xx in range(2):
                        arrived(t,yy,xx,cc,zz)
    local=[pltpu.make_async_copy(s_ref.at[t],slot(t,y,x,c,z),lsem.at[t]) for t in range(tensors)]
    for cp in local: cp.start()
    token_copies(True)
    first=(y,1-x); second=(1-y,x)
    def flow(cc):
        near=net.xn if cc==0 else net.yn
        far=net.yn if cc==0 else net.xn
        nearp=(y,1-x) if cc==0 else (1-y,x)
        farp=(1-y,x) if cc==0 else (y,1-x)
        def when(cond,fn):
            pl.when(cond)(fn)
        up=z<3; down=z>0
        def zput(dev,cond,t,zz,own=False):
            src=s_ref.at[t] if own else slot(t,y,x,cc,zz)
            cp=pltpu.make_async_remote_copy(src_ref=src,dst_ref=slot(t,y,x,cc,zz),send_sem=send.at[counter[0]],recv_sem=sem_of(t,y,x,cc,zz,None),device_id=dev,device_id_type=MESH)
            counter[0]+=1
            pl.when(cond)(cp.start); guarded.append((cond,cp))
        guarded=[]
        zpn=(y,x,cc,lax.rem(z+1,4)); zmn=(y,x,cc,lax.rem(z+3,4))
        for t in range(tensors):
            put(near,t,y,x,cc,z,own=True); put(far,t,y,x,cc,z,own=True)
            zput(zpn,up,t,z,own=True); zput(zmn,down,t,z,own=True)
            put(net.cn,t,y,x,cc,z,own=True)
        def spread(t,zz):
            put(near,t,y,x,cc,zz); put(far,t,y,x,cc,zz); put(net.cn,t,y,x,cc,zz)
        def onward(t,zz):
            arrived(t,nearp[0],nearp[1],cc,zz); put(far,t,nearp[0],nearp[1],cc,zz); put(net.cn,t,nearp[0],nearp[1],cc,zz)
            arrived(t,farp[0],farp[1],cc,zz); put(net.cn,t,farp[0],farp[1],cc,zz)
        def nth(k):
            if k==0: return z
            table=((1,2,3),(0,2,3),(3,1,0),(2,1,0))
            return sum(jnp.where(z==i,table[i][k-1],0) for i in range(4))
        for k in range(1,4):
            zz=nth(k)
            for t in range(tensors):
                arrived(t,y,x,cc,zz)
                zput(zpn,jnp.logical_and(zz<z,up),t,zz)
                zput(zmn,jnp.logical_and(zz>z,down),t,zz)
                spread(t,zz)
            for t in range(tensors): onward(t,nth(k-1))
        for t in range(tensors): onward(t,nth(3))
        for k in range(4):
            for t in range(tensors):
                arrived(t,1-y,1-x,cc,nth(k)); put(net.cn,t,1-y,1-x,cc,nth(k))
        from_partner(1-cc)
        for cond,cp in guarded: pl.when(cond)(cp.wait_send)
        finish()
    @pl.when(c==0)
    def _(): flow(0)
    @pl.when(c==1)
    def _(): flow(1)
    for cp in local: cp.wait()
    token_arrivals()
    token_copies(False)

def gather(s,tok,cot):
    T=s.shape[0]
    hbm=pl.BlockSpec(memory_space=pl.ANY)
    return pl.pallas_call(functools.partial(gather_kernel,T),
      out_shape=(jax.ShapeDtypeStruct((8*ROWS,4*COLS),jnp.bfloat16),)*3+(jax.ShapeDtypeStruct((512,COLS),tok.dtype),jax.ShapeDtypeStruct((512,COLS),cot.dtype)),
      in_specs=[hbm]*3,out_specs=(hbm,)*5,
      scratch_shapes=[pltpu.SemaphoreType.DMA((40*T,)),pltpu.SemaphoreType.DMA((T,8,4,2)),pltpu.SemaphoreType.DMA((2,2)),pltpu.SemaphoreType.DMA((2,2)),pltpu.SemaphoreType.DMA((T,))],
      compiler_params=pltpu.CompilerParams(collective_id=1,has_side_effects=True))(s,tok,cot)
HEAD_DIM=72; HS=288; KV0=256; KVW=640; AT0=768; ATW=384
C=HEAD_DIM**-0.5; LOG2E=1.4426950408889634
TOK=512
bf=jnp.bfloat16; f32=jnp.float32

def dg(a,b,ca,cb): return lax.dot_general(a,b,(((ca,),(cb,)),((),())),preferred_element_type=f32)

def partner():
    y,x,c,z=(lax.axis_index(a) for a in ("y","x","core","z"))
    return (y,x,1-c,z)

def greet_partner(dev):
    bar=pltpu.get_barrier_semaphore()
    pl.semaphore_signal(bar,inc=1,device_id=dev,device_id_type=MESH)
    pl.semaphore_wait(bar,1)

def att_fwd_kernel(x_ref,g0_ref,bias_ref,qkv_ref,kvo_ref,att_ref,lse_ref,peak_ref,branch_ref,w,qh,kh,vh,oh,wsem,ssem,rsem):
    dev=partner()
    for z in range(4): pltpu.make_async_copy(g0_ref.at[:,pl.ds(z*COLS,COLS)],w.at[z],wsem.at[z]).start()
    greet_partner(dev)
    def send(z):
        return pltpu.make_async_remote_copy(src_ref=qkv_ref.at[z,:,pl.ds(KV0,KVW)],dst_ref=kvo_ref.at[z],send_sem=ssem.at[z],recv_sem=rsem.at[z],device_id=dev,device_id_type=MESH)
    for z in range(4):
        pltpu.make_async_copy(g0_ref.at[:,pl.ds(z*COLS,COLS)],w.at[z],wsem.at[z]).wait()
        def tile(i,_):
            cols=pl.ds(pl.multiple_of(i*384,384),384)
            qkv_ref[z,:,cols]=(dg(x_ref[...],w[z,:,cols],1,0)+bias_ref[z,:,cols]).astype(bf)
            return 0
        lax.fori_loop(0,3,tile,0)
        send(z).start()
    branch_ref[...]=jnp.zeros_like(branch_ref)
    def chunk(z,_):
        send(z).wait_recv()
        for j in range(4):
            a=j*HEAD_DIM
            qh[j]=qkv_ref[z,:,a:a+HEAD_DIM]
            kh[j,:TOK]=qkv_ref[z,:,HS+a:HS+a+HEAD_DIM]
            vh[j,:TOK]=qkv_ref[z,:,2*HS+a:2*HS+a+HEAD_DIM]
            kh[j,TOK:]=kvo_ref[z,:,HS-KV0+a:HS-KV0+a+HEAD_DIM]
            vh[j,TOK:]=kvo_ref[z,:,2*HS-KV0+a:2*HS-KV0+a+HEAD_DIM]
        def head(j,_):
            h=z*4+j
            s=dg(kh[j],qh[j],1,1)
            m=jnp.max(s,axis=0,keepdims=True)
            p=jnp.exp2((s-m)*(C*LOG2E))
            l=jnp.sum(p,axis=0,keepdims=True)
            o=dg(vh[j],p.astype(bf),0,0)/l
            oh[j]=o.T.astype(bf)
            lse_ref[h]=m*(C*LOG2E)+jnp.log2(l)
            peak_ref[h]=jnp.broadcast_to(jnp.max(m,axis=1,keepdims=True)*C,(1,128))
            return 0
        lax.fori_loop(0,4,head,0)
        att_ref[z]=jnp.concatenate([jnp.zeros((TOK,ATW-HS),bf)]+[oh[j] for j in range(4)],axis=1)
        def tile(i,_):
            cols=pl.ds(pl.multiple_of(i*384,384),384)
            branch_ref[:,cols]+=dg(att_ref[z],w[z,cols,AT0:],1,1)
            return 0
        lax.fori_loop(0,3,tile,0)
        return 0
    lax.fori_loop(0,4,chunk,0)
    for z in range(4): send(z).wait_send()

VM=pl.BlockSpec(memory_space=pltpu.VMEM); HB=pl.BlockSpec(memory_space=pl.ANY)
S=jax.ShapeDtypeStruct
def att_fwd(x,g0,bias):
    D=pltpu.SemaphoreType.DMA
    return pl.pallas_call(att_fwd_kernel,name="att_fwd",
      out_shape=(S((4,TOK,COLS),bf),S((4,TOK,KVW),bf),S((4,TOK,ATW),bf),S((16,1,TOK),f32),S((16,1,128),f32),S((TOK,COLS),f32)),
      in_specs=[VM,HB,VM],out_specs=(VM,)*6,
      scratch_shapes=[pltpu.VMEM((4,COLS,COLS),bf),pltpu.VMEM((4,TOK,HEAD_DIM),bf),pltpu.VMEM((4,2*TOK,HEAD_DIM),bf),pltpu.VMEM((4,2*TOK,HEAD_DIM),bf),pltpu.VMEM((4,TOK,HEAD_DIM),bf),D((4,)),D((4,)),D((4,))],
      compiler_params=pltpu.CompilerParams(collective_id=3,has_side_effects=True,vmem_limit_bytes=58*2**20))(x,g0,bias)

def att_bwd_kernel(x_ref,gb_ref,g0_ref,qkv_ref,kvo_ref,att_ref,lse_ref,d0_ref,gx_ref,bsum_ref,w,qh,kh,vh,gh,dqh,dkh,dvh,mate_out,mate_in,pack,xt,gt,dbuf,wsem,ssem,rsem,dsem):
    dev=partner()
    def load(z): return pltpu.make_async_copy(g0_ref.at[:,pl.ds(pl.multiple_of(z*COLS,COLS),COLS)],w.at[lax.rem(z,2)],wsem.at[lax.rem(z,2)])
    load(0).start()
    greet_partner(dev)
    xt[...]=x_ref[...].T
    gt[...]=gb_ref[...].T
    gx_ref[...]=jnp.zeros_like(gx_ref)
    def send(z):
        return pltpu.make_async_remote_copy(src_ref=mate_out.at[z],dst_ref=mate_in.at[z],send_sem=ssem.at[z],recv_sem=rsem.at[z],device_id=dev,device_id_type=MESH)
    def store(z):
        return pltpu.make_async_copy(dbuf.at[lax.rem(z,2)],d0_ref.at[:,pl.ds(pl.multiple_of(z*COLS,COLS),COLS)],dsem.at[lax.rem(z,2)])
    def chunk(z,_):
        k2=lax.rem(z,2)
        load(z).wait()
        pl.when(z<3)(lambda: load(z+1).start())
        ga=dg(gb_ref[...],w[k2,:,AT0:],1,0).astype(bf)
        for j in range(4):
            a=j*HEAD_DIM
            gh[j]=ga[:,ATW-HS+a:ATW-HS+a+HEAD_DIM]
            qh[j]=qkv_ref[z,:,a:a+HEAD_DIM]
            kh[j,:TOK]=qkv_ref[z,:,HS+a:HS+a+HEAD_DIM]
            vh[j,:TOK]=qkv_ref[z,:,2*HS+a:2*HS+a+HEAD_DIM]
            kh[j,TOK:]=kvo_ref[z,:,HS-KV0+a:HS-KV0+a+HEAD_DIM]
            vh[j,TOK:]=kvo_ref[z,:,2*HS-KV0+a:2*HS-KV0+a+HEAD_DIM]
        def head(j,_):
            k=kh[j]; q=qh[j]; g=gh[j]
            p=jnp.exp2(dg(k,q,1,1)*(C*LOG2E)-lse_ref[z*4+j])
            t=p*dg(vh[j],g,1,1)
            inner=jnp.sum(t,axis=0,keepdims=True)
            ds=(t-p*inner).astype(bf)
            dvh[j]=dg(p.astype(bf),g,1,0)
            dkh[j]=dg(ds,q,1,0)*C
            dqh[j]=(dg(k,ds,0,0)*C).T.astype(bf)
            return 0
        lax.fori_loop(0,4,head,0)
        mate_out[z]=jnp.concatenate([dkh[j,TOK:].astype(bf) for j in range(4)]+[dvh[j,TOK:].astype(bf) for j in range(4)]+[jnp.zeros((TOK,KVW-2*HS),bf)],axis=1)
        send(z).start()
        send(z).wait_recv()
        o=mate_in[z].astype(f32)
        own=jnp.concatenate([dkh[j,:TOK] for j in range(4)]+[dvh[j,:TOK] for j in range(4)],axis=1)
        both=(own+o[:,:2*HS]).astype(bf)
        pack[...]=jnp.concatenate([dqh[j] for j in range(4)]+[both,jnp.zeros((TOK,HS),bf)],axis=1)
        bsum_ref[z]=jnp.sum(pack[...].astype(f32),axis=0,keepdims=True)
        pl.when(z>=2)(lambda: store(z-2).wait())
        def tile(i,_):
            cols=pl.ds(pl.multiple_of(i*384,384),384)
            gx_ref[:,cols]+=dg(pack[...],w[k2,cols,:],1,1)
            d1=dg(xt[cols],pack[:,:896],1,0)
            d2=dg(gt[cols],att_ref[z],1,0)
            dbuf[k2,cols,:AT0]=d1[:,:AT0].astype(bf)
            dbuf[k2,cols,AT0:896]=(d1[:,AT0:]+d2[:,:128]).astype(bf)
            dbuf[k2,cols,896:]=d2[:,128:].astype(bf)
            return 0
        lax.fori_loop(0,3,tile,0)
        store(z).start()
        return 0
    lax.fori_loop(0,4,chunk,0)
    store(2).wait(); store(3).wait()
    for z in range(4): send(z).wait_send()

def att_bwd(x,gb,g0,qkv,kvo,att,lse):
    D=pltpu.SemaphoreType.DMA; M=pltpu.VMEM
    return pl.pallas_call(att_bwd_kernel,name="att_bwd",
      out_shape=(S((COLS,4*COLS),bf),S((TOK,COLS),f32),S((4,1,COLS),f32)),
      in_specs=[VM,VM,HB,VM,VM,VM,VM],out_specs=(HB,VM,VM),
      scratch_shapes=[M((2,COLS,COLS),bf),M((4,TOK,HEAD_DIM),bf),M((4,2*TOK,HEAD_DIM),bf),M((4,2*TOK,HEAD_DIM),bf),M((4,TOK,HEAD_DIM),bf),
         M((4,TOK,HEAD_DIM),bf),M((4,2*TOK,HEAD_DIM),f32),M((4,2*TOK,HEAD_DIM),f32),M((4,TOK,KVW),bf),M((4,TOK,KVW),bf),M((TOK,COLS),bf),M((COLS,TOK),bf),M((COLS,TOK),bf),M((2,COLS,COLS),bf),
         D((2,)),D((4,)),D((4,)),D((2,))],
      compiler_params=pltpu.CompilerParams(collective_id=4,has_side_effects=True,vmem_limit_bytes=58*2**20))(x,gb,g0,qkv,kvo,att,lse)

class Scatter:
    def __init__(self, net, tensors, cc, d, rc, acc, tmp, far_in, near_in, line_in, out, send, core_sem, load_sem, tmp_sem, far_sem, near_sem, line_sem):
        self.__dict__.update(locals()); self.count=0; self.started=[]; self.pending=[]
        y,x=net.y,net.x
        self.far_dev=net.yn if cc==0 else net.xn
        self.near_dev=net.xn if cc==0 else net.yn
    def place(self, far, near):
        return (far,near) if self.cc==0 else (near,far)
    def mine(self):
        return (self.net.y,self.net.x) if self.cc==0 else (self.net.x,self.net.y)
    def remote(self, src, dst, dev, recv, cond=None):
        cp=pltpu.make_async_remote_copy(src_ref=src,dst_ref=dst,send_sem=self.send.at[self.count],recv_sem=recv,device_id=dev,device_id_type=MESH)
        self.count+=1
        if cond is None: cp.start()
        else: pl.when(cond)(cp.start)
        self.started.append((cond,cp))
    def slots(self):
        f,n=self.mine()
        return [(ff,nn,z) for ff in (1-f,f) for nn in (1-n,n) for z in (0,3,1,2)]
    def block(self,t,ff,nn,cc,z):
        yy,xx=self.place(ff,nn)
        row=(4*yy+2*xx+cc)*ROWS
        return self.d[t].at[pl.ds(pl.multiple_of(row,16),ROWS),pl.ds(z*COLS,COLS)]
    def begin(self,t):
        for ff,nn,z in self.slots():
            yy,xx=self.place(ff,nn)
            self.remote(self.block(t,ff,nn,1-self.cc,z),self.rc.at[t,yy,xx,z],self.net.cn,self.core_sem.at[t,yy,xx,z])
            pltpu.make_async_copy(self.block(t,ff,nn,self.cc,z),self.acc.at[t,yy,xx,z],self.load_sem.at[t,yy,xx,z]).start()
    def add(self,a,b):
        def one(i,_):
            r=pl.ds(pl.multiple_of(i*16,16),16)
            a[r]=(a[r].astype(jnp.float32)+b[r].astype(jnp.float32)).astype(a.dtype)
            return 0
        lax.fori_loop(0,ROWS//16,one,0)
    def core_steps(self,t):
        slots=self.slots()
        n=len(slots)
        def fetch(i):
            ff,nn,z=slots[i]; yy,xx=self.place(ff,nn); r=self.rc.at[t,yy,xx,z]
            pltpu.make_async_copy(r,r,self.core_sem.at[t,yy,xx,z]).wait()
            pltpu.make_async_copy(r,self.tmp.at[i%2],self.tmp_sem.at[i%2]).start()
        def step(i):
            if i==0: fetch(0)
            if i+1<n: fetch(i+1)
            ff,nn,z=slots[i]; yy,xx=self.place(ff,nn)
            a=self.acc.at[t,yy,xx,z]
            pltpu.make_async_copy(a,a,self.load_sem.at[t,yy,xx,z]).wait()
            pltpu.make_async_copy(self.rc.at[t,yy,xx,z],self.tmp.at[i%2],self.tmp_sem.at[i%2]).wait()
            self.add(a,self.tmp.at[i%2])
            if i<n//2: self.remote(a,self.far_in.at[t,nn,z],self.far_dev,self.far_sem.at[t,nn,z])
        return [functools.partial(step,i) for i in range(n)]
    def far_steps(self,t):
        f,n=self.mine()
        def step(nn,z,last):
            yy,xx=self.place(f,nn); a=self.acc.at[t,yy,xx,z]; r=self.far_in.at[t,nn,z]
            pltpu.make_async_copy(r,r,self.far_sem.at[t,nn,z]).wait()
            self.add(a,r)
            if not last: self.remote(a,self.near_in.at[t,z],self.near_dev,self.near_sem.at[t,z])
        return [functools.partial(step,nn,z,last) for nn,last in ((1-n,False),(n,True)) for z in (0,3,1,2)]
    def near_steps(self,t):
        net=self.net; z=net.z
        def step(zz):
            a=self.acc.at[t,net.y,net.x,zz]; r=self.near_in.at[t,zz]
            pltpu.make_async_copy(r,r,self.near_sem.at[t,zz]).wait()
            self.add(a,r)
            if zz==3:
                pl.when(z==0)(lambda: self.line_send(t,3,1))
            if zz==0:
                pl.when(z==3)(lambda: self.line_send(t,0,0))
        return [functools.partial(step,zz) for zz in (0,3,1,2)]
    def line_send(self,t,zz,up):
        pass
    def line_steps(self,t):
        net=self.net; z=net.z
        up_dev=(net.y,net.x,net.c,lax.rem(z+1,4)); down_dev=(net.y,net.x,net.c,lax.rem(z+3,4))
        def arrive(side,zz):
            r=self.line_in.at[t,side,zz]
            pltpu.make_async_copy(r,r,self.line_sem.at[t,side,zz]).wait()
            return r
        def up(zz):
            a=self.acc.at[t,net.y,net.x,zz]
            @pl.when(jnp.logical_and(z<zz,z>0))
            def _(): self.add(a,arrive(0,zz))
            self.remote(a,self.line_in.at[t,0,zz],up_dev,self.line_sem.at[t,0,zz],z<zz)
        def down(zz):
            a=self.acc.at[t,net.y,net.x,zz]
            @pl.when(jnp.logical_and(z>zz,z<3))
            def _(): self.add(a,arrive(1,zz))
            self.remote(a,self.line_in.at[t,1,zz],down_dev,self.line_sem.at[t,1,zz],z>zz)
        def last():
            a=self.acc.at[t,net.y,net.x,z]
            pl.when(z>0)(lambda: arrive(0,z) and None)
            pl.when(z<3)(lambda: arrive(1,z) and None)
            below=self.line_in.at[t,0,z]; above=self.line_in.at[t,1,z]
            def one(i,_):
                r=pl.ds(pl.multiple_of(i*16,16),16)
                v=a[r].astype(jnp.float32)
                v=v+jnp.where(z>0,below[r].astype(jnp.float32),0.0)
                v=v+jnp.where(z<3,above[r].astype(jnp.float32),0.0)
                self.out[t,r]=v
                return 0
            lax.fori_loop(0,ROWS//16,one,0)
        return [functools.partial(up,3),functools.partial(down,0),functools.partial(up,2),functools.partial(down,1),functools.partial(up,1),functools.partial(down,2),last]
    def finish(self):
        for cond,cp in self.started:
            if cond is None: cp.wait_send()
            else: pl.when(cond)(cp.wait_send)

def row_copies(net, pairs, send, recv):
    y,x,c,z=net.y,net.x,net.c,net.z
    dc=lax.div(z,2)
    def each(start):
        for a,(src,dst) in enumerate(pairs):
            for k in range(2):
                dz=2*c+k
                here=jnp.logical_and(dc==c,dz==z)
                rows=src.at[pl.ds(k*256,256)]; image=dst.at[lax.rem(z,2)]
                cp=pltpu.make_async_remote_copy(src_ref=rows,dst_ref=image,send_sem=send.at[a,k],recv_sem=recv.at[a,lax.rem(z,2)],device_id=(y,x,dc,dz),device_id_type=MESH)
                lc=pltpu.make_async_copy(rows,image,recv.at[a,lax.rem(z,2)])
                pl.when(jnp.logical_not(here))(cp.start if start else cp.wait_send)
                if start: pl.when(here)(lc.start)
    def arrivals():
        for a,(src,dst) in enumerate(pairs):
            for i in range(2):
                pltpu.make_async_copy(dst.at[i],dst.at[i],recv.at[a,i]).wait()
    return each,arrivals

def scatter_kernel(T, d0, d1, d2, r0, r1, out, rc, b0, b1, acc, tmp, far_in, near_in, line_in, row_send, row_recv, *sems):
    net=Net(); enter(net,True)
    each,arrivals=row_copies(net,((r0,b0),(r1,b1)),row_send,row_recv)
    each(True)
    def flow(cc):
        s=Scatter(net,T,cc,[d0,d1,d2],rc,acc,tmp,far_in,near_in,line_in,out,*sems)
        for t in range(T): s.begin(t)
        for t in range(T):
            for f in s.core_steps(t): f()
            if t>0:
                for f in s.far_steps(t-1): f()
            if t>1:
                for f in s.near_steps(t-2)+s.line_steps(t-2): f()
        for f in s.far_steps(T-1): f()
        for t in range(max(T-2,0),T):
            for f in s.near_steps(t)+s.line_steps(t): f()
        s.finish()
    pl.when(net.c==0)(lambda: flow(0))
    pl.when(net.c==1)(lambda: flow(1))
    arrivals(); each(False)

def scatter(d0,d1,d2,r0,r1):
    T=3; bf=jnp.bfloat16
    D=pltpu.SemaphoreType.DMA
    hbm=pl.BlockSpec(memory_space=pl.ANY)
    B=(ROWS,COLS)
    out=pl.pallas_call(functools.partial(scatter_kernel,T),name="scatter",
      out_shape=(jax.ShapeDtypeStruct((T,)+B,jnp.float32),jax.ShapeDtypeStruct((T,2,2,4)+B,bf))+(jax.ShapeDtypeStruct((2,256,COLS),bf),)*2,
      in_specs=[hbm]*5,out_specs=(pl.BlockSpec(memory_space=pltpu.VMEM),hbm,hbm,hbm),
      scratch_shapes=[pltpu.VMEM((T,2,2,4)+B,bf),pltpu.VMEM((2,)+B,bf),pltpu.VMEM((T,2,4)+B,bf),pltpu.VMEM((T,4)+B,bf),pltpu.VMEM((T,2,4)+B,bf),
         D((2,2)),D((2,2)),D((T*36,)),D((T,2,2,4)),D((T,2,2,4)),D((2,)),D((T,2,4)),D((T,4)),D((T,2,4))],
      compiler_params=pltpu.CompilerParams(collective_id=2,has_side_effects=True,vmem_limit_bytes=58*2**20))(d0,d1,d2,r0,r1)
    return out[0],out[2],out[3]

def modulate(values, shift, scale):
    average = jnp.mean(values, axis=-1, keepdims=True)
    centred = values - average
    spread = jnp.mean(centred * centred, axis=-1, keepdims=True)
    return centred * lax.rsqrt(spread + epsilon) * (1.0 + scale) + shift


def one_image_per_chip(
    tokens, conditioning, cotangent, query_weight, key_weight, value_weight, out_weight, up_weight,
    down_weight, ada_weight, query_bias, value_bias, out_bias, up_bias, down_bias, ada_bias, threshold,
):
    y, x, c, z = (lax.axis_index(a) for a in AXES)
    plane = 2 * y + x
    batch = 4 * y + 2 * x + c
    first = jnp.concatenate([query_weight, key_weight, value_weight, out_weight.T], axis=1)
    shard = jnp.stack([first, up_weight, down_weight.T])
    full0, full1, full2, own_tokens, own_cotangent = gather(shard, tokens, cotangent)

    lifted = jax.nn.silu(conditioning).astype(bf)
    every_lifted = lax.all_gather(lifted, ("y", "x", "core"), axis=0, tiled=True)
    lifted_rows = lax.dynamic_slice(every_lifted, (0, batch * ROWS), (16, ROWS))
    partial = product(lifted_rows, ada_weight)
    columns = lax.psum(partial, ("y", "x", "core")) + ada_bias
    four = lax.dynamic_slice(columns, (4 * plane, 0), (4, columns.shape[1]))
    biases = jnp.concatenate([query_bias, value_bias, up_bias])[None]
    by_z = lax.all_gather(jnp.concatenate([four, biases]), "z", axis=0)
    vectors = lax.dynamic_slice(by_z, (0, z, 0), (4, 1, by_z.shape[2])).reshape(6, 1, COLS)
    shift_attn, scale_attn, gate_attn, shift_mlp, scale_mlp, gate_mlp = vectors
    all_bias = by_z[:, 4]
    nothing = jnp.zeros((4, HS), f32)
    bias0 = jnp.concatenate([all_bias[:, :HS], nothing, all_bias[:, HS : 2 * HS], nothing], axis=1)
    full_up_bias = all_bias[:, 2 * HS :].reshape(1, 4 * COLS)

    inputs = own_tokens.astype(f32)
    normed_attn = modulate(inputs, shift_attn, scale_attn).astype(bf)
    qkv, mate_kv, attended, totals, peak, branch_attn = att_fwd(normed_attn, full0, bias0[:, None])
    branch_attn = branch_attn + out_bias
    after_attn = inputs + gate_attn * branch_attn
    normed_mlp = modulate(after_attn, shift_mlp, scale_mlp).astype(bf)
    upward = product(normed_mlp, full1) + full_up_bias
    active = jax.nn.gelu(upward, approximate=True).astype(bf)
    branch_mlp = against(active, full2) + down_bias
    block_out = (after_attn + gate_mlp * branch_mlp).astype(bf)

    grad_out = own_cotangent.astype(f32)
    grad_branch_mlp = (gate_mlp * grad_out).astype(bf)
    grad_gate_mlp = jnp.sum(grad_out * branch_mlp, axis=0)
    grad_down_bias = jnp.sum(grad_branch_mlp, axis=0, dtype=f32)
    grad_down = inner_rows(grad_branch_mlp, active).astype(bf)
    grad_active = product(grad_branch_mlp, full2)
    _, gelu_pull = jax.vjp(partial_gelu, upward)
    grad_upward = gelu_pull(grad_active)[0].astype(bf)
    grad_up_bias = jnp.sum(grad_upward, axis=0, dtype=f32)
    grad_up = inner_rows(normed_mlp, grad_upward).astype(bf)
    grad_normed_mlp = against(grad_upward, full1)
    _, mlp_pull = jax.vjp(modulate, after_attn, shift_mlp, scale_mlp)
    grad_after, grad_shift_mlp, grad_scale_mlp = mlp_pull(grad_normed_mlp)
    grad_after = grad_out + grad_after
    grad_branch_attn = (gate_attn * grad_after).astype(bf)
    grad_gate_attn = jnp.sum(grad_after * branch_attn, axis=0)
    grad_out_bias = jnp.sum(grad_branch_attn, axis=0, dtype=f32)
    grad_first, grad_normed_attn, bias_sums = att_bwd(
        normed_attn, grad_branch_attn, full0, qkv, mate_kv, attended, totals
    )
    _, attn_pull = jax.vjp(modulate, inputs, shift_attn, scale_attn)
    grad_inputs, grad_shift_attn, grad_scale_attn = attn_pull(grad_normed_attn)
    grad_tokens = grad_after + grad_inputs
    sums, block_rows, token_rows = scatter(
        grad_first, grad_up, grad_down, block_out, grad_tokens.astype(bf)
    )

    own_terms = jnp.concatenate(
        [
            grad_shift_attn, grad_scale_attn, grad_gate_attn[None],
            grad_shift_mlp, grad_scale_mlp, grad_gate_mlp[None],
        ],
        axis=0,
    ).reshape(4, 6 * COLS // 4)
    image_terms = lax.psum(own_terms, "core").astype(bf)
    four_images = lax.all_gather(image_terms, "z", axis=0)
    four_images = lax.dynamic_slice(four_images, (0, z, 0), (4, 1, image_terms.shape[1]))[:, 0]
    grad_modulation = lax.all_gather(four_images, ("y", "x"), axis=0, tiled=True)
    grad_ada_bias = jnp.sum(grad_modulation, axis=0, dtype=f32)
    grad_ada_weight = inner_rows(lifted_rows, grad_modulation)
    grad_lifted = lax.psum(against(grad_modulation, ada_weight), "z")
    by_batch = lax.all_gather(grad_lifted, ("y", "x", "core"), axis=0)
    own_lifted = lax.dynamic_slice(by_batch, (0, 2 * batch, 0), (8, 2, ROWS))
    own_lifted = jnp.swapaxes(own_lifted, 0, 1).reshape(2, 8 * ROWS)
    _, silu_pull = jax.vjp(jax.nn.silu, conditioning)
    grad_conditioning = silu_pull(own_lifted)[0]

    bias_vector = jnp.concatenate(
        [bias_sums.reshape(-1), grad_up_bias, grad_out_bias, grad_down_bias]
    )
    bias_total = lax.psum(bias_vector, AXES)
    first_bias = lax.dynamic_slice(bias_total, (z * COLS,), (COLS,))
    grad_query_bias = first_bias[:HS]
    grad_value_bias = first_bias[2 * HS : 3 * HS]
    grad_up_bias = lax.dynamic_slice(bias_total, ((4 + z) * COLS,), (COLS,))
    grad_out_bias = bias_total[8 * COLS : 9 * COLS]
    grad_down_bias = bias_total[9 * COLS :]

    peaks = lax.pmax(peak[:, 0, 0], AXES)
    limit = threshold[0]
    factor = jnp.sqrt(limit / jnp.maximum(lax.dynamic_slice(peaks, (4 * z,), (4,)), limit))
    column_factor = jnp.repeat(factor, HEAD_DIM)
    query_clipped = (query_weight.astype(f32) * column_factor).astype(bf)
    key_clipped = (key_weight.astype(f32) * column_factor).astype(bf)
    return (
        block_rows,
        token_rows.astype(f32),
        grad_conditioning,
        sums[0, :, :HS],
        sums[0, :, HS : 2 * HS],
        sums[0, :, 2 * HS : 3 * HS],
        sums[0, :, 3 * HS :].T,
        sums[1],
        sums[2].T,
        grad_ada_weight,
        grad_query_bias,
        grad_value_bias,
        grad_out_bias,
        grad_up_bias,
        grad_down_bias,
        grad_ada_bias,
        query_clipped,
        key_clipped,
        query_bias * column_factor,
    )


def solution(mesh):
    if dict(mesh.shape) == {"dp": 8, "tensor": 4}:
        mesh = Mesh(mesh.devices.reshape(2, 2, 2, 4), AXES)
        split, heads, body = ("y", "x", "core"), "z", one_image_per_chip
    else:
        split, heads, body = "dp", "tensor", local
    weight, turned, bias = P(split, heads), P(heads, split), P(heads)
    rows = P(split, heads, None)
    in_specs = (
        rows, P(split, None), rows, weight, weight, weight, turned, weight, turned, weight,
        bias, bias, P(), bias, P(), bias, P(),
    )
    out_specs = (
        rows, rows, P(split, None), weight, weight, weight, turned, weight, turned, weight,
        bias, bias, P(), bias, P(), bias, weight, weight, bias,
    )
    return jax.shard_map(body, mesh=mesh, in_specs=in_specs, out_specs=out_specs, check_vma=False)
```

```python
import functools
from functools import partial

import jax
import jax.numpy as jnp
from jax import lax
from jax.experimental import pallas as pl
from jax.experimental.pallas import tpu as pltpu
from jax.sharding import Mesh, PartitionSpec as P

HEAD_DIM = 72
epsilon = 1e-06
partial_gelu = partial(jax.nn.gelu, approximate=True)

def modulate_images(values, shift, scale):
    average = jnp.mean(values, axis=-1, keepdims=True)
    centred = values - average
    spread = jnp.mean(centred * centred, axis=-1, keepdims=True)
    return centred * lax.rsqrt(spread + epsilon) * (1.0 + scale[:, None, :]) + shift[:, None, :]


def product(left, right):
    return jnp.dot(left, right, preferred_element_type=jnp.float32)


def inner_rows(left, right):
    return lax.dot_general(
        left, right, (((0,), (0,)), ((), ())), preferred_element_type=jnp.float32
    )


def against(left, right):
    return lax.dot_general(
        left, right, (((1,), (1,)), ((), ())), preferred_element_type=jnp.float32
    )


def spread_rows(values):
    return lax.all_gather(values, "tensor", axis=1, tiled=True)


def fold_rows(values):
    return lax.psum_scatter(values, "tensor", scatter_dimension=1, tiled=True)


def spread_grads(values):
    return lax.all_gather(values, "tensor", axis=1, tiled=True)


def fold_grads(values):
    return lax.psum_scatter(values, "tensor", scatter_dimension=1, tiled=True)


def local(
    tokens,
    conditioning,
    cotangent,
    query_weight,
    key_weight,
    value_weight,
    out_weight,
    up_weight,
    down_weight,
    ada_weight,
    query_bias,
    value_bias,
    out_bias,
    up_bias,
    down_bias,
    ada_bias,
    threshold,
):
    images = tokens.shape[0]
    model_width = tokens.shape[2]
    gathered = (
        lax.all_gather(query_weight, "dp", axis=0, tiled=True),
        lax.all_gather(key_weight, "dp", axis=0, tiled=True),
        lax.all_gather(value_weight, "dp", axis=0, tiled=True),
        lax.all_gather(out_weight, "dp", axis=1, tiled=True),
        lax.all_gather(up_weight, "dp", axis=0, tiled=True),
        lax.all_gather(down_weight, "dp", axis=1, tiled=True),
        lax.all_gather(ada_weight, "dp", axis=0, tiled=True),
    )
    full_query, full_key, full_value, full_out, full_up, full_down, full_ada = gathered
    lifted_low = jax.nn.silu(conditioning).astype(jnp.bfloat16)
    own_columns = product(lifted_low, full_ada) + ada_bias
    modulation = lax.all_gather(own_columns, "tensor", axis=1, tiled=True)
    pieces = [
        modulation[:, piece_index * model_width : (piece_index + 1) * model_width]
        for piece_index in range(6)
    ]
    shift_attn, scale_attn, gate_attn, shift_mlp, scale_mlp, gate_mlp = pieces
    inputs = tokens.astype(jnp.float32)
    normed_attn = spread_rows(modulate_images(inputs, shift_attn, scale_attn).astype(jnp.bfloat16))
    length = normed_attn.shape[1]
    row_count = images * length
    flat_attn = normed_attn.reshape(row_count, model_width)
    local_width = full_query.shape[1]
    heads_here = local_width // HEAD_DIM
    queries = (product(flat_attn, full_query) + query_bias).astype(jnp.bfloat16)
    key_rows = product(flat_attn, full_key).astype(jnp.bfloat16)
    value_rows = (product(flat_attn, full_value) + value_bias).astype(jnp.bfloat16)
    block_rows = min(512, length)
    head_scale = HEAD_DIM ** (-0.5)

    def by_head(matrix):
        return matrix.reshape(images, length, heads_here, HEAD_DIM)

    def attend_image(bundle):
        queries_img, keys_img, values_img = bundle
        outputs, totals, highest = ([], [], [])
        for offset in range(0, length, block_rows):
            logits = (
                jnp.einsum(
                    "qhe,khe->hqk",
                    queries_img[offset : offset + block_rows],
                    keys_img,
                    preferred_element_type=jnp.float32,
                )
                * head_scale
            )
            row_top = jnp.max(logits, axis=2, keepdims=True)
            raised = jnp.exp(logits - row_top)
            summed = jnp.sum(raised, axis=2, keepdims=True)
            shares = (raised / summed).astype(jnp.bfloat16)
            outputs.append(
                jnp.einsum(
                    "hqk,khe->qhe", shares, values_img, preferred_element_type=jnp.float32
                ).astype(jnp.bfloat16)
            )
            totals.append(row_top[:, :, 0] + jnp.log(summed[:, :, 0]))
            highest.append(jnp.max(row_top[:, :, 0], axis=1))
        return (
            jnp.concatenate(outputs, 0),
            jnp.concatenate(totals, 1),
            jnp.max(jnp.stack(highest), axis=0),
        )

    attended, log_totals, image_peaks = lax.map(
        attend_image, (by_head(queries), by_head(key_rows), by_head(value_rows))
    )
    flat_attended = attended.reshape(row_count, local_width)
    branch_attn = (
        fold_rows(product(flat_attended, full_out).reshape(images, length, model_width)) + out_bias
    )
    after_attn = inputs + gate_attn[:, None, :] * branch_attn
    normed_mlp = spread_rows(modulate_images(after_attn, shift_mlp, scale_mlp).astype(jnp.bfloat16))
    flat_mlp = normed_mlp.reshape(row_count, model_width)
    upward = product(flat_mlp, full_up) + up_bias
    active = jax.nn.gelu(upward, approximate=True).astype(jnp.bfloat16)
    branch_mlp = (
        fold_rows(product(active, full_down).reshape(images, length, model_width)) + down_bias
    )
    block_out = (after_attn + gate_mlp[:, None, :] * branch_mlp).astype(jnp.bfloat16)
    peaks = lax.pmax(jnp.max(image_peaks, axis=0), "dp")
    again = (
        lax.all_gather(query_weight, "dp", axis=0, tiled=True),
        lax.all_gather(key_weight, "dp", axis=0, tiled=True),
        lax.all_gather(value_weight, "dp", axis=0, tiled=True),
        lax.all_gather(out_weight, "dp", axis=1, tiled=True),
        lax.all_gather(up_weight, "dp", axis=0, tiled=True),
        lax.all_gather(down_weight, "dp", axis=1, tiled=True),
        lax.all_gather(ada_weight, "dp", axis=0, tiled=True),
    )
    back_query, back_key, back_value, back_out, back_up, back_down, back_ada = again
    grad_out = cotangent.astype(jnp.float32)
    grad_branch_mlp = (gate_mlp[:, None, :] * grad_out).astype(jnp.bfloat16)
    grad_gate_mlp = jnp.sum(grad_out * branch_mlp, axis=1)
    flat_grad_mlp = spread_grads(grad_branch_mlp).reshape(row_count, model_width)
    grad_down_bias = jnp.sum(flat_grad_mlp, axis=0, dtype=jnp.float32)
    grad_down_weight = inner_rows(active, flat_grad_mlp)
    grad_active = against(flat_grad_mlp, back_down)
    _, gelu_pull = jax.vjp(partial(jax.nn.gelu, approximate=True), upward)
    grad_upward = gelu_pull(grad_active)[0].astype(jnp.bfloat16)
    grad_up_bias = jnp.sum(grad_upward, axis=0, dtype=jnp.float32)
    grad_up_weight = inner_rows(flat_mlp, grad_upward)
    grad_normed_mlp = fold_grads(against(grad_upward, back_up).reshape(images, length, model_width))
    _, mlp_pull = jax.vjp(modulate_images, after_attn, shift_mlp, scale_mlp)
    grad_after, grad_shift_mlp, grad_scale_mlp = mlp_pull(grad_normed_mlp)
    grad_after = grad_out + grad_after
    grad_branch_attn = (gate_attn[:, None, :] * grad_after).astype(jnp.bfloat16)
    grad_gate_attn = jnp.sum(grad_after * branch_attn, axis=1)
    flat_grad_attn = spread_grads(grad_branch_attn).reshape(row_count, model_width)
    grad_out_bias = jnp.sum(flat_grad_attn, axis=0, dtype=jnp.float32)
    grad_out_weight = inner_rows(flat_attended, flat_grad_attn)
    grad_attended = against(flat_grad_attn, back_out).astype(jnp.bfloat16)

    def attend_back(bundle):
        queries_img, keys_img, values_img, grads_img, totals_img = bundle
        query_parts = []
        grad_keys_img = jnp.zeros(keys_img.shape, jnp.float32)
        grad_values_img = jnp.zeros(values_img.shape, jnp.float32)
        for offset in range(0, length, block_rows):
            query_block = queries_img[offset : offset + block_rows]
            grad_block = grads_img[offset : offset + block_rows]
            logits = (
                jnp.einsum(
                    "qhe,khe->hqk", query_block, keys_img, preferred_element_type=jnp.float32
                )
                * head_scale
            )
            shares = jnp.exp(logits - totals_img[:, offset : offset + block_rows, None])
            grad_shares = jnp.einsum(
                "qhe,khe->hqk", grad_block, values_img, preferred_element_type=jnp.float32
            )
            row_inner = jnp.sum(shares * grad_shares, axis=2, keepdims=True)
            grad_logits = (shares * (grad_shares - row_inner)).astype(jnp.bfloat16)
            query_parts.append(
                (
                    jnp.einsum(
                        "hqk,khe->qhe", grad_logits, keys_img, preferred_element_type=jnp.float32
                    )
                    * head_scale
                ).astype(jnp.bfloat16)
            )
            grad_keys_img = (
                grad_keys_img
                + jnp.einsum(
                    "hqk,qhe->khe", grad_logits, query_block, preferred_element_type=jnp.float32
                )
                * head_scale
            )
            grad_values_img = grad_values_img + jnp.einsum(
                "hqk,qhe->khe",
                shares.astype(jnp.bfloat16),
                grad_block,
                preferred_element_type=jnp.float32,
            )
        return (
            jnp.concatenate(query_parts, 0),
            grad_keys_img.astype(jnp.bfloat16),
            grad_values_img.astype(jnp.bfloat16),
        )

    grad_queries, grad_keys, grad_values = lax.map(
        attend_back,
        (
            by_head(queries),
            by_head(key_rows),
            by_head(value_rows),
            by_head(grad_attended),
            log_totals,
        ),
    )
    grad_queries = grad_queries.reshape(row_count, local_width)
    grad_keys = grad_keys.reshape(row_count, local_width)
    grad_values = grad_values.reshape(row_count, local_width)
    grad_query_bias = jnp.sum(grad_queries, axis=0, dtype=jnp.float32)
    grad_value_bias = jnp.sum(grad_values, axis=0, dtype=jnp.float32)
    grad_query_weight = inner_rows(flat_attn, grad_queries)
    grad_key_weight = inner_rows(flat_attn, grad_keys)
    grad_value_weight = inner_rows(flat_attn, grad_values)
    partial_normed = (
        against(grad_queries, back_query)
        + against(grad_keys, back_key)
        + against(grad_values, back_value)
    )
    grad_normed_attn = fold_grads(partial_normed.reshape(images, length, model_width))
    _, attn_pull = jax.vjp(modulate_images, inputs, shift_attn, scale_attn)
    grad_inputs, grad_shift_attn, grad_scale_attn = attn_pull(grad_normed_attn)
    grad_tokens = grad_after + grad_inputs
    modulation_terms = jnp.concatenate(
        [
            grad_shift_attn,
            grad_scale_attn,
            grad_gate_attn,
            grad_shift_mlp,
            grad_scale_mlp,
            grad_gate_mlp,
        ],
        axis=1,
    )
    grad_modulation = lax.psum_scatter(
        modulation_terms, "tensor", scatter_dimension=1, tiled=True
    ).astype(jnp.bfloat16)
    grad_ada_bias = jnp.sum(grad_modulation, axis=0, dtype=jnp.float32)
    grad_ada_weight = inner_rows(lifted_low, grad_modulation)
    grad_lifted = lax.psum(against(grad_modulation, back_ada), "tensor")
    _, silu_pull = jax.vjp(jax.nn.silu, conditioning)
    grad_conditioning = silu_pull(grad_lifted)[0]
    weight_grads = (
        lax.psum_scatter(grad_query_weight, "dp", scatter_dimension=0, tiled=True),
        lax.psum_scatter(grad_key_weight, "dp", scatter_dimension=0, tiled=True),
        lax.psum_scatter(grad_value_weight, "dp", scatter_dimension=0, tiled=True),
        lax.psum_scatter(grad_out_weight, "dp", scatter_dimension=1, tiled=True),
        lax.psum_scatter(grad_up_weight, "dp", scatter_dimension=0, tiled=True),
        lax.psum_scatter(grad_down_weight, "dp", scatter_dimension=1, tiled=True),
        lax.psum_scatter(grad_ada_weight, "dp", scatter_dimension=0, tiled=True),
    )
    bias_grads = lax.psum(
        (
            grad_query_bias,
            grad_value_bias,
            grad_out_bias,
            grad_up_bias,
            grad_down_bias,
            grad_ada_bias,
        ),
        "dp",
    )
    limit = threshold[0]
    factor = jnp.sqrt(limit / jnp.maximum(peaks, limit))
    column_factor = jnp.repeat(factor, HEAD_DIM)
    query_clipped = (query_weight.astype(jnp.float32) * column_factor).astype(jnp.bfloat16)
    key_clipped = (key_weight.astype(jnp.float32) * column_factor).astype(jnp.bfloat16)
    query_bias_clipped = query_bias * column_factor
    return (
        block_out,
        grad_tokens,
        grad_conditioning,
        weight_grads[0],
        weight_grads[1],
        weight_grads[2],
        weight_grads[3],
        weight_grads[4],
        weight_grads[5],
        weight_grads[6],
        bias_grads[0],
        bias_grads[1],
        bias_grads[2],
        bias_grads[3],
        bias_grads[4],
        bias_grads[5],
        query_clipped,
        key_clipped,
        query_bias_clipped,
    )


HEAD_DIM=72; HS=288; KV0=256; KVW=640; AT0=768; ATW=384
C=HEAD_DIM**-0.5; LOG2E=1.4426950408889634
TOK=512
bf=jnp.bfloat16; f32=jnp.float32

def dg(a,b,ca,cb): return lax.dot_general(a,b,(((ca,),(cb,)),((),())),preferred_element_type=f32)

def partner():
    y,x,c,z=(lax.axis_index(a) for a in ("y","x","core","z"))
    return (y,x,1-c,z)

def greet_partner(dev):
    bar=pltpu.get_barrier_semaphore()
    pl.semaphore_signal(bar,inc=1,device_id=dev,device_id_type=MESH)
    pl.semaphore_wait(bar,1)

def att_fwd_kernel(x_ref,g0_ref,bias_ref,qkv_ref,kvo_ref,att_ref,lse_ref,peak_ref,branch_ref,w,qh,kh,vh,oh,wsem,ssem,rsem):
    dev=partner()
    for z in range(4): pltpu.make_async_copy(g0_ref.at[:,pl.ds(z*COLS,COLS)],w.at[z],wsem.at[z]).start()
    greet_partner(dev)
    def send(z):
        return pltpu.make_async_remote_copy(src_ref=qkv_ref.at[z,:,pl.ds(KV0,KVW)],dst_ref=kvo_ref.at[z],send_sem=ssem.at[z],recv_sem=rsem.at[z],device_id=dev,device_id_type=MESH)
    for z in range(4):
        pltpu.make_async_copy(g0_ref.at[:,pl.ds(z*COLS,COLS)],w.at[z],wsem.at[z]).wait()
        def tile(i,_):
            cols=pl.ds(pl.multiple_of(i*384,384),384)
            qkv_ref[z,:,cols]=(dg(x_ref[...],w[z,:,cols],1,0)+bias_ref[z,:,cols]).astype(bf)
            return 0
        lax.fori_loop(0,3,tile,0)
        send(z).start()
    branch_ref[...]=jnp.zeros_like(branch_ref)
    def chunk(z,_):
        send(z).wait_recv()
        for j in range(4):
            a=j*HEAD_DIM
            qh[j]=qkv_ref[z,:,a:a+HEAD_DIM]
            kh[j,:TOK]=qkv_ref[z,:,HS+a:HS+a+HEAD_DIM]
            vh[j,:TOK]=qkv_ref[z,:,2*HS+a:2*HS+a+HEAD_DIM]
            kh[j,TOK:]=kvo_ref[z,:,HS-KV0+a:HS-KV0+a+HEAD_DIM]
            vh[j,TOK:]=kvo_ref[z,:,2*HS-KV0+a:2*HS-KV0+a+HEAD_DIM]
        def head(j,_):
            h=z*4+j
            s=dg(kh[j],qh[j],1,1)
            m=jnp.max(s,axis=0,keepdims=True)
            p=jnp.exp2((s-m)*(C*LOG2E))
            l=jnp.sum(p,axis=0,keepdims=True)
            o=dg(vh[j],p.astype(bf),0,0)/l
            oh[j]=o.T.astype(bf)
            lse_ref[h]=m*(C*LOG2E)+jnp.log2(l)
            peak_ref[h]=jnp.broadcast_to(jnp.max(m,axis=1,keepdims=True)*C,(1,128))
            return 0
        lax.fori_loop(0,4,head,0)
        att_ref[z]=jnp.concatenate([jnp.zeros((TOK,ATW-HS),bf)]+[oh[j] for j in range(4)],axis=1)
        def tile(i,_):
            cols=pl.ds(pl.multiple_of(i*384,384),384)
            branch_ref[:,cols]+=dg(att_ref[z],w[z,cols,AT0:],1,1)
            return 0
        lax.fori_loop(0,3,tile,0)
        return 0
    lax.fori_loop(0,4,chunk,0)
    for z in range(4): send(z).wait_send()

VM=pl.BlockSpec(memory_space=pltpu.VMEM); HB=pl.BlockSpec(memory_space=pl.ANY)
S=jax.ShapeDtypeStruct
def att_fwd(x,g0,bias):
    D=pltpu.SemaphoreType.DMA
    return pl.pallas_call(att_fwd_kernel,name="att_fwd",
      out_shape=(S((4,TOK,COLS),bf),S((4,TOK,KVW),bf),S((4,TOK,ATW),bf),S((16,1,TOK),f32),S((16,1,128),f32),S((TOK,COLS),f32)),
      in_specs=[VM,HB,VM],out_specs=(VM,)*6,
      scratch_shapes=[pltpu.VMEM((4,COLS,COLS),bf),pltpu.VMEM((4,TOK,HEAD_DIM),bf),pltpu.VMEM((4,2*TOK,HEAD_DIM),bf),pltpu.VMEM((4,2*TOK,HEAD_DIM),bf),pltpu.VMEM((4,TOK,HEAD_DIM),bf),D((4,)),D((4,)),D((4,))],
      compiler_params=pltpu.CompilerParams(collective_id=3,has_side_effects=True,vmem_limit_bytes=58*2**20))(x,g0,bias)

def att_bwd_kernel(x_ref,gb_ref,g0_ref,qkv_ref,kvo_ref,att_ref,lse_ref,d0_ref,gx_ref,bsum_ref,w,qh,kh,vh,gh,dqh,dkh,dvh,mate_out,mate_in,pack,xt,gt,dbuf,wsem,ssem,rsem,dsem):
    dev=partner()
    def load(z): return pltpu.make_async_copy(g0_ref.at[:,pl.ds(pl.multiple_of(z*COLS,COLS),COLS)],w.at[lax.rem(z,2)],wsem.at[lax.rem(z,2)])
    load(0).start()
    greet_partner(dev)
    xt[...]=x_ref[...].T
    gt[...]=gb_ref[...].T
    gx_ref[...]=jnp.zeros_like(gx_ref)
    def send(z):
        return pltpu.make_async_remote_copy(src_ref=mate_out.at[z],dst_ref=mate_in.at[z],send_sem=ssem.at[z],recv_sem=rsem.at[z],device_id=dev,device_id_type=MESH)
    def store(z):
        return pltpu.make_async_copy(dbuf.at[lax.rem(z,2)],d0_ref.at[:,pl.ds(pl.multiple_of(z*COLS,COLS),COLS)],dsem.at[lax.rem(z,2)])
    def chunk(z,_):
        k2=lax.rem(z,2)
        load(z).wait()
        pl.when(z<3)(lambda: load(z+1).start())
        ga=dg(gb_ref[...],w[k2,:,AT0:],1,0).astype(bf)
        for j in range(4):
            a=j*HEAD_DIM
            gh[j]=ga[:,ATW-HS+a:ATW-HS+a+HEAD_DIM]
            qh[j]=qkv_ref[z,:,a:a+HEAD_DIM]
            kh[j,:TOK]=qkv_ref[z,:,HS+a:HS+a+HEAD_DIM]
            vh[j,:TOK]=qkv_ref[z,:,2*HS+a:2*HS+a+HEAD_DIM]
            kh[j,TOK:]=kvo_ref[z,:,HS-KV0+a:HS-KV0+a+HEAD_DIM]
            vh[j,TOK:]=kvo_ref[z,:,2*HS-KV0+a:2*HS-KV0+a+HEAD_DIM]
        def head(j,_):
            k=kh[j]; q=qh[j]; g=gh[j]
            p=jnp.exp2(dg(k,q,1,1)*(C*LOG2E)-lse_ref[z*4+j])
            t=p*dg(vh[j],g,1,1)
            inner=jnp.sum(t,axis=0,keepdims=True)
            ds=(t-p*inner).astype(bf)
            dvh[j]=dg(p.astype(bf),g,1,0)
            dkh[j]=dg(ds,q,1,0)*C
            dqh[j]=(dg(k,ds,0,0)*C).T.astype(bf)
            return 0
        lax.fori_loop(0,4,head,0)
        mate_out[z]=jnp.concatenate([dkh[j,TOK:].astype(bf) for j in range(4)]+[dvh[j,TOK:].astype(bf) for j in range(4)]+[jnp.zeros((TOK,KVW-2*HS),bf)],axis=1)
        send(z).start()
        send(z).wait_recv()
        o=mate_in[z].astype(f32)
        own=jnp.concatenate([dkh[j,:TOK] for j in range(4)]+[dvh[j,:TOK] for j in range(4)],axis=1)
        both=(own+o[:,:2*HS]).astype(bf)
        pack[...]=jnp.concatenate([dqh[j] for j in range(4)]+[both,jnp.zeros((TOK,HS),bf)],axis=1)
        bsum_ref[z]=jnp.sum(pack[...].astype(f32),axis=0,keepdims=True)
        pl.when(z>=2)(lambda: store(z-2).wait())
        def tile(i,_):
            cols=pl.ds(pl.multiple_of(i*384,384),384)
            gx_ref[:,cols]+=dg(pack[...],w[k2,cols,:],1,1)
            d1=dg(xt[cols],pack[:,:896],1,0)
            d2=dg(gt[cols],att_ref[z],1,0)
            dbuf[k2,cols,:AT0]=d1[:,:AT0].astype(bf)
            dbuf[k2,cols,AT0:896]=(d1[:,AT0:]+d2[:,:128]).astype(bf)
            dbuf[k2,cols,896:]=d2[:,128:].astype(bf)
            return 0
        lax.fori_loop(0,3,tile,0)
        store(z).start()
        return 0
    lax.fori_loop(0,4,chunk,0)
    store(2).wait(); store(3).wait()
    for z in range(4): send(z).wait_send()

def att_bwd(x,gb,g0,qkv,kvo,att,lse):
    D=pltpu.SemaphoreType.DMA; M=pltpu.VMEM
    return pl.pallas_call(att_bwd_kernel,name="att_bwd",
      out_shape=(S((COLS,4*COLS),bf),S((TOK,COLS),f32),S((4,1,COLS),f32)),
      in_specs=[VM,VM,HB,VM,VM,VM,VM],out_specs=(HB,VM,VM),
      scratch_shapes=[M((2,COLS,COLS),bf),M((4,TOK,HEAD_DIM),bf),M((4,2*TOK,HEAD_DIM),bf),M((4,2*TOK,HEAD_DIM),bf),M((4,TOK,HEAD_DIM),bf),
         M((4,TOK,HEAD_DIM),bf),M((4,2*TOK,HEAD_DIM),f32),M((4,2*TOK,HEAD_DIM),f32),M((4,TOK,KVW),bf),M((4,TOK,KVW),bf),M((TOK,COLS),bf),M((COLS,TOK),bf),M((COLS,TOK),bf),M((2,COLS,COLS),bf),
         D((2,)),D((4,)),D((4,)),D((2,))],
      compiler_params=pltpu.CompilerParams(collective_id=4,has_side_effects=True,vmem_limit_bytes=58*2**20))(x,gb,g0,qkv,kvo,att,lse)
class OldNet:
    def __init__(self):
        self.y,self.x,self.c,self.z=(lax.axis_index(a) for a in AXES)
        y,x,c,z=self.y,self.x,self.c,self.z
        self.zp=lax.rem(z+1,4); self.zm=lax.rem(z+3,4); self.zo=lax.rem(z+2,4)
        self.xn=(y,1-x,c,z); self.yn=(1-y,x,c,z); self.cn=(y,x,1-c,z)
        self.zpn=(y,x,c,self.zp); self.zmn=(y,x,c,self.zm)

def enter(net, column):
    bar=pltpu.get_barrier_semaphore()
    y,x,c,z=net.y,net.x,net.c,net.z
    others=[net.xn,net.yn]
    if column:
        for dc in range(2):
            for dz in range(4):
                if dc or dz: others.append((y,x,lax.rem(c+dc,2),lax.rem(z+dz,4)))
    else:
        others+= [net.cn,net.zpn,net.zmn]
    for o in others: pl.semaphore_signal(bar,inc=1,device_id=o,device_id_type=MESH)
    pl.semaphore_wait(bar,len(others))

ROWS=144; COLS=1152; TOP=80


class Scatter:
    def __init__(self, net, tensors, cc, d, rc, acc, tmp, far_in, near_in, line_in, out, send, core_sem, load_sem, tmp_sem, far_sem, near_sem, line_sem):
        self.__dict__.update(locals()); self.count=0; self.started=[]; self.pending=[]
        y,x=net.y,net.x
        self.far_dev=net.yn if cc==0 else net.xn
        self.near_dev=net.xn if cc==0 else net.yn
    def place(self, far, near):
        return (far,near) if self.cc==0 else (near,far)
    def mine(self):
        return (self.net.y,self.net.x) if self.cc==0 else (self.net.x,self.net.y)
    def remote(self, src, dst, dev, recv, cond=None):
        cp=pltpu.make_async_remote_copy(src_ref=src,dst_ref=dst,send_sem=self.send.at[self.count],recv_sem=recv,device_id=dev,device_id_type=MESH)
        self.count+=1
        if cond is None: cp.start()
        else: pl.when(cond)(cp.start)
        self.started.append((cond,cp))
    def slots(self):
        f,n=self.mine()
        return [(ff,nn,z) for ff in (1-f,f) for nn in (1-n,n) for z in (0,3,1,2)]
    def block(self,t,ff,nn,cc,z):
        yy,xx=self.place(ff,nn)
        row=(4*yy+2*xx+cc)*ROWS
        return self.d[t].at[pl.ds(pl.multiple_of(row,16),ROWS),pl.ds(z*COLS,COLS)]
    def begin(self,t):
        for ff,nn,z in self.slots():
            yy,xx=self.place(ff,nn)
            self.remote(self.block(t,ff,nn,1-self.cc,z),self.rc.at[t,yy,xx,z],self.net.cn,self.core_sem.at[t,yy,xx,z])
            pltpu.make_async_copy(self.block(t,ff,nn,self.cc,z),self.acc.at[t,yy,xx,z],self.load_sem.at[t,yy,xx,z]).start()
    def add(self,a,b):
        def one(i,_):
            r=pl.ds(pl.multiple_of(i*16,16),16)
            a[r]=(a[r].astype(jnp.float32)+b[r].astype(jnp.float32)).astype(a.dtype)
            return 0
        lax.fori_loop(0,ROWS//16,one,0)
    def core_steps(self,t):
        slots=self.slots()
        n=len(slots)
        def fetch(i):
            ff,nn,z=slots[i]; yy,xx=self.place(ff,nn); r=self.rc.at[t,yy,xx,z]
            pltpu.make_async_copy(r,r,self.core_sem.at[t,yy,xx,z]).wait()
            pltpu.make_async_copy(r,self.tmp.at[i%2],self.tmp_sem.at[i%2]).start()
        def step(i):
            if i==0: fetch(0)
            if i+1<n: fetch(i+1)
            ff,nn,z=slots[i]; yy,xx=self.place(ff,nn)
            a=self.acc.at[t,yy,xx,z]
            pltpu.make_async_copy(a,a,self.load_sem.at[t,yy,xx,z]).wait()
            pltpu.make_async_copy(self.rc.at[t,yy,xx,z],self.tmp.at[i%2],self.tmp_sem.at[i%2]).wait()
            self.add(a,self.tmp.at[i%2])
            if i<n//2: self.remote(a,self.far_in.at[t,nn,z],self.far_dev,self.far_sem.at[t,nn,z])
        return [functools.partial(step,i) for i in range(n)]
    def far_steps(self,t):
        f,n=self.mine()
        def step(nn,z,last):
            yy,xx=self.place(f,nn); a=self.acc.at[t,yy,xx,z]; r=self.far_in.at[t,nn,z]
            pltpu.make_async_copy(r,r,self.far_sem.at[t,nn,z]).wait()
            self.add(a,r)
            if not last: self.remote(a,self.near_in.at[t,z],self.near_dev,self.near_sem.at[t,z])
        return [functools.partial(step,nn,z,last) for nn,last in ((1-n,False),(n,True)) for z in (0,3,1,2)]
    def near_steps(self,t):
        net=self.net; z=net.z
        def step(zz):
            a=self.acc.at[t,net.y,net.x,zz]; r=self.near_in.at[t,zz]
            pltpu.make_async_copy(r,r,self.near_sem.at[t,zz]).wait()
            self.add(a,r)
            if zz==3:
                pl.when(z==0)(lambda: self.line_send(t,3,1))
            if zz==0:
                pl.when(z==3)(lambda: self.line_send(t,0,0))
        return [functools.partial(step,zz) for zz in (0,3,1,2)]
    def line_send(self,t,zz,up):
        pass
    def line_steps(self,t):
        net=self.net; z=net.z
        up_dev=(net.y,net.x,net.c,lax.rem(z+1,4)); down_dev=(net.y,net.x,net.c,lax.rem(z+3,4))
        def arrive(side,zz):
            r=self.line_in.at[t,side,zz]
            pltpu.make_async_copy(r,r,self.line_sem.at[t,side,zz]).wait()
            return r
        def up(zz):
            a=self.acc.at[t,net.y,net.x,zz]
            @pl.when(jnp.logical_and(z<zz,z>0))
            def _(): self.add(a,arrive(0,zz))
            self.remote(a,self.line_in.at[t,0,zz],up_dev,self.line_sem.at[t,0,zz],z<zz)
        def down(zz):
            a=self.acc.at[t,net.y,net.x,zz]
            @pl.when(jnp.logical_and(z>zz,z<3))
            def _(): self.add(a,arrive(1,zz))
            self.remote(a,self.line_in.at[t,1,zz],down_dev,self.line_sem.at[t,1,zz],z>zz)
        def last():
            a=self.acc.at[t,net.y,net.x,z]
            pl.when(z>0)(lambda: arrive(0,z) and None)
            pl.when(z<3)(lambda: arrive(1,z) and None)
            below=self.line_in.at[t,0,z]; above=self.line_in.at[t,1,z]
            def one(i,_):
                r=pl.ds(pl.multiple_of(i*16,16),16)
                v=a[r].astype(jnp.float32)
                v=v+jnp.where(z>0,below[r].astype(jnp.float32),0.0)
                v=v+jnp.where(z<3,above[r].astype(jnp.float32),0.0)
                self.out[t,r]=v
                return 0
            lax.fori_loop(0,ROWS//16,one,0)
        return [functools.partial(up,3),functools.partial(down,0),functools.partial(up,2),functools.partial(down,1),functools.partial(up,1),functools.partial(down,2),last]
    def finish(self):
        for cond,cp in self.started:
            if cond is None: cp.wait_send()
            else: pl.when(cond)(cp.wait_send)

def row_copies(net, pairs, send, recv):
    y,x,c,z=net.y,net.x,net.c,net.z
    dc=lax.div(z,2)
    def each(start):
        for a,(src,dst) in enumerate(pairs):
            for k in range(2):
                dz=2*c+k
                here=jnp.logical_and(dc==c,dz==z)
                rows=src.at[pl.ds(k*256,256)]; image=dst.at[lax.rem(z,2)]
                cp=pltpu.make_async_remote_copy(src_ref=rows,dst_ref=image,send_sem=send.at[a,k],recv_sem=recv.at[a,lax.rem(z,2)],device_id=(y,x,dc,dz),device_id_type=MESH)
                lc=pltpu.make_async_copy(rows,image,recv.at[a,lax.rem(z,2)])
                pl.when(jnp.logical_not(here))(cp.start if start else cp.wait_send)
                if start: pl.when(here)(lc.start)
    def arrivals():
        for a,(src,dst) in enumerate(pairs):
            for i in range(2):
                pltpu.make_async_copy(dst.at[i],dst.at[i],recv.at[a,i]).wait()
    return each,arrivals

def scatter_kernel(T, d0, d1, d2, r0, r1, out, rc, b0, b1, acc, tmp, far_in, near_in, line_in, row_send, row_recv, *sems):
    net=OldNet(); enter(net,True)
    each,arrivals=row_copies(net,((r0,b0),(r1,b1)),row_send,row_recv)
    each(True)
    def flow(cc):
        s=Scatter(net,T,cc,[d0,d1,d2],rc,acc,tmp,far_in,near_in,line_in,out,*sems)
        for t in range(T): s.begin(t)
        for t in range(T):
            for f in s.core_steps(t): f()
            if t>0:
                for f in s.far_steps(t-1): f()
            if t>1:
                for f in s.near_steps(t-2)+s.line_steps(t-2): f()
        for f in s.far_steps(T-1): f()
        for t in range(max(T-2,0),T):
            for f in s.near_steps(t)+s.line_steps(t): f()
        s.finish()
    pl.when(net.c==0)(lambda: flow(0))
    pl.when(net.c==1)(lambda: flow(1))
    arrivals(); each(False)

def scatter(d0,d1,d2,r0,r1):
    T=3; bf=jnp.bfloat16
    D=pltpu.SemaphoreType.DMA
    hbm=pl.BlockSpec(memory_space=pl.ANY)
    B=(ROWS,COLS)
    out=pl.pallas_call(functools.partial(scatter_kernel,T),name="scatter",
      out_shape=(jax.ShapeDtypeStruct((T,)+B,jnp.float32),jax.ShapeDtypeStruct((T,2,2,4)+B,bf))+(jax.ShapeDtypeStruct((2,256,COLS),bf),)*2,
      in_specs=[hbm]*5,out_specs=(pl.BlockSpec(memory_space=pltpu.VMEM),hbm,hbm,hbm),
      scratch_shapes=[pltpu.VMEM((T,2,2,4)+B,bf),pltpu.VMEM((2,)+B,bf),pltpu.VMEM((T,2,4)+B,bf),pltpu.VMEM((T,4)+B,bf),pltpu.VMEM((T,2,4)+B,bf),
         D((2,2)),D((2,2)),D((T*36,)),D((T,2,2,4)),D((T,2,2,4)),D((2,)),D((T,2,4)),D((T,4)),D((T,2,4))],
      compiler_params=pltpu.CompilerParams(collective_id=2,has_side_effects=True,vmem_limit_bytes=58*2**20))(d0,d1,d2,r0,r1)
    return out[0],out[2],out[3]
HEAD_DIM=72
epsilon=1e-06
MESH = pl.DeviceIdType.MESH
AXES = ("y", "x", "core", "z")
ROWS, COLS, TOK = 144, 1152, 512
HS, KV0, KVW, AT0, ATW, ADA = 288, 256, 640, 768, 384, 1728
C = HEAD_DIM**-0.5
LOG2E = 1.4426950408889634
bf = jnp.bfloat16
f32 = jnp.float32
VM = pl.BlockSpec(memory_space=pltpu.VMEM)
HB = pl.BlockSpec(memory_space=pl.ANY)
S = jax.ShapeDtypeStruct
D = pltpu.SemaphoreType.DMA
V = pltpu.VMEM


def dg(a, b, ca, cb):
    return lax.dot_general(a, b, (((ca,), (cb,)), ((), ())), preferred_element_type=f32)


class Net:
    def __init__(self):
        self.y, self.x, self.c, self.z = (lax.axis_index(a) for a in AXES)
        y, x, c, z = self.y, self.x, self.c, self.z
        self.up, self.down = lax.rem(z + 1, 4), lax.rem(z + 3, 4)
        self.xn, self.yn, self.dn = (y, 1 - x, c, z), (1 - y, x, c, z), (1 - y, 1 - x, c, z)
        self.cn = (y, x, 1 - c, z)
        self.zpn, self.zmn = (y, x, c, self.up), (y, x, c, self.down)
        self.f, self.n = self.place(y, x)
        self.far = self.device(1 - self.f, self.n)
        self.near = self.device(self.f, 1 - self.n)

    def place(self, a, b):
        return (1 - self.c) * a + self.c * b, (1 - self.c) * b + self.c * a

    def device(self, f, n):
        y, x = self.place(f, n)
        return (y, x, self.c, self.z)

    def along_z(self, step):
        return (self.y, self.x, self.c, lax.rem(self.z + step, 4))

    def greet(self):
        bar = pltpu.get_barrier_semaphore()
        others = [self.xn, self.yn, self.dn]
        for dc in range(2):
            for dz in range(4):
                if dc or dz:
                    others.append((self.y, self.x, lax.rem(self.c + dc, 2), lax.rem(self.z + dz, 4)))
        for o in others:
            pl.semaphore_signal(bar, inc=1, device_id=o, device_id_type=MESH)
        pl.semaphore_wait(bar, len(others))


def remote(src, dst, send, recv, device):
    return pltpu.make_async_remote_copy(
        src_ref=src, dst_ref=dst, send_sem=send, recv_sem=recv, device_id=device, device_id_type=MESH
    )


def landed(ref, sem):
    pltpu.make_async_copy(ref, ref, sem).wait()


def gelu_pair(u):
    k = 0.7978845608028654
    u2 = u * u
    t = jnp.tanh(k * u * (1.0 + 0.044715 * u2))
    h = 0.5 * (1.0 + t)
    return u * h, h + 0.5 * u * (1.0 - t * t) * (k * (1.0 + 3.0 * 0.044715 * u2))


class Gather:
    def __init__(self, net, g, shard, send, zsend, recv):
        self.net, self.g, self.shard, self.send, self.zsend, self.recv = net, g, shard, send, zsend, recv

    def slot(self, t, f, n, c, z):
        y, x = self.net.place(f, n)
        row = pl.multiple_of((4 * y + 2 * x + c) * ROWS, 16)
        return self.g.at[t, pl.ds(row, ROWS), pl.ds(pl.multiple_of(z * COLS, 128), COLS)]

    def sem(self, t, f, n, c, z):
        y, x = self.net.place(f, n)
        return self.recv.at[t, 4 * y + 2 * x + c, z]

    def put(self, u, k, device, f, n, z, own=False):
        t = lax.div(u, 4)
        s = self.slot(t, f, n, self.net.c, z)
        return remote(self.shard.at[t] if own else s, s, self.send.at[u, k], self.sem(t, f, n, self.net.c, z), device)

    def arrived(self, t, f, n, c, z):
        landed(self.slot(t, f, n, c, z), self.sem(t, f, n, c, z))

    def nth(self, k):
        z = self.net.z
        after = ((0, 1, 2, 3), (1, 0, 2, 3), (2, 3, 1, 0), (3, 2, 1, 0))
        return sum(
            jnp.where(jnp.logical_and(z == i, k == j), after[i][j], 0)
            for i in range(4) for j in range(4)
        )

    def onward(self, t, k, zz, act, own=False):
        net = self.net
        s = self.slot(t, net.f, net.n, net.c, zz)
        src = self.shard.at[t] if own else s
        sem = self.sem(t, net.f, net.n, net.c, zz)
        up = jnp.logical_and(zz <= net.z, net.z < 3)
        down = jnp.logical_and(zz >= net.z, net.z > 0)

        @pl.when(up)
        def _():
            act(remote(src, s, self.zsend.at[t, k, 0], sem, net.zpn))

        @pl.when(down)
        def _():
            act(remote(src, s, self.zsend.at[t, k, 1], sem, net.zmn))

    def copies(self, u, own=False):
        net = self.net
        zz = net.z if own else self.nth(lax.rem(u, 4))
        f, n = net.f, net.n
        return (
            [self.put(u, 0, net.near, f, n, zz, own), self.put(u, 1, net.far, f, n, zz, own), self.put(u, 2, net.cn, f, n, zz, own)],
            [self.put(u, 3, net.far, f, 1 - n, zz), self.put(u, 4, net.cn, f, 1 - n, zz), self.put(u, 5, net.cn, 1 - f, n, zz)],
            [self.put(u, 6, net.cn, 1 - f, 1 - n, zz)],
        )

    def line(self, u):
        t, k = lax.div(u, 4), lax.rem(u, 4)
        pl.when(k == 0)(lambda: self.onward(t, k, self.net.z, lambda cp: cp.start(), True))

        @pl.when(k > 0)
        def _():
            zz = self.nth(k)
            self.arrived(t, self.net.f, self.net.n, self.net.c, zz)
            self.onward(t, k, zz, lambda cp: cp.start())

    def spread(self, u):
        k = lax.rem(u, 4)

        @pl.when(k == 0)
        def _():
            for cp in self.copies(u, True)[0]:
                cp.start()

        @pl.when(k > 0)
        def _():
            for cp in self.copies(u)[0]:
                cp.start()

    def across(self, u):
        net, t = self.net, lax.div(u, 4)
        zz = self.nth(lax.rem(u, 4))
        a, b, d = self.copies(u)[1]
        self.arrived(t, net.f, 1 - net.n, net.c, zz)
        a.start()
        b.start()
        self.arrived(t, 1 - net.f, net.n, net.c, zz)
        d.start()

    def corner(self, u):
        net, t = self.net, lax.div(u, 4)
        self.arrived(t, 1 - net.f, 1 - net.n, net.c, self.nth(lax.rem(u, 4)))
        self.copies(u)[2][0].start()

    def do(self, *steps):
        for name, u in steps:
            getattr(self, name)(jnp.int32(u))

    def at(self, point, table):
        for p, steps in enumerate(table):
            pl.when(point == p)(lambda: self.do(*steps))

    def from_mate(self, t):
        def one(i, _):
            self.arrived(t, lax.div(i, 8), lax.rem(lax.div(i, 4), 2), 1 - self.net.c, lax.rem(i, 4))
            return 0

        lax.fori_loop(0, 16, one, 0)

    def finish(self):
        def one(u, _):
            for group in self.copies(u):
                for cp in group:
                    cp.wait_send()
            t, k = lax.div(u, 4), lax.rem(u, 4)
            self.onward(t, k, self.nth(k), lambda cp: cp.wait_send())
            return 0

        lax.fori_loop(0, 12, one, 0)


def rows_out(net, i):
    dc, dz = lax.div(net.z, 2), 2 * net.c + i
    here = jnp.logical_and(dc == net.c, dz == net.z)
    return (net.y, net.x, dc, dz), pl.multiple_of(lax.rem(net.z, 2) * 256, 256), here


class Rows:
    def __init__(self, net, src, dst, send, recv):
        self.net, self.src, self.dst, self.send, self.recv = net, src, dst, send, recv

    def each(self, start):
        for i in range(2):
            device, row, here = rows_out(self.net, i)
            rows = self.dst.at[pl.ds(row, 256)]
            sem = self.recv.at[lax.rem(self.net.z, 2)]

            @pl.when(jnp.logical_not(here))
            def _():
                cp = remote(self.src.at[i], rows, self.send.at[i], sem, device)
                cp.start() if start else cp.wait_send()

            if start:

                @pl.when(here)
                def _():
                    rows[...] = self.src[i]

    def arrivals(self):
        net = self.net
        for k in range(2):
            here = jnp.logical_and(lax.div(net.z, 2) == net.c, 2 * net.c + k == net.z)
            pl.when(jnp.logical_not(here))(lambda: landed(self.dst.at[pl.ds(k * 256, 256)], self.recv.at[k]))


def normalize(v):
    mean = jnp.mean(v, axis=-1, keepdims=True)
    centred = v - mean
    r = lax.rsqrt(jnp.mean(centred * centred, axis=-1, keepdims=True) + epsilon)
    return centred * r, r


def by_rows(step, body):
    def one(i, _):
        body(pl.ds(pl.multiple_of(i * step, step), step))
        return 0

    lax.fori_loop(0, TOK // step, one, 0)


TABLE = (
    (("line", 7), ("line", 8), ("spread", 7), ("spread", 8), ("across", 6)),
    (("corner", 5),),
    (("line", 9), ("corner", 6)),
    (("across", 7), ("line", 10), ("spread", 9)),
    (("line", 11), ("across", 8), ("corner", 7)),
    (("spread", 10),),
    (("spread", 11), ("corner", 8)),
    (("across", 9),),
    (("across", 10), ("corner", 9)),
    (("across", 11), ("corner", 10)),
    (("corner", 11),),
)


def forward_kernel(
    shard, tokens, cotangent, lift_own, ada, ada_bias, z_bias, out_bias,
    g, tok, cot, lift_rows, vectors, biases, x_out, qkv_out, kvo_out, att_out, lse, peak, branch_out, nm_out, act_out, gd_out, d2,
    tok_v, cot_v, lift, part, part_in, four, four_in, zall, x_ref, w, qkv, kvo, att, branch, qh, kh, vh, oh, gbt, act_buf, gd_buf, dbuf,
    gsend, gzsend, grecv, lsem, rsend, rrecv, small_send, small_recv, wsem, ksend, krecv, osem, asem, gdsem, dsem,
):
    net = Net()
    y, x, c, z = net.y, net.x, net.c, net.z
    plane = 2 * y + x
    net.greet()
    flow = Gather(net, g, shard, gsend, gzsend, grecv)
    lift[plane, c] = lift_own[...]
    small = [remote(lift.at[plane, c], lift.at[plane, c], small_send.at[0], small_recv.at[0], net.cn)]
    small[0].start()
    token_rows = Rows(net, tokens, tok_v, rsend.at[0], rrecv.at[0])
    cot_rows = Rows(net, cotangent, cot_v, rsend.at[1], rrecv.at[1])
    flow.do(("line", 0))
    own = [pltpu.make_async_copy(shard.at[t], flow.slot(t, net.f, net.n, c, z), lsem.at[t]) for t in range(3)]
    for cp in own:
        cp.start()

    landed(lift.at[plane, 1 - c], small_recv.at[0])
    peers = ((net.xn, 2 * y + 1 - x), (net.yn, 2 - 2 * y + x), (net.dn, 3 - plane))
    for k, (dev, _) in enumerate(peers):
        cp = remote(lift.at[plane], lift.at[plane], small_send.at[1 + k], small_recv.at[1 + k], dev)
        cp.start()
        small.append(cp)
    flow.do(("spread", 0), ("spread", 4), ("line", 1))
    for k, (_, p) in enumerate(peers):
        landed(lift.at[p], small_recv.at[1 + k])
    every = jnp.concatenate([lift[p, k, 0:2] for p in range(4) for k in range(2)], axis=0).astype(bf)
    batch = 4 * y + 2 * x + c
    pick = lax.broadcasted_iota(jnp.int32, (COLS, ROWS), 0) == lax.broadcasted_iota(jnp.int32, (COLS, ROWS), 1) + batch * ROWS
    rows = dg(every, jnp.where(pick, 1.0, 0.0).astype(bf), 1, 0)
    lift_rows[...] = rows
    partial = dg(rows.astype(bf), ada[...], 1, 0)
    part[...] = jnp.zeros_like(part)
    for p in range(4):
        part[p, 0:4] = partial[4 * p : 4 * p + 4]
    for k, (dev, p) in enumerate(peers):
        cp = remote(part.at[p], part_in.at[k], small_send.at[4 + k], small_recv.at[4 + k], dev)
        cp.start()
        small.append(cp)
    flow.do(("spread", 1), ("line", 2), ("across", 0))
    token_rows.each(True)
    flow.do(("spread", 2), ("line", 3))
    for k in range(3):
        landed(part_in.at[k], small_recv.at[4 + k])
    four[...] = part[plane] + part_in[0] + part_in[1] + part_in[2]
    cp = remote(four, four_in, small_send.at[7], small_recv.at[7], net.cn)
    cp.start()
    small.append(cp)
    flow.do(("across", 4), ("line", 4), ("spread", 3), ("across", 1), ("corner", 0))
    landed(four_in, small_recv.at[7])
    zall[z] = four[...] + four_in[...] + ada_bias[...]
    zall[z, 4:5] = z_bias[...]
    for k in range(3):
        cp = remote(zall.at[z], zall.at[z], small_send.at[8 + k], small_recv.at[8 + k], net.along_z(k + 1))
        cp.start()
        small.append(cp)
    flow.do(("across", 2), ("corner", 4))
    for k in range(3):
        landed(zall.at[lax.rem(z + 3 - k, 4)], small_recv.at[8 + k])
    pieces = [zall[k, pl.ds(z, 1)] for k in range(4)]
    half = COLS // 2
    vectors[0:1] = pieces[0][:, :COLS]
    vectors[1:2] = jnp.concatenate([pieces[0][:, COLS:], pieces[1][:, :half]], axis=1)
    vectors[2:3] = pieces[1][:, half:]
    vectors[3:4] = pieces[2][:, :COLS]
    vectors[4:5] = jnp.concatenate([pieces[2][:, COLS:], pieces[3][:, :half]], axis=1)
    vectors[5:6] = pieces[3][:, half:]
    vectors[6:8] = jnp.zeros((2, COLS), f32)
    nothing = jnp.zeros((1, HS), f32)
    for k in range(4):
        b = zall[k, 4:5]
        biases[k, 0:1] = jnp.concatenate([b[:, :HS], nothing, b[:, HS : 2 * HS], nothing], axis=1)
        biases[k, 1:2] = b[:, 2 * HS :]

    flow.do(("across", 3), ("corner", 1), ("line", 5), ("spread", 5), ("corner", 2))
    token_rows.arrivals()

    def first_norm(r):
        n, _ = normalize(tok_v[r].astype(f32))
        x_ref[r] = (n * (1.0 + vectors[1:2]) + vectors[0:1]).astype(bf)

    by_rows(64, first_norm)
    outs = [pltpu.make_async_copy(x_ref, x_out, osem.at[1]), pltpu.make_async_copy(tok_v, tok, osem.at[0])]
    for cp in outs:
        cp.start()
    flow.do(("corner", 3), ("line", 6), ("spread", 6), ("across", 5))
    flow.from_mate(0)

    def load_w(t, k):
        return pltpu.make_async_copy(g.at[t, :, pl.ds(k * COLS, COLS)], w.at[k], wsem.at[k])

    own[0].wait()
    for k in range(4):
        load_w(0, k).start()

    def kv(k):
        return remote(qkv.at[k, :, pl.ds(KV0, KVW)], kvo.at[k], ksend.at[k], krecv.at[k], net.cn)

    for k in range(4):
        load_w(0, k).wait()
        qkv[k] = (dg(x_ref[...], w[k], 1, 0) + biases[k, 0:1]).astype(bf)
        kv(k).start()
    cp = pltpu.make_async_copy(qkv, qkv_out, osem.at[2])
    cp.start()
    outs.append(cp)
    branch[...] = jnp.broadcast_to(out_bias[...], (TOK, COLS))


    def chunk(k, _):
        flow.at(2 * k, TABLE)
        pl.when(k == 2)(lambda: cot_rows.each(True))
        kv(k).wait_recv()
        for j in range(4):
            a = j * HEAD_DIM
            qh[j] = qkv[k, :, a : a + HEAD_DIM]
            kh[j, :TOK] = qkv[k, :, HS + a : HS + a + HEAD_DIM]
            vh[j, :TOK] = qkv[k, :, 2 * HS + a : 2 * HS + a + HEAD_DIM]
            kh[j, TOK:] = kvo[k, :, HS - KV0 + a : HS - KV0 + a + HEAD_DIM]
            vh[j, TOK:] = kvo[k, :, 2 * HS - KV0 + a : 2 * HS - KV0 + a + HEAD_DIM]

        def head(j, _):
            h = k * 4 + j
            s = dg(kh[j], qh[j], 1, 1)
            m = jnp.max(s, axis=0, keepdims=True)
            p = jnp.exp2((s - m) * (C * LOG2E))
            l = jnp.sum(p, axis=0, keepdims=True)
            o = dg(vh[j], p.astype(bf), 0, 0) / l
            oh[j] = o.T.astype(bf)
            lse[h] = m * (C * LOG2E) + jnp.log2(l)
            peak[h] = jnp.broadcast_to(jnp.max(m, axis=1, keepdims=True) * C, (1, 128))
            pl.when(j == 1)(lambda: flow.at(2 * k + 1, TABLE))
            return 0

        lax.fori_loop(0, 4, head, 0)
        att[k] = jnp.concatenate([jnp.zeros((TOK, ATW - HS), bf)] + [oh[j] for j in range(4)], axis=1)
        branch[...] += dg(att[k], w[k, :, AT0:], 1, 1)
        return 0

    lax.fori_loop(0, 4, chunk, 0)
    for src, dst, k in ((kvo, kvo_out, 3), (att, att_out, 4), (branch, branch_out, 5)):
        cp = pltpu.make_async_copy(src, dst, osem.at[k])
        cp.start()
        outs.append(cp)
    outs[0].wait()

    def second_norm(r):
        after = tok_v[r].astype(f32) + vectors[2:3] * branch[r]
        n, _ = normalize(after)
        x_ref[r] = (n * (1.0 + vectors[4:5]) + vectors[3:4]).astype(bf)

    by_rows(64, second_norm)
    cp = pltpu.make_async_copy(x_ref, nm_out, osem.at[6])
    cp.start()
    outs[0] = cp
    flow.from_mate(1)
    own[1].wait()
    for k in range(4):
        load_w(1, k).start()

    def slope_store(k):
        i = lax.rem(k, 2)
        return pltpu.make_async_copy(gd_buf.at[i], gd_out.at[k], gdsem.at[i])

    def hidden(k, _):
        i = lax.rem(k, 2)
        pltpu.make_async_copy(g.at[1, :, pl.ds(pl.multiple_of(k * COLS, 128), COLS)], w.at[k], wsem.at[k]).wait()
        pl.when(k >= 2)(lambda: slope_store(k - 2).wait())
        gd_buf[i] = dg(x_ref[...], w[k], 1, 0)

        def activate(r):
            a, d = gelu_pair(gd_buf[i, r] + biases[k, 1:2])
            act_buf[k, r] = a.astype(bf)
            gd_buf[i, r] = d

        by_rows(64, activate)
        slope_store(k).start()
        pltpu.make_async_copy(act_buf.at[k], act_out.at[k], asem.at[k]).start()
        flow.at(8 + k, TABLE)
        return 0

    lax.fori_loop(0, 4, hidden, 0)
    cot_rows.arrivals()
    cp = pltpu.make_async_copy(cot_v, cot, osem.at[1])
    cp.start()
    outs.append(cp)

    def gated(r):
        x_ref[r] = (vectors[5:6] * cot_v[r].astype(f32)).astype(bf)

    outs[0].wait()
    by_rows(64, gated)
    gbt[...] = x_ref[...].T

    def down_store(k):
        i = lax.rem(k, 2)
        return pltpu.make_async_copy(dbuf.at[i], d2.at[:, pl.ds(pl.multiple_of(k * COLS, 128), COLS)], dsem.at[i])

    def down(k, _):
        i = lax.rem(k, 2)
        pl.when(k >= 2)(lambda: down_store(k - 2).wait())
        dbuf[i] = dg(gbt[...], act_buf[k], 1, 0).astype(bf)
        down_store(k).start()
        return 0

    lax.fori_loop(0, 4, down, 0)
    for k in (2, 3):
        slope_store(k).wait()
        down_store(k).wait()
    for k in range(4):
        pltpu.make_async_copy(act_buf.at[k], act_out.at[k], asem.at[k]).wait()
    flow.from_mate(2)
    flow.finish()
    for cp in outs[1:]:
        cp.wait()
    for k in range(4):
        kv(k).wait_send()
    for cp in small:
        cp.wait_send()
    own[2].wait()
    token_rows.each(False)
    cot_rows.each(False)


def forward(shard, tokens, cotangent, lift_own, ada, ada_bias, z_bias, out_bias):
    rows = S((TOK, COLS), bf)
    wide = S((TOK, COLS), f32)
    return pl.pallas_call(
        forward_kernel,
        name="forward",
        out_shape=(
            S((3, 8 * ROWS, 4 * COLS), bf), rows, rows, S((16, ROWS), f32), S((8, COLS), f32), S((4, 2, COLS), f32),
            rows, S((4, TOK, COLS), bf), S((4, TOK, KVW), bf), S((4, TOK, ATW), bf), S((16, 1, TOK), f32),
            S((16, 1, 128), f32), wide, rows, S((4, TOK, COLS), bf), S((4, TOK, COLS), f32), S((8 * ROWS, 4 * COLS), bf),
        ),
        in_specs=[VM] * 8,
        out_specs=(HB, HB, HB, VM, VM, VM, HB, HB, HB, HB, VM, VM, HB, HB, HB, HB, HB),
        scratch_shapes=[
            V((TOK, COLS), bf), V((TOK, COLS), bf), V((4, 2, 8, COLS), f32), V((4, 8, ADA), f32), V((3, 8, ADA), f32),
            V((8, ADA), f32), V((8, ADA), f32), V((4, 8, ADA), f32), V((TOK, COLS), bf), V((4, COLS, COLS), bf),
            V((4, TOK, COLS), bf), V((4, TOK, KVW), bf), V((4, TOK, ATW), bf), V((TOK, COLS), f32),
            V((4, TOK, HEAD_DIM), bf), V((4, 2 * TOK, HEAD_DIM), bf), V((4, 2 * TOK, HEAD_DIM), bf), V((4, TOK, HEAD_DIM), bf),
            V((COLS, TOK), bf), V((4, TOK, COLS), bf), V((2, TOK, COLS), f32), V((2, COLS, COLS), bf),
            D((12, 7)), D((3, 4, 2)), D((3, 8, 4)), D((3,)), D((2, 2)), D((2, 2)), D((11,)), D((11,)), D((4,)), D((4,)), D((4,)),
            D((7,)), D((4,)), D((2,)), D((2,)),
        ],
        compiler_params=pltpu.CompilerParams(collective_id=1, has_side_effects=True, vmem_limit_bytes=60 * 2**20),
    )(shard, tokens, cotangent, lift_own, ada, ada_bias, z_bias, out_bias)

def modulate(values, shift, scale):
    average = jnp.mean(values, axis=-1, keepdims=True)
    centred = values - average
    spread = jnp.mean(centred * centred, axis=-1, keepdims=True)
    return centred * lax.rsqrt(spread + epsilon) * (1.0 + scale) + shift


def one_image_per_chip(
    tokens, conditioning, cotangent, query_weight, key_weight, value_weight, out_weight, up_weight,
    down_weight, ada_weight, query_bias, value_bias, out_bias, up_bias, down_bias, ada_bias, threshold,
):
    y, x, c, z = (lax.axis_index(a) for a in AXES)
    plane = 2 * y + x
    batch = 4 * y + 2 * x + c
    first = jnp.concatenate([query_weight, key_weight, value_weight, out_weight.T], axis=1)
    shard = jnp.stack([first, up_weight, down_weight.T])
    lift_own = jnp.pad(jax.nn.silu(conditioning).astype(bf).astype(f32), ((0, 6), (0, 0)))
    z_bias = jnp.concatenate([query_bias, value_bias, up_bias])[None]
    (
        full, own_tokens, own_cotangent, lifted_rows, vectors, biases, normed_attn, qkv, mate_kv, attended, totals,
        peak, branch_attn, normed_mlp, active, slope, grad_down,
    ) = forward(shard, tokens, cotangent, lift_own, ada_weight, ada_bias[None], z_bias, out_bias[None])
    lifted_rows = lifted_rows.astype(bf)
    shift_attn, scale_attn, gate_attn, shift_mlp, scale_mlp, gate_mlp = [vectors[i : i + 1] for i in range(6)]
    full0, full1, full2 = full[0], full[1], full[2]
    inputs = own_tokens.astype(f32)
    after_attn = inputs + gate_attn * branch_attn
    active = jnp.swapaxes(active, 0, 1).reshape(TOK, 4 * COLS)
    slope = jnp.swapaxes(slope, 0, 1).reshape(TOK, 4 * COLS)
    branch_mlp = against(active, full2) + down_bias
    block_out = (after_attn + gate_mlp * branch_mlp).astype(bf)

    grad_out = own_cotangent.astype(f32)
    grad_branch_mlp = (gate_mlp * grad_out).astype(bf)
    grad_gate_mlp = jnp.sum(grad_out * branch_mlp, axis=0)
    grad_down_bias = jnp.sum(grad_branch_mlp, axis=0, dtype=f32)
    grad_active = product(grad_branch_mlp, full2)
    grad_upward = (grad_active * slope).astype(bf)
    grad_up_bias = jnp.sum(grad_upward, axis=0, dtype=f32)
    grad_up = inner_rows(normed_mlp, grad_upward).astype(bf)
    grad_normed_mlp = against(grad_upward, full1)
    _, mlp_pull = jax.vjp(modulate, after_attn, shift_mlp, scale_mlp)
    grad_after, grad_shift_mlp, grad_scale_mlp = mlp_pull(grad_normed_mlp)
    grad_after = grad_out + grad_after
    grad_branch_attn = (gate_attn * grad_after).astype(bf)
    grad_gate_attn = jnp.sum(grad_after * branch_attn, axis=0)
    grad_out_bias = jnp.sum(grad_branch_attn, axis=0, dtype=f32)
    grad_first, grad_normed_attn, bias_sums = att_bwd(
        normed_attn, grad_branch_attn, full0, qkv, mate_kv, attended, totals
    )
    _, attn_pull = jax.vjp(modulate, inputs, shift_attn, scale_attn)
    grad_inputs, grad_shift_attn, grad_scale_attn = attn_pull(grad_normed_attn)
    grad_tokens = grad_after + grad_inputs
    sums, block_rows, token_rows = scatter(
        grad_first, grad_up, grad_down, block_out, grad_tokens.astype(bf)
    )

    own_terms = jnp.concatenate(
        [
            grad_shift_attn, grad_scale_attn, grad_gate_attn[None],
            grad_shift_mlp, grad_scale_mlp, grad_gate_mlp[None],
        ],
        axis=0,
    ).reshape(4, 6 * COLS // 4)
    image_terms = lax.psum(own_terms, "core").astype(bf)
    four_images = lax.all_gather(image_terms, "z", axis=0)
    four_images = lax.dynamic_slice(four_images, (0, z, 0), (4, 1, image_terms.shape[1]))[:, 0]
    grad_modulation = lax.all_gather(four_images, ("y", "x"), axis=0, tiled=True)
    grad_ada_bias = jnp.sum(grad_modulation, axis=0, dtype=f32)
    grad_ada_weight = inner_rows(lifted_rows, grad_modulation)
    grad_lifted = lax.psum(against(grad_modulation, ada_weight), "z")
    by_batch = lax.all_gather(grad_lifted, ("y", "x", "core"), axis=0)
    own_lifted = lax.dynamic_slice(by_batch, (0, 2 * batch, 0), (8, 2, ROWS))
    own_lifted = jnp.swapaxes(own_lifted, 0, 1).reshape(2, 8 * ROWS)
    _, silu_pull = jax.vjp(jax.nn.silu, conditioning)
    grad_conditioning = silu_pull(own_lifted)[0]

    bias_vector = jnp.concatenate(
        [bias_sums.reshape(-1), grad_up_bias, grad_out_bias, grad_down_bias]
    )
    bias_total = lax.psum(bias_vector, AXES)
    first_bias = lax.dynamic_slice(bias_total, (z * COLS,), (COLS,))
    grad_query_bias = first_bias[:HS]
    grad_value_bias = first_bias[2 * HS : 3 * HS]
    grad_up_bias = lax.dynamic_slice(bias_total, ((4 + z) * COLS,), (COLS,))
    grad_out_bias = bias_total[8 * COLS : 9 * COLS]
    grad_down_bias = bias_total[9 * COLS :]

    peaks = lax.pmax(peak[:, 0, 0], AXES)
    limit = threshold[0]
    factor = jnp.sqrt(limit / jnp.maximum(lax.dynamic_slice(peaks, (4 * z,), (4,)), limit))
    column_factor = jnp.repeat(factor, HEAD_DIM)
    query_clipped = (query_weight.astype(f32) * column_factor).astype(bf)
    key_clipped = (key_weight.astype(f32) * column_factor).astype(bf)
    return (
        block_rows,
        token_rows.astype(f32),
        grad_conditioning,
        sums[0, :, :HS],
        sums[0, :, HS : 2 * HS],
        sums[0, :, 2 * HS : 3 * HS],
        sums[0, :, 3 * HS :].T,
        sums[1],
        sums[2].T,
        grad_ada_weight,
        grad_query_bias,
        grad_value_bias,
        grad_out_bias,
        grad_up_bias,
        grad_down_bias,
        grad_ada_bias,
        query_clipped,
        key_clipped,
        query_bias * column_factor,
    )


def solution(mesh):
    if dict(mesh.shape) == {"dp": 8, "tensor": 4}:
        mesh = Mesh(mesh.devices.reshape(2, 2, 2, 4), AXES)
        split, heads, body = ("y", "x", "core"), "z", one_image_per_chip
    else:
        split, heads, body = "dp", "tensor", local
    weight, turned, bias = P(split, heads), P(heads, split), P(heads)
    rows = P(split, heads, None)
    in_specs = (
        rows, P(split, None), rows, weight, weight, weight, turned, weight, turned, weight,
        bias, bias, P(), bias, P(), bias, P(),
    )
    out_specs = (
        rows, rows, P(split, None), weight, weight, weight, turned, weight, turned, weight,
        bias, bias, P(), bias, P(), bias, weight, weight, bias,
    )
    return jax.shard_map(body, mesh=mesh, in_specs=in_specs, out_specs=out_specs, check_vma=False)
```

```python
from functools import partial

import jax
import jax.numpy as jnp
from jax import lax
from jax.experimental import pallas as pl
from jax.experimental.pallas import tpu as pltpu
from jax.sharding import Mesh, PartitionSpec as P

HEAD_DIM=72
epsilon=1e-06
MESH = pl.DeviceIdType.MESH
AXES = ("y", "x", "core", "z")
ROWS, COLS, TOK = 144, 1152, 512
HS, KV0, KVW, AT0, ATW, ADA = 288, 256, 640, 768, 384, 1728
C = HEAD_DIM**-0.5
LOG2E = 1.4426950408889634
bf = jnp.bfloat16
f32 = jnp.float32
VM = pl.BlockSpec(memory_space=pltpu.VMEM)
HB = pl.BlockSpec(memory_space=pl.ANY)
S = jax.ShapeDtypeStruct
D = pltpu.SemaphoreType.DMA
V = pltpu.VMEM


def dg(a, b, ca, cb):
    return lax.dot_general(a, b, (((ca,), (cb,)), ((), ())), preferred_element_type=f32)


class Net:
    def __init__(self):
        self.y, self.x, self.c, self.z = (lax.axis_index(a) for a in AXES)
        y, x, c, z = self.y, self.x, self.c, self.z
        self.up, self.down = lax.rem(z + 1, 4), lax.rem(z + 3, 4)
        self.xn, self.yn, self.dn = (y, 1 - x, c, z), (1 - y, x, c, z), (1 - y, 1 - x, c, z)
        self.cn = (y, x, 1 - c, z)
        self.zpn, self.zmn = (y, x, c, self.up), (y, x, c, self.down)
        self.f, self.n = self.place(y, x)
        self.far = self.device(1 - self.f, self.n)
        self.near = self.device(self.f, 1 - self.n)

    def place(self, a, b):
        return (1 - self.c) * a + self.c * b, (1 - self.c) * b + self.c * a

    def device(self, f, n):
        y, x = self.place(f, n)
        return (y, x, self.c, self.z)

    def along_z(self, step):
        return (self.y, self.x, self.c, lax.rem(self.z + step, 4))

    def greet(self):
        bar = pltpu.get_barrier_semaphore()
        others = [self.xn, self.yn, self.dn]
        for dc in range(2):
            for dz in range(4):
                if dc or dz:
                    others.append((self.y, self.x, lax.rem(self.c + dc, 2), lax.rem(self.z + dz, 4)))
        for o in others:
            pl.semaphore_signal(bar, inc=1, device_id=o, device_id_type=MESH)
        pl.semaphore_wait(bar, len(others))


def remote(src, dst, send, recv, device):
    return pltpu.make_async_remote_copy(
        src_ref=src, dst_ref=dst, send_sem=send, recv_sem=recv, device_id=device, device_id_type=MESH
    )


def landed(ref, sem):
    pltpu.make_async_copy(ref, ref, sem).wait()


def gelu_pair(u):
    k = 0.7978845608028654
    u2 = u * u
    t = jnp.tanh(k * u * (1.0 + 0.044715 * u2))
    h = 0.5 * (1.0 + t)
    return u * h, h + 0.5 * u * (1.0 - t * t) * (k * (1.0 + 3.0 * 0.044715 * u2))


class Gather:
    def __init__(self, net, g, shard, send, zsend, recv):
        self.net, self.g, self.shard, self.send, self.zsend, self.recv = net, g, shard, send, zsend, recv

    def slot(self, t, f, n, c, z):
        y, x = self.net.place(f, n)
        row = pl.multiple_of((4 * y + 2 * x + c) * ROWS, 16)
        return self.g.at[t, pl.ds(row, ROWS), pl.ds(pl.multiple_of(z * COLS, 128), COLS)]

    def sem(self, t, f, n, c, z):
        y, x = self.net.place(f, n)
        return self.recv.at[t, 4 * y + 2 * x + c, z]

    def put(self, u, k, device, f, n, z, own=False):
        t = lax.div(u, 4)
        s = self.slot(t, f, n, self.net.c, z)
        return remote(self.shard.at[t] if own else s, s, self.send.at[u, k], self.sem(t, f, n, self.net.c, z), device)

    def arrived(self, t, f, n, c, z):
        landed(self.slot(t, f, n, c, z), self.sem(t, f, n, c, z))

    def nth(self, k):
        z = self.net.z
        after = ((0, 1, 2, 3), (1, 0, 2, 3), (2, 3, 1, 0), (3, 2, 1, 0))
        return sum(
            jnp.where(jnp.logical_and(z == i, k == j), after[i][j], 0)
            for i in range(4) for j in range(4)
        )

    def onward(self, t, k, zz, act, own=False):
        net = self.net
        s = self.slot(t, net.f, net.n, net.c, zz)
        src = self.shard.at[t] if own else s
        sem = self.sem(t, net.f, net.n, net.c, zz)
        up = jnp.logical_and(zz <= net.z, net.z < 3)
        down = jnp.logical_and(zz >= net.z, net.z > 0)

        @pl.when(up)
        def _():
            act(remote(src, s, self.zsend.at[t, k, 0], sem, net.zpn))

        @pl.when(down)
        def _():
            act(remote(src, s, self.zsend.at[t, k, 1], sem, net.zmn))

    def copies(self, u, own=False):
        net = self.net
        zz = net.z if own else self.nth(lax.rem(u, 4))
        f, n = net.f, net.n
        return (
            [self.put(u, 0, net.near, f, n, zz, own), self.put(u, 1, net.far, f, n, zz, own), self.put(u, 2, net.cn, f, n, zz, own)],
            [self.put(u, 3, net.far, f, 1 - n, zz), self.put(u, 4, net.cn, f, 1 - n, zz), self.put(u, 5, net.cn, 1 - f, n, zz)],
            [self.put(u, 6, net.cn, 1 - f, 1 - n, zz)],
        )

    def line(self, u):
        t, k = lax.div(u, 4), lax.rem(u, 4)
        pl.when(k == 0)(lambda: self.onward(t, k, self.net.z, lambda cp: cp.start(), True))

        @pl.when(k > 0)
        def _():
            zz = self.nth(k)
            self.arrived(t, self.net.f, self.net.n, self.net.c, zz)
            self.onward(t, k, zz, lambda cp: cp.start())

    def spread(self, u):
        k = lax.rem(u, 4)

        @pl.when(k == 0)
        def _():
            for cp in self.copies(u, True)[0]:
                cp.start()

        @pl.when(k > 0)
        def _():
            for cp in self.copies(u)[0]:
                cp.start()

    def across(self, u):
        net, t = self.net, lax.div(u, 4)
        zz = self.nth(lax.rem(u, 4))
        a, b, d = self.copies(u)[1]
        self.arrived(t, net.f, 1 - net.n, net.c, zz)
        a.start()
        b.start()
        self.arrived(t, 1 - net.f, net.n, net.c, zz)
        d.start()

    def corner(self, u):
        net, t = self.net, lax.div(u, 4)
        self.arrived(t, 1 - net.f, 1 - net.n, net.c, self.nth(lax.rem(u, 4)))
        self.copies(u)[2][0].start()

    def do(self, *steps):
        for name, u in steps:
            getattr(self, name)(jnp.int32(u))

    def at(self, point, table):
        for p, steps in enumerate(table):
            pl.when(point == p)(lambda: self.do(*steps))

    def from_mate(self, t):
        def one(i, _):
            self.arrived(t, lax.div(i, 8), lax.rem(lax.div(i, 4), 2), 1 - self.net.c, lax.rem(i, 4))
            return 0

        lax.fori_loop(0, 16, one, 0)

    def finish(self):
        def one(u, _):
            for group in self.copies(u):
                for cp in group:
                    cp.wait_send()
            t, k = lax.div(u, 4), lax.rem(u, 4)
            self.onward(t, k, self.nth(k), lambda cp: cp.wait_send())
            return 0

        lax.fori_loop(0, 12, one, 0)


def rows_out(net, i):
    dc, dz = lax.div(net.z, 2), 2 * net.c + i
    here = jnp.logical_and(dc == net.c, dz == net.z)
    return (net.y, net.x, dc, dz), pl.multiple_of(lax.rem(net.z, 2) * 256, 256), here


class Rows:
    def __init__(self, net, src, dst, send, recv):
        self.net, self.src, self.dst, self.send, self.recv = net, src, dst, send, recv

    def each(self, start):
        for i in range(2):
            device, row, here = rows_out(self.net, i)
            rows = self.dst.at[pl.ds(row, 256)]
            sem = self.recv.at[lax.rem(self.net.z, 2)]

            @pl.when(jnp.logical_not(here))
            def _():
                cp = remote(self.src.at[i], rows, self.send.at[i], sem, device)
                cp.start() if start else cp.wait_send()

            if start:

                @pl.when(here)
                def _():
                    rows[...] = self.src[i]

    def arrivals(self):
        net = self.net
        for k in range(2):
            here = jnp.logical_and(lax.div(net.z, 2) == net.c, 2 * net.c + k == net.z)
            pl.when(jnp.logical_not(here))(lambda: landed(self.dst.at[pl.ds(k * 256, 256)], self.recv.at[k]))


def normalize(v):
    mean = jnp.mean(v, axis=-1, keepdims=True)
    centred = v - mean
    r = lax.rsqrt(jnp.mean(centred * centred, axis=-1, keepdims=True) + epsilon)
    return centred * r, r


def by_rows(step, body):
    def one(i, _):
        body(pl.ds(pl.multiple_of(i * step, step), step))
        return 0

    lax.fori_loop(0, TOK // step, one, 0)


TABLE = (
    (("line", 7), ("line", 8), ("spread", 7), ("spread", 8), ("across", 6)),
    (("corner", 5),),
    (("line", 9), ("corner", 6)),
    (("across", 7), ("line", 10), ("spread", 9)),
    (("line", 11), ("across", 8), ("corner", 7)),
    (("spread", 10),),
    (("spread", 11), ("corner", 8)),
    (("across", 9),),
    (("across", 10), ("corner", 9)),
    (("across", 11), ("corner", 10)),
    (("corner", 11),),
)


def forward_kernel(
    shard, tokens, cotangent, lift_own, ada, ada_bias, z_bias, out_bias,
    g, tok, cot, lift_rows, vectors, biases, x_out, qkv_out, kvo_out, att_out, lse, peak, branch_out, nm_out, act_out, gd_out, d2,
    tok_v, cot_v, lift, part, part_in, four, four_in, zall, x_ref, w, qkv, kvo, att, branch, qh, kh, vh, oh, gbt, act_buf, gd_buf, dbuf,
    gsend, gzsend, grecv, lsem, rsend, rrecv, small_send, small_recv, wsem, ksend, krecv, osem, asem, gdsem, dsem,
):
    net = Net()
    y, x, c, z = net.y, net.x, net.c, net.z
    plane = 2 * y + x
    net.greet()
    flow = Gather(net, g, shard, gsend, gzsend, grecv)
    lift[plane, c] = lift_own[...]
    small = [remote(lift.at[plane, c], lift.at[plane, c], small_send.at[0], small_recv.at[0], net.cn)]
    small[0].start()
    token_rows = Rows(net, tokens, tok_v, rsend.at[0], rrecv.at[0])
    cot_rows = Rows(net, cotangent, cot_v, rsend.at[1], rrecv.at[1])
    flow.do(("line", 0))
    own = [pltpu.make_async_copy(shard.at[t], flow.slot(t, net.f, net.n, c, z), lsem.at[t]) for t in range(3)]
    for cp in own:
        cp.start()

    landed(lift.at[plane, 1 - c], small_recv.at[0])
    peers = ((net.xn, 2 * y + 1 - x), (net.yn, 2 - 2 * y + x), (net.dn, 3 - plane))
    for k, (dev, _) in enumerate(peers):
        cp = remote(lift.at[plane], lift.at[plane], small_send.at[1 + k], small_recv.at[1 + k], dev)
        cp.start()
        small.append(cp)
    flow.do(("spread", 0), ("spread", 4), ("line", 1))
    for k, (_, p) in enumerate(peers):
        landed(lift.at[p], small_recv.at[1 + k])
    every = jnp.concatenate([lift[p, k, 0:2] for p in range(4) for k in range(2)], axis=0).astype(bf)
    batch = 4 * y + 2 * x + c
    pick = lax.broadcasted_iota(jnp.int32, (COLS, ROWS), 0) == lax.broadcasted_iota(jnp.int32, (COLS, ROWS), 1) + batch * ROWS
    rows = dg(every, jnp.where(pick, 1.0, 0.0).astype(bf), 1, 0)
    lift_rows[...] = rows
    partial = dg(rows.astype(bf), ada[...], 1, 0)
    part[...] = jnp.zeros_like(part)
    for p in range(4):
        part[p, 0:4] = partial[4 * p : 4 * p + 4]
    for k, (dev, p) in enumerate(peers):
        cp = remote(part.at[p], part_in.at[k], small_send.at[4 + k], small_recv.at[4 + k], dev)
        cp.start()
        small.append(cp)
    flow.do(("spread", 1), ("line", 2), ("across", 0))
    token_rows.each(True)
    flow.do(("spread", 2), ("line", 3))
    for k in range(3):
        landed(part_in.at[k], small_recv.at[4 + k])
    four[...] = part[plane] + part_in[0] + part_in[1] + part_in[2]
    cp = remote(four, four_in, small_send.at[7], small_recv.at[7], net.cn)
    cp.start()
    small.append(cp)
    flow.do(("across", 4), ("line", 4), ("spread", 3), ("across", 1), ("corner", 0))
    landed(four_in, small_recv.at[7])
    zall[z] = four[...] + four_in[...] + ada_bias[...]
    zall[z, 4:5] = z_bias[...]
    for k in range(3):
        cp = remote(zall.at[z], zall.at[z], small_send.at[8 + k], small_recv.at[8 + k], net.along_z(k + 1))
        cp.start()
        small.append(cp)
    flow.do(("across", 2), ("corner", 4))
    for k in range(3):
        landed(zall.at[lax.rem(z + 3 - k, 4)], small_recv.at[8 + k])
    pieces = [zall[k, pl.ds(z, 1)] for k in range(4)]
    half = COLS // 2
    vectors[0:1] = pieces[0][:, :COLS]
    vectors[1:2] = jnp.concatenate([pieces[0][:, COLS:], pieces[1][:, :half]], axis=1)
    vectors[2:3] = pieces[1][:, half:]
    vectors[3:4] = pieces[2][:, :COLS]
    vectors[4:5] = jnp.concatenate([pieces[2][:, COLS:], pieces[3][:, :half]], axis=1)
    vectors[5:6] = pieces[3][:, half:]
    vectors[6:8] = jnp.zeros((2, COLS), f32)
    nothing = jnp.zeros((1, HS), f32)
    for k in range(4):
        b = zall[k, 4:5]
        biases[k, 0:1] = jnp.concatenate([b[:, :HS], nothing, b[:, HS : 2 * HS], nothing], axis=1)
        biases[k, 1:2] = b[:, 2 * HS :]

    flow.do(("across", 3), ("corner", 1), ("line", 5), ("spread", 5), ("corner", 2))
    token_rows.arrivals()

    def first_norm(r):
        n, _ = normalize(tok_v[r].astype(f32))
        x_ref[r] = (n * (1.0 + vectors[1:2]) + vectors[0:1]).astype(bf)

    by_rows(64, first_norm)
    outs = [pltpu.make_async_copy(x_ref, x_out, osem.at[1]), pltpu.make_async_copy(tok_v, tok, osem.at[0])]
    for cp in outs:
        cp.start()
    flow.do(("corner", 3), ("line", 6), ("spread", 6), ("across", 5))
    flow.from_mate(0)

    def load_w(t, k):
        return pltpu.make_async_copy(g.at[t, :, pl.ds(k * COLS, COLS)], w.at[k], wsem.at[k])

    own[0].wait()
    for k in range(4):
        load_w(0, k).start()

    def kv(k):
        return remote(qkv.at[k, :, pl.ds(KV0, KVW)], kvo.at[k], ksend.at[k], krecv.at[k], net.cn)

    for k in range(4):
        load_w(0, k).wait()
        qkv[k] = (dg(x_ref[...], w[k], 1, 0) + biases[k, 0:1]).astype(bf)
        kv(k).start()
    cp = pltpu.make_async_copy(qkv, qkv_out, osem.at[2])
    cp.start()
    outs.append(cp)
    branch[...] = jnp.broadcast_to(out_bias[...], (TOK, COLS))


    def chunk(k, _):
        flow.at(2 * k, TABLE)
        pl.when(k == 2)(lambda: cot_rows.each(True))
        kv(k).wait_recv()
        for j in range(4):
            a = j * HEAD_DIM
            qh[j] = qkv[k, :, a : a + HEAD_DIM]
            kh[j, :TOK] = qkv[k, :, HS + a : HS + a + HEAD_DIM]
            vh[j, :TOK] = qkv[k, :, 2 * HS + a : 2 * HS + a + HEAD_DIM]
            kh[j, TOK:] = kvo[k, :, HS - KV0 + a : HS - KV0 + a + HEAD_DIM]
            vh[j, TOK:] = kvo[k, :, 2 * HS - KV0 + a : 2 * HS - KV0 + a + HEAD_DIM]

        def head(j, _):
            h = k * 4 + j
            s = dg(kh[j], qh[j], 1, 1)
            m = jnp.max(s, axis=0, keepdims=True)
            p = jnp.exp2((s - m) * (C * LOG2E))
            l = jnp.sum(p, axis=0, keepdims=True)
            o = dg(vh[j], p.astype(bf), 0, 0) / l
            oh[j] = o.T.astype(bf)
            lse[h] = m * (C * LOG2E) + jnp.log2(l)
            peak[h] = jnp.broadcast_to(jnp.max(m, axis=1, keepdims=True) * C, (1, 128))
            pl.when(j == 1)(lambda: flow.at(2 * k + 1, TABLE))
            return 0

        lax.fori_loop(0, 4, head, 0)
        att[k] = jnp.concatenate([jnp.zeros((TOK, ATW - HS), bf)] + [oh[j] for j in range(4)], axis=1)
        branch[...] += dg(att[k], w[k, :, AT0:], 1, 1)
        return 0

    lax.fori_loop(0, 4, chunk, 0)
    for src, dst, k in ((kvo, kvo_out, 3), (att, att_out, 4), (branch, branch_out, 5)):
        cp = pltpu.make_async_copy(src, dst, osem.at[k])
        cp.start()
        outs.append(cp)
    outs[0].wait()

    def second_norm(r):
        after = tok_v[r].astype(f32) + vectors[2:3] * branch[r]
        n, _ = normalize(after)
        x_ref[r] = (n * (1.0 + vectors[4:5]) + vectors[3:4]).astype(bf)

    by_rows(64, second_norm)
    cp = pltpu.make_async_copy(x_ref, nm_out, osem.at[6])
    cp.start()
    outs[0] = cp
    flow.from_mate(1)
    own[1].wait()
    for k in range(4):
        load_w(1, k).start()

    def slope_store(k):
        i = lax.rem(k, 2)
        return pltpu.make_async_copy(gd_buf.at[i], gd_out.at[k], gdsem.at[i])

    def hidden(k, _):
        i = lax.rem(k, 2)
        pltpu.make_async_copy(g.at[1, :, pl.ds(pl.multiple_of(k * COLS, 128), COLS)], w.at[k], wsem.at[k]).wait()
        pl.when(k >= 2)(lambda: slope_store(k - 2).wait())
        gd_buf[i] = dg(x_ref[...], w[k], 1, 0)

        def activate(r):
            a, d = gelu_pair(gd_buf[i, r] + biases[k, 1:2])
            act_buf[k, r] = a.astype(bf)
            gd_buf[i, r] = d

        by_rows(64, activate)
        slope_store(k).start()
        pltpu.make_async_copy(act_buf.at[k], act_out.at[k], asem.at[k]).start()
        flow.at(8 + k, TABLE)
        return 0

    lax.fori_loop(0, 4, hidden, 0)
    cot_rows.arrivals()
    cp = pltpu.make_async_copy(cot_v, cot, osem.at[1])
    cp.start()
    outs.append(cp)

    def gated(r):
        x_ref[r] = (vectors[5:6] * cot_v[r].astype(f32)).astype(bf)

    outs[0].wait()
    by_rows(64, gated)
    gbt[...] = x_ref[...].T

    def down_store(k):
        i = lax.rem(k, 2)
        return pltpu.make_async_copy(dbuf.at[i], d2.at[:, pl.ds(pl.multiple_of(k * COLS, 128), COLS)], dsem.at[i])

    def down(k, _):
        i = lax.rem(k, 2)
        pl.when(k >= 2)(lambda: down_store(k - 2).wait())
        dbuf[i] = dg(gbt[...], act_buf[k], 1, 0).astype(bf)
        down_store(k).start()
        return 0

    lax.fori_loop(0, 4, down, 0)
    for k in (2, 3):
        slope_store(k).wait()
        down_store(k).wait()
    for k in range(4):
        pltpu.make_async_copy(act_buf.at[k], act_out.at[k], asem.at[k]).wait()
    flow.from_mate(2)
    flow.finish()
    for cp in outs[1:]:
        cp.wait()
    for k in range(4):
        kv(k).wait_send()
    for cp in small:
        cp.wait_send()
    own[2].wait()
    token_rows.each(False)
    cot_rows.each(False)


def forward(shard, tokens, cotangent, lift_own, ada, ada_bias, z_bias, out_bias):
    rows = S((TOK, COLS), bf)
    wide = S((TOK, COLS), f32)
    return pl.pallas_call(
        forward_kernel,
        name="forward",
        out_shape=(
            S((3, 8 * ROWS, 4 * COLS), bf), rows, rows, S((16, ROWS), f32), S((8, COLS), f32), S((4, 2, COLS), f32),
            rows, S((4, TOK, COLS), bf), S((4, TOK, KVW), bf), S((4, TOK, ATW), bf), S((16, 1, TOK), f32),
            S((16, 1, 128), f32), wide, rows, S((4, TOK, COLS), bf), S((4, TOK, COLS), f32), S((8 * ROWS, 4 * COLS), bf),
        ),
        in_specs=[VM] * 8,
        out_specs=(HB, HB, HB, VM, VM, VM, HB, HB, HB, HB, VM, VM, HB, HB, HB, HB, HB),
        scratch_shapes=[
            V((TOK, COLS), bf), V((TOK, COLS), bf), V((4, 2, 8, COLS), f32), V((4, 8, ADA), f32), V((3, 8, ADA), f32),
            V((8, ADA), f32), V((8, ADA), f32), V((4, 8, ADA), f32), V((TOK, COLS), bf), V((4, COLS, COLS), bf),
            V((4, TOK, COLS), bf), V((4, TOK, KVW), bf), V((4, TOK, ATW), bf), V((TOK, COLS), f32),
            V((4, TOK, HEAD_DIM), bf), V((4, 2 * TOK, HEAD_DIM), bf), V((4, 2 * TOK, HEAD_DIM), bf), V((4, TOK, HEAD_DIM), bf),
            V((COLS, TOK), bf), V((4, TOK, COLS), bf), V((2, TOK, COLS), f32), V((2, COLS, COLS), bf),
            D((12, 7)), D((3, 4, 2)), D((3, 8, 4)), D((3,)), D((2, 2)), D((2, 2)), D((11,)), D((11,)), D((4,)), D((4,)), D((4,)),
            D((7,)), D((4,)), D((2,)), D((2,)),
        ],
        compiler_params=pltpu.CompilerParams(collective_id=1, has_side_effects=True, vmem_limit_bytes=60 * 2**20),
    )(shard, tokens, cotangent, lift_own, ada, ada_bias, z_bias, out_bias)


LINE = (0, 3, 1, 2)
STEPS = (
    (("far", 0),),
    (("near", 0), ("fetch", 4), ("far", 1), ("core", 4)),
    (("near", 1), ("fetch", 5), ("far", 2), ("line0", 0), ("core", 5)),
    (("near", 2), ("fetch", 6), ("far", 3), ("line0", 1), ("line1", 0), ("core", 6)),
    (("near", 3), ("fetch", 7), ("far", 4), ("line0", 2), ("line1", 1), ("line2", 0), ("core", 7)),
    (("line0", 3), ("line1", 2), ("line2", 1), ("last", 0)),
    (("far", 5), ("near", 4), ("line1", 3)),
    (("line0", 4), ("line2", 2), ("last", 1)),
    (("far", 6), ("near", 5), ("line1", 4)),
    (("line0", 5), ("line2", 3), ("last", 2)),
    (("far", 7), ("near", 6), ("line1", 5)),
    (("line0", 6), ("line2", 4), ("last", 3), ("begin", 8)),
    (("fetch", 8), ("near", 7), ("line1", 6), ("core", 8)),
    (("line0", 7), ("line2", 5), ("last", 4)),
    (("line1", 7), ("far", 8)),
    (("line2", 6), ("last", 5), ("begin", 9)),
    (("fetch", 9), ("near", 8), ("line2", 7), ("core", 9)),
    (("line0", 8), ("last", 6)),
    (("far", 9), ("line1", 8)),
    (("last", 7), ("line2", 8), ("begin", 10)),
    (("fetch", 10), ("near", 9), ("core", 10)),
)


class Scatter:
    def __init__(self, net, source, out, stage, out_sem, rc, far_in, near_in, line_in, side_in, acc, ctmp, ftmp,
                 csend, crecv, own_sem, ctmp_sem, fsend, frecv, ftmp_sem, nsend, nrecv, lsend, lrecv, srecv):
        self.__dict__.update(locals())

    def block(self, v, yy, xx, c):
        row = pl.multiple_of((4 * yy + 2 * xx + c) * ROWS, 16)
        return self.source(v).at[pl.ds(row, ROWS), pl.ds(LINE[v % 4] * COLS, COLS)]

    def places(self):
        return [(yy, xx) for yy in range(2) for xx in range(2)]

    def to_mate(self, v, yy, xx):
        return remote(
            self.block(v, yy, xx, 1 - self.net.c), self.rc.at[v, yy, xx],
            self.csend.at[v, yy, xx], self.crecv.at[v, yy, xx], self.net.cn,
        )

    def begin(self, v):
        for yy, xx in self.places():
            self.to_mate(v, yy, xx).start()

    def to_far(self, v, n):
        yy, xx = self.net.place(1 - self.net.f, n)
        return remote(self.acc.at[v % 4, yy, xx], self.far_in.at[v, n], self.fsend.at[v, n], self.frecv.at[v, n], self.net.far)

    def to_near(self, v):
        yy, xx = self.net.place(self.net.f, 1 - self.net.n)
        return remote(self.acc.at[v % 4, yy, xx], self.near_in.at[v], self.nsend.at[v], self.nrecv.at[v], self.net.near)

    def own_loads(self, v):
        return [
            pltpu.make_async_copy(self.block(v, yy, xx, self.net.c), self.acc.at[v % 4, yy, xx], self.own_sem.at[yy, xx])
            for yy, xx in self.places()
        ]

    def mate_loads(self, v, f):
        for n in range(2):
            yy, xx = self.net.place(f, n)
            yield pltpu.make_async_copy(self.rc.at[v, yy, xx], self.ctmp.at[n], self.ctmp_sem.at[n])

    def add(self, a, b):
        def one(i, _):
            r = pl.ds(pl.multiple_of(i * 16, 16), 16)
            a[r] = (a[r].astype(f32) + b[r].astype(f32)).astype(bf)
            return 0

        lax.fori_loop(0, ROWS // 16, one, 0)

    def fetch(self, v):
        if v >= 4:
            for n in range(2):
                self.to_far(v - 4, n).wait_send()
            self.to_near(v - 4).wait_send()
        for cp in self.own_loads(v):
            cp.start()
        for yy, xx in self.places():
            landed(self.rc.at[v, yy, xx], self.crecv.at[v, yy, xx])
        for cp in self.mate_loads(v, 1 - self.net.f):
            cp.start()

    def core(self, v):
        for cp in self.own_loads(v):
            cp.wait()
        for f in (1 - self.net.f, self.net.f):
            for n, cp in enumerate(self.mate_loads(v, f)):
                cp.wait()
                yy, xx = self.net.place(f, n)
                self.add(self.acc.at[v % 4, yy, xx], self.ctmp.at[n])
                if f is not self.net.f:
                    self.to_far(v, n).start()
                    list(self.mate_loads(v, self.net.f))[n].start()

    def far(self, v):
        cps = [pltpu.make_async_copy(self.far_in.at[v, n], self.ftmp.at[n], self.ftmp_sem.at[n]) for n in range(2)]
        for n in range(2):
            landed(self.far_in.at[v, n], self.frecv.at[v, n])
            cps[n].start()
        for cp in cps:
            cp.wait()
        for n in (1 - self.net.n, self.net.n):
            yy, xx = self.net.place(self.net.f, n)
            self.add(self.acc.at[v % 4, yy, xx], self.ftmp.at[n])
            if n is not self.net.n:
                self.to_near(v).start()

    def near(self, v):
        landed(self.near_in.at[v], self.nrecv.at[v])
        self.add(self.near_in.at[v], self.acc.at[v % 4, self.net.y, self.net.x])

    def hop(self, v, h, act):
        net, zz = self.net, LINE[v % 4]
        if h < zz:

            @pl.when(net.z == h)
            def _():
                act(v, h, remote(self.near_in.at[v], self.line_in.at[v], self.lsend.at[v], self.lrecv.at[v], net.zpn))

        if 3 - h > zz:

            @pl.when(net.z == 3 - h)
            def _():
                side = 3 - h - 1 == zz
                dst = self.side_in.at[v // 4] if side else self.line_in.at[v]
                sem = self.srecv.at[v // 4] if side else self.lrecv.at[v]
                act(v, h, remote(self.near_in.at[v], dst, self.lsend.at[v], sem, net.zmn))

    def pass_on(self, v, h, cp):
        if h:
            landed(self.line_in.at[v], self.lrecv.at[v])
            self.add(self.near_in.at[v], self.line_in.at[v])
        cp.start()

    def line0(self, v):
        self.hop(v, 0, self.pass_on)

    def line1(self, v):
        self.hop(v, 1, self.pass_on)

    def line2(self, v):
        self.hop(v, 2, self.pass_on)

    def last(self, v):
        t, zz = 2 - v // 4, LINE[v % 4]

        @pl.when(self.net.z == zz)
        def _():
            if zz > 0:
                landed(self.line_in.at[v], self.lrecv.at[v])
            if zz < 3:
                landed(self.side_in.at[v // 4], self.srecv.at[v // 4])

            def one(i, _):
                r = pl.ds(pl.multiple_of(i * 16, 16), 16)
                total = self.near_in[v, r].astype(f32)
                if zz > 0:
                    total = total + self.line_in[v, r].astype(f32)
                if zz < 3:
                    total = total + self.side_in[v // 4, r].astype(f32)
                self.stage[r] = total
                return 0

            lax.fori_loop(0, ROWS // 16, one, 0)
            cp = pltpu.make_async_copy(self.stage, self.out.at[t], self.out_sem)
            cp.start()
            cp.wait()

    def do(self, *steps):
        for name, v in steps:
            getattr(self, name)(v)

    def at(self, point, table, base=0):
        for p, steps in enumerate(table):
            if steps:
                pl.when(point == base + p)(lambda: self.do(*steps))

    def finish(self):
        for v in range(12):
            for yy, xx in self.places():
                self.to_mate(v, yy, xx).wait_send()
            if v >= 8:
                for n in range(2):
                    self.to_far(v, n).wait_send()
                self.to_near(v).wait_send()
            for h in range(3):
                self.hop(v, h, lambda v, h, cp: cp.wait_send())


class Back:
    def __init__(self, net, src, dst, send, recv):
        self.net, self.src, self.dst, self.send, self.recv = net, src, dst, send, recv

    def each(self, start):
        net = self.net
        for k in range(2):
            dc, dz = lax.div(net.z, 2), 2 * net.c + k
            here = jnp.logical_and(dc == net.c, dz == net.z)
            rows, image = self.src.at[pl.ds(k * 256, 256)], self.dst.at[lax.rem(net.z, 2)]
            sem = self.recv.at[lax.rem(net.z, 2)]

            @pl.when(jnp.logical_not(here))
            def _():
                cp = remote(rows, image, self.send.at[k], sem, (net.y, net.x, dc, dz))
                cp.start() if start else cp.wait_send()

            if start:

                @pl.when(here)
                def _():
                    pltpu.make_async_copy(rows, image, sem).start()

    def arrivals(self):
        for i in range(2):
            landed(self.dst.at[i], self.recv.at[i])


def column_sum(v):
    return jnp.sum(v.astype(f32), axis=0, keepdims=True)


def backward_kernel(
    g, tok_in, cot_in, x_in, nm_in, qkv_in, kvo_in, att_in, lse, peak, branch_in, act_in, gd_in, d2, vectors, lift_rows, ada, down_bias,
    sums, block_rows, token_rows, d, rc, far_in, ada_grad, ada_bias_grad, lifted, totals,
    tok, cot, branch, gn, br, gb, gub, xt, gt, w1, act, dbuf, near_in, line_in, side_in, acc, ctmp, ftmp, mate_in,
    stage, bias, bias_in, terms, terms_in, image, pgl, pgl_in, four,
    out_sem, csend, crecv, own_sem, ctmp_sem, fsend, frecv, ftmp_sem, nsend, nrecv, lsend, lrecv, srecv,
    bsend, brecv, isem, w1_sem, w2_sem, act_sem, gd_sem, dsem, msend, mrecv, kvsem, small_send, small_recv,
):
    net = Net()
    y, x, c, z = net.y, net.x, net.c, net.z
    plane = 2 * y + x

    def fetch(src, dst, k):
        cp = pltpu.make_async_copy(src, dst, isem.at[k])
        cp.start()
        return cp

    first = [fetch(cot_in, cot, 0), fetch(nm_in, gub, 1), fetch(tok_in, tok, 2), fetch(branch_in, branch, 3)]

    def cols(ref, k):
        return ref.at[:, pl.ds(pl.multiple_of(zs(k) * COLS, 128), COLS)]

    def zs(k):
        return jnp.where(k == 0, 0, jnp.where(k == 1, 3, k - 1))

    def load_first(t, k):
        return pltpu.make_async_copy(cols(g.at[t], k), w1.at[lax.rem(k, 2)], w1_sem.at[lax.rem(k, 2)])

    def d_store(t, k):
        return pltpu.make_async_copy(dbuf, cols(d.at[t], k), dsem)

    load_first(1, jnp.int32(0)).start()
    net.greet()
    flow = Scatter(
        net, lambda v: d2 if v < 4 else d.at[2 - v // 4], sums, stage, out_sem, rc, far_in, near_in, line_in, side_in, acc, ctmp, ftmp,
        csend, crecv, own_sem, ctmp_sem, fsend, frecv, ftmp_sem, nsend, nrecv, lsend, lrecv, srecv,
    )
    for v in range(4):
        flow.begin(v)
    shift_attn, scale_attn, gate_attn, shift_mlp, scale_mlp, gate_mlp = [vectors[i : i + 1] for i in range(6)]
    terms[...] = jnp.zeros_like(terms)
    bias[...] = jnp.zeros_like(bias)
    for h in range(16):
        bias[h : h + 1, COLS:] = peak[h]
    gn[...] = jnp.zeros_like(gn)
    br[...] = jnp.zeros_like(br)
    first[0].wait()

    def gated(r):
        gb[r] = (gate_mlp * cot[r].astype(f32)).astype(bf)

    by_rows(64, gated)
    first[1].wait()
    xt[...] = gub[...].T

    def mlp(w2, gd):
        def loads(k):
            i = lax.rem(k, 2)
            return (
                load_first(1, k),
                pltpu.make_async_copy(cols(g.at[2], k), w2.at[i], w2_sem.at[i]),
                pltpu.make_async_copy(act_in.at[zs(k)], act.at[i], act_sem.at[i]),
                pltpu.make_async_copy(gd_in.at[zs(k)], gd.at[i], gd_sem.at[i]),
            )

        for cp in loads(jnp.int32(0))[1:]:
            cp.start()
        flow.do(("fetch", 0), ("core", 0), ("fetch", 1), ("core", 1))

        def hidden(k, _):
            i = lax.rem(k, 2)
            for cp in loads(k):
                cp.wait()

            @pl.when(k < 3)
            def _():
                for cp in loads(k + 1):
                    cp.start()

            gub[...] = (dg(gb[...], w2[i], 1, 0) * gd[i]).astype(bf)
            bias[pl.ds(4 + zs(k), 1), :COLS] = column_sum(gub[...])
            br[...] += dg(act[i], w2[i], 1, 1)
            pl.when(k == 0)(lambda: flow.do(("fetch", 2), ("core", 2), ("fetch", 3), ("core", 3)))

            @pl.when(k > 0)
            def _():
                d_store(1, k - 1).wait()
                flow.at(k - 1, [(("begin", 4 + q),) for q in range(3)])

            dbuf[...] = dg(xt[...], gub[...], 1, 0).astype(bf)
            d_store(1, k).start()
            gn[...] += dg(gub[...], w1[i], 1, 1)
            flow.at(k, STEPS)
            return 0

        lax.fori_loop(0, 4, hidden, 0)

    pl.run_scoped(mlp, V((2, COLS, COLS), bf), V((2, TOK, COLS), f32))
    load_first(0, jnp.int32(0)).start()
    d_store(1, jnp.int32(3)).wait()
    flow.begin(7)
    first[2].wait()
    first[3].wait()

    def second_norm(r):
        after = tok[r].astype(f32) + gate_attn * branch[r]
        n, s = normalize(after)
        mlp_out = br[r] + down_bias[...]
        gub[r] = (after + gate_mlp * mlp_out).astype(bf)
        go = cot[r].astype(f32)
        terms[5:6] += column_sum(go * mlp_out)
        gr = gn[r]
        terms[3:4] += column_sum(gr)
        terms[4:5] += column_sum(gr * n)
        e = gr * (1.0 + scale_mlp)
        ga = go + s * (e - jnp.mean(e, axis=-1, keepdims=True) - n * jnp.mean(e * n, axis=-1, keepdims=True))
        br[r] = ga
        terms[2:3] += column_sum(ga * branch[r])
        bias[9:10, :COLS] += column_sum(gb[r])
        low = (gate_attn * ga).astype(bf)
        bias[8:9, :COLS] += column_sum(low)
        gb[r] = low

    by_rows(64, second_norm)
    block_back = Back(net, gub, block_rows, bsend.at[0], brecv.at[0])
    block_back.each(True)
    load = fetch(x_in, cot, 0)
    gt[...] = gb[...].T
    flow.at(4, STEPS)
    gn[...] = jnp.zeros_like(gn)
    load.wait()
    xt[...] = cot[...].T

    def attention(kvo, att, qh, kh, vh, gh, dqh, dkh, dvh, dkm, dvm, mate_out):
        pack = cot

        def loads(k):
            i = lax.rem(k, 2)
            return (
                load_first(0, k),
                pltpu.make_async_copy(qkv_in.at[zs(k)], act.at[i], act_sem.at[i]),
                pltpu.make_async_copy(kvo_in.at[zs(k)], kvo.at[i], kvsem.at[0, i]),
                pltpu.make_async_copy(att_in.at[zs(k)], att.at[i], kvsem.at[1, i]),
            )

        for cp in loads(jnp.int32(0))[1:]:
            cp.start()

        def to_mate(k):
            return remote(mate_out, mate_in.at[lax.rem(k, 2)], msend, mrecv.at[k], net.cn)

        def complete(k):
            i = lax.rem(k, 2)
            to_mate(k).wait_send()
            landed(mate_in.at[i], mrecv.at[k])
            both = (branch[:, : 2 * HS] + mate_in[i, :, : 2 * HS].astype(f32)).astype(bf)
            pack[:, HS:] = jnp.concatenate([both, jnp.zeros((TOK, HS), bf)], axis=1)
            bias[pl.ds(zs(k), 1), :COLS] = column_sum(pack[...])
            gn[...] += dg(pack[...], w1[i], 1, 1)
            d1 = dg(xt[...], pack[:, :896], 1, 0)
            d2_ = dg(gt[...], att[i], 1, 0)
            dbuf[:, :AT0] = d1[:, :AT0].astype(bf)
            dbuf[:, AT0:896] = (d1[:, AT0:] + d2_[:, :128]).astype(bf)
            dbuf[:, 896:] = d2_[:, 128:].astype(bf)
            d_store(0, k).start()

        def chunk(k, _):
            i = lax.rem(k, 2)
            for cp in loads(k):
                cp.wait()
            ga = dg(gb[...], w1[i, :, AT0:], 1, 0).astype(bf)
            for j in range(4):
                a = j * HEAD_DIM
                gh[j] = ga[:, ATW - HS + a : ATW - HS + a + HEAD_DIM]
                qh[j] = act[i, :, a : a + HEAD_DIM]
                kh[j, :TOK] = act[i, :, HS + a : HS + a + HEAD_DIM]
                vh[j, :TOK] = act[i, :, 2 * HS + a : 2 * HS + a + HEAD_DIM]
                kh[j, TOK:] = kvo[i, :, HS - KV0 + a : HS - KV0 + a + HEAD_DIM]
                vh[j, TOK:] = kvo[i, :, 2 * HS - KV0 + a : 2 * HS - KV0 + a + HEAD_DIM]

            def head(j, _):
                kk, q, gg = kh[j], qh[j], gh[j]
                p = jnp.exp2(dg(kk, q, 1, 1) * (C * LOG2E) - lse[zs(k) * 4 + j])
                t = p * dg(vh[j], gg, 1, 1)
                inner = jnp.sum(t, axis=0, keepdims=True)
                ds = (t - p * inner).astype(bf)
                dv = dg(p.astype(bf), gg, 1, 0)
                dvh[j], dvm[j] = dv[:TOK], dv[TOK:].astype(bf)
                dk = dg(ds, q, 1, 0) * C
                dkh[j], dkm[j] = dk[:TOK], dk[TOK:].astype(bf)
                dqh[j] = (dg(kk, ds, 0, 0) * C).T.astype(bf)
                pl.when(jnp.logical_and(j == 1, k > 0))(lambda: complete(k - 1))

                @pl.when(jnp.logical_and(j == 1, k < 3))
                def _():
                    for cp in loads(k + 1):
                        cp.start()

                pl.when(jnp.logical_and(j == 2, k > 0))(lambda: d_store(0, k - 1).wait())
                flow.at(5 + 4 * k + j, STEPS[5:], 5)
                return 0

            lax.fori_loop(0, 4, head, 0)
            mate_out[...] = jnp.concatenate(
                [dkm[j] for j in range(4)] + [dvm[j] for j in range(4)] + [jnp.zeros((TOK, KVW - 2 * HS), bf)], axis=1,
            )
            to_mate(k).start()
            branch[:, : 2 * HS] = jnp.concatenate([dkh[j] for j in range(4)] + [dvh[j] for j in range(4)], axis=1)
            pack[:, :HS] = jnp.concatenate([dqh[j] for j in range(4)], axis=1)
            return 0

        lax.fori_loop(0, 4, chunk, 0)
        flow.do(("far", 10), ("line0", 9))
        complete(jnp.int32(3))

    T = (4, TOK, HEAD_DIM)
    T2 = (4, 2 * TOK, HEAD_DIM)
    pl.run_scoped(
        attention, V((2, TOK, KVW), bf), V((2, TOK, ATW), bf), V(T, bf), V(T2, bf), V(T2, bf), V(T, bf), V(T, bf), V(T, f32), V(T, f32),
        V(T, bf), V(T, bf), V((TOK, KVW), bf),
    )

    def first_norm(r):
        n, s = normalize(tok[r].astype(f32))
        gr = gn[r]
        terms[0:1] += column_sum(gr)
        terms[1:2] += column_sum(gr * n)
        e = gr * (1.0 + scale_attn)
        gr = s * (e - jnp.mean(e, axis=-1, keepdims=True) - n * jnp.mean(e * n, axis=-1, keepdims=True))
        tok[r] = (br[r] + gr).astype(bf)

    by_rows(64, first_norm)
    d_store(0, jnp.int32(3)).wait()
    flow.begin(11)
    token_back = Back(net, tok, token_rows, bsend.at[1], brecv.at[1])

    small = []

    def exchange(k, src, dst, dev):
        cp = remote(src, dst, small_send.at[k], small_recv.at[k], dev)
        cp.start()
        small.append(cp)

    def combine(k):
        bias[:, :COLS] += bias_in[k, :, :COLS]
        bias[:, COLS:] = jnp.maximum(bias[:, COLS:], bias_in[k, :, COLS:])

    peers = ((net.xn, 2 * y + 1 - x), (net.yn, 2 - 2 * y + x), (net.dn, 3 - plane))
    exchange(0, terms, terms_in, net.cn)
    four[0] = bias[...]
    exchange(1, four.at[0], bias_in.at[0], net.cn)
    token_back.each(True)
    landed(terms_in, small_recv.at[0])
    image[plane, z] = (terms[...] + terms_in[...]).astype(bf).astype(f32)
    for k in range(3):
        exchange(2 + k, image.at[plane, z], image.at[plane, z], net.along_z(k + 1))
    landed(bias_in.at[0], small_recv.at[1])
    combine(0)
    four[1] = bias[...]
    for k in range(3):
        exchange(5 + k, four.at[1], bias_in.at[1 + k], net.along_z(k + 1))
    flow.do(("fetch", 11), ("near", 10), ("line1", 9), ("core", 11))
    for k in range(3):
        landed(image.at[plane, lax.rem(z + 3 - k, 4)], small_recv.at[2 + k])
    for k, (dev, _) in enumerate(peers):
        exchange(8 + k, image.at[plane], image.at[plane], dev)
    for k in range(3):
        landed(bias_in.at[1 + k], small_recv.at[5 + k])
        combine(1 + k)
    four[2] = bias[...]
    for k, (dev, _) in enumerate(peers):
        exchange(11 + k, four.at[2], bias_in.at[4 + k], dev)
    flow.do(("line0", 10), ("line2", 9), ("last", 8))
    for k, (_, p) in enumerate(peers):
        landed(image.at[p], small_recv.at[8 + k])
    every = [jnp.concatenate([image[p, q, i : i + 1] for p in range(4) for q in range(4)], axis=0) for i in range(6)]
    half = COLS // 2
    options = (
        (every[0], every[1][:, :half]), (every[1][:, half:], every[2]),
        (every[3], every[4][:, :half]), (every[4][:, half:], every[5]),
    )
    grad = sum(jnp.where(z == k, jnp.concatenate(o, axis=1), 0.0) for k, o in enumerate(options))
    low = grad.astype(bf)
    pgl[0] = dg(low, ada[...], 1, 1)
    for k in range(3):
        exchange(14 + k, pgl.at[0], pgl_in.at[k], net.along_z(k + 1))
    ada_bias_grad[...] = column_sum(grad)
    ada_grad[...] = dg(lift_rows[...].astype(bf), low, 0, 0)
    flow.do(("far", 11), ("line1", 10), ("last", 9))
    for k in range(3):
        landed(pgl_in.at[k], small_recv.at[14 + k])
    lifted[plane, c] = pgl[0] + pgl_in[0] + pgl_in[1] + pgl_in[2]
    exchange(17, lifted.at[plane, c], lifted.at[plane, c], net.cn)
    for k in range(3):
        landed(bias_in.at[4 + k], small_recv.at[11 + k])
        combine(4 + k)
    totals[...] = bias[...]
    flow.do(("near", 11), ("line0", 11), ("line2", 10))
    landed(lifted.at[plane, 1 - c], small_recv.at[17])
    for k, (dev, _) in enumerate(peers):
        exchange(18 + k, lifted.at[plane], lifted.at[plane], dev)
    flow.do(("last", 10), ("line1", 11), ("line2", 11))
    for k, (_, p) in enumerate(peers):
        landed(lifted.at[p], small_recv.at[18 + k])
    flow.do(("last", 11))
    block_back.arrivals()
    token_back.arrivals()
    flow.finish()
    for cp in small:
        cp.wait_send()
    block_back.each(False)
    token_back.each(False)


def backward(*args):
    B = (ROWS, COLS)
    wide, rows = (TOK, COLS), (2, 256, COLS)
    pair = D((2,))
    return pl.pallas_call(
        backward_kernel,
        name="backward",
        out_shape=(
            S((3,) + B, f32), S(rows, bf), S(rows, bf), S((2, 8 * ROWS, 4 * COLS), bf), S((12, 2, 2) + B, bf), S((12, 2) + B, bf),
            S((ROWS, ADA), f32), S((1, ADA), f32), S((4, 2, 16, ROWS), f32), S((16, COLS + 128), f32),
        ),
        in_specs=[HB] * 8 + [VM, VM] + [HB] * 4 + [VM] * 4,
        out_specs=(HB,) * 6 + (VM,) * 4,
        scratch_shapes=[
            V(wide, bf), V(wide, bf), V(wide, f32), V(wide, f32), V(wide, f32), V(wide, bf), V(wide, bf), V((COLS, TOK), bf), V((COLS, TOK), bf),
            V((2, COLS, COLS), bf), V((2, TOK, COLS), bf), V((COLS, COLS), bf),
            V((12,) + B, bf), V((12,) + B, bf), V((3,) + B, bf), V((4, 2, 2) + B, bf), V((2,) + B, bf), V((2,) + B, bf), V((2, TOK, KVW), bf),
            V(B, f32), V((16, COLS + 128), f32), V((7, 16, COLS + 128), f32), V((8, COLS), f32), V((8, COLS), f32), V((4, 4, 8, COLS), f32),
            V((1, 16, ROWS), f32), V((3, 16, ROWS), f32), V((3, 16, COLS + 128), f32),
            D, D((12, 2, 2)), D((12, 2, 2)), D((2, 2)), pair, D((12, 2)), D((12, 2)), pair, D((12,)), D((12,)), D((12,)), D((12,)), D((3,)),
            D((2, 2)), D((2, 2)), D((4,)), pair, pair, pair, pair, D, D, D((4,)), D((2, 2)), D((21,)), D((21,)),
        ],
        compiler_params=pltpu.CompilerParams(collective_id=2, has_side_effects=True, vmem_limit_bytes=62 * 2**20),
    )(*args)


def modulate_images(values, shift, scale):
    average = jnp.mean(values, axis=-1, keepdims=True)
    centred = values - average
    spread = jnp.mean(centred * centred, axis=-1, keepdims=True)
    return centred * lax.rsqrt(spread + epsilon) * (1.0 + scale[:, None, :]) + shift[:, None, :]


def product(left, right):
    return jnp.dot(left, right, preferred_element_type=jnp.float32)


def inner_rows(left, right):
    return lax.dot_general(
        left, right, (((0,), (0,)), ((), ())), preferred_element_type=jnp.float32
    )


def against(left, right):
    return lax.dot_general(
        left, right, (((1,), (1,)), ((), ())), preferred_element_type=jnp.float32
    )


def spread_rows(values):
    return lax.all_gather(values, "tensor", axis=1, tiled=True)


def fold_rows(values):
    return lax.psum_scatter(values, "tensor", scatter_dimension=1, tiled=True)


def spread_grads(values):
    return lax.all_gather(values, "tensor", axis=1, tiled=True)


def fold_grads(values):
    return lax.psum_scatter(values, "tensor", scatter_dimension=1, tiled=True)


def local(
    tokens,
    conditioning,
    cotangent,
    query_weight,
    key_weight,
    value_weight,
    out_weight,
    up_weight,
    down_weight,
    ada_weight,
    query_bias,
    value_bias,
    out_bias,
    up_bias,
    down_bias,
    ada_bias,
    threshold,
):
    images = tokens.shape[0]
    model_width = tokens.shape[2]
    gathered = (
        lax.all_gather(query_weight, "dp", axis=0, tiled=True),
        lax.all_gather(key_weight, "dp", axis=0, tiled=True),
        lax.all_gather(value_weight, "dp", axis=0, tiled=True),
        lax.all_gather(out_weight, "dp", axis=1, tiled=True),
        lax.all_gather(up_weight, "dp", axis=0, tiled=True),
        lax.all_gather(down_weight, "dp", axis=1, tiled=True),
        lax.all_gather(ada_weight, "dp", axis=0, tiled=True),
    )
    full_query, full_key, full_value, full_out, full_up, full_down, full_ada = gathered
    lifted_low = jax.nn.silu(conditioning).astype(jnp.bfloat16)
    own_columns = product(lifted_low, full_ada) + ada_bias
    modulation = lax.all_gather(own_columns, "tensor", axis=1, tiled=True)
    pieces = [
        modulation[:, piece_index * model_width : (piece_index + 1) * model_width]
        for piece_index in range(6)
    ]
    shift_attn, scale_attn, gate_attn, shift_mlp, scale_mlp, gate_mlp = pieces
    inputs = tokens.astype(jnp.float32)
    normed_attn = spread_rows(modulate_images(inputs, shift_attn, scale_attn).astype(jnp.bfloat16))
    length = normed_attn.shape[1]
    row_count = images * length
    flat_attn = normed_attn.reshape(row_count, model_width)
    local_width = full_query.shape[1]
    heads_here = local_width // HEAD_DIM
    queries = (product(flat_attn, full_query) + query_bias).astype(jnp.bfloat16)
    key_rows = product(flat_attn, full_key).astype(jnp.bfloat16)
    value_rows = (product(flat_attn, full_value) + value_bias).astype(jnp.bfloat16)
    block_rows = min(512, length)
    head_scale = HEAD_DIM ** (-0.5)

    def by_head(matrix):
        return matrix.reshape(images, length, heads_here, HEAD_DIM)

    def attend_image(bundle):
        queries_img, keys_img, values_img = bundle
        outputs, totals, highest = ([], [], [])
        for offset in range(0, length, block_rows):
            logits = (
                jnp.einsum(
                    "qhe,khe->hqk",
                    queries_img[offset : offset + block_rows],
                    keys_img,
                    preferred_element_type=jnp.float32,
                )
                * head_scale
            )
            row_top = jnp.max(logits, axis=2, keepdims=True)
            raised = jnp.exp(logits - row_top)
            summed = jnp.sum(raised, axis=2, keepdims=True)
            shares = (raised / summed).astype(jnp.bfloat16)
            outputs.append(
                jnp.einsum(
                    "hqk,khe->qhe", shares, values_img, preferred_element_type=jnp.float32
                ).astype(jnp.bfloat16)
            )
            totals.append(row_top[:, :, 0] + jnp.log(summed[:, :, 0]))
            highest.append(jnp.max(row_top[:, :, 0], axis=1))
        return (
            jnp.concatenate(outputs, 0),
            jnp.concatenate(totals, 1),
            jnp.max(jnp.stack(highest), axis=0),
        )

    attended, log_totals, image_peaks = lax.map(
        attend_image, (by_head(queries), by_head(key_rows), by_head(value_rows))
    )
    flat_attended = attended.reshape(row_count, local_width)
    branch_attn = (
        fold_rows(product(flat_attended, full_out).reshape(images, length, model_width)) + out_bias
    )
    after_attn = inputs + gate_attn[:, None, :] * branch_attn
    normed_mlp = spread_rows(modulate_images(after_attn, shift_mlp, scale_mlp).astype(jnp.bfloat16))
    flat_mlp = normed_mlp.reshape(row_count, model_width)
    upward = product(flat_mlp, full_up) + up_bias
    active = jax.nn.gelu(upward, approximate=True).astype(jnp.bfloat16)
    branch_mlp = (
        fold_rows(product(active, full_down).reshape(images, length, model_width)) + down_bias
    )
    block_out = (after_attn + gate_mlp[:, None, :] * branch_mlp).astype(jnp.bfloat16)
    peaks = lax.pmax(jnp.max(image_peaks, axis=0), "dp")
    again = (
        lax.all_gather(query_weight, "dp", axis=0, tiled=True),
        lax.all_gather(key_weight, "dp", axis=0, tiled=True),
        lax.all_gather(value_weight, "dp", axis=0, tiled=True),
        lax.all_gather(out_weight, "dp", axis=1, tiled=True),
        lax.all_gather(up_weight, "dp", axis=0, tiled=True),
        lax.all_gather(down_weight, "dp", axis=1, tiled=True),
        lax.all_gather(ada_weight, "dp", axis=0, tiled=True),
    )
    back_query, back_key, back_value, back_out, back_up, back_down, back_ada = again
    grad_out = cotangent.astype(jnp.float32)
    grad_branch_mlp = (gate_mlp[:, None, :] * grad_out).astype(jnp.bfloat16)
    grad_gate_mlp = jnp.sum(grad_out * branch_mlp, axis=1)
    flat_grad_mlp = spread_grads(grad_branch_mlp).reshape(row_count, model_width)
    grad_down_bias = jnp.sum(flat_grad_mlp, axis=0, dtype=jnp.float32)
    grad_down_weight = inner_rows(active, flat_grad_mlp)
    grad_active = against(flat_grad_mlp, back_down)
    _, gelu_pull = jax.vjp(partial(jax.nn.gelu, approximate=True), upward)
    grad_upward = gelu_pull(grad_active)[0].astype(jnp.bfloat16)
    grad_up_bias = jnp.sum(grad_upward, axis=0, dtype=jnp.float32)
    grad_up_weight = inner_rows(flat_mlp, grad_upward)
    grad_normed_mlp = fold_grads(against(grad_upward, back_up).reshape(images, length, model_width))
    _, mlp_pull = jax.vjp(modulate_images, after_attn, shift_mlp, scale_mlp)
    grad_after, grad_shift_mlp, grad_scale_mlp = mlp_pull(grad_normed_mlp)
    grad_after = grad_out + grad_after
    grad_branch_attn = (gate_attn[:, None, :] * grad_after).astype(jnp.bfloat16)
    grad_gate_attn = jnp.sum(grad_after * branch_attn, axis=1)
    flat_grad_attn = spread_grads(grad_branch_attn).reshape(row_count, model_width)
    grad_out_bias = jnp.sum(flat_grad_attn, axis=0, dtype=jnp.float32)
    grad_out_weight = inner_rows(flat_attended, flat_grad_attn)
    grad_attended = against(flat_grad_attn, back_out).astype(jnp.bfloat16)

    def attend_back(bundle):
        queries_img, keys_img, values_img, grads_img, totals_img = bundle
        query_parts = []
        grad_keys_img = jnp.zeros(keys_img.shape, jnp.float32)
        grad_values_img = jnp.zeros(values_img.shape, jnp.float32)
        for offset in range(0, length, block_rows):
            query_block = queries_img[offset : offset + block_rows]
            grad_block = grads_img[offset : offset + block_rows]
            logits = (
                jnp.einsum(
                    "qhe,khe->hqk", query_block, keys_img, preferred_element_type=jnp.float32
                )
                * head_scale
            )
            shares = jnp.exp(logits - totals_img[:, offset : offset + block_rows, None])
            grad_shares = jnp.einsum(
                "qhe,khe->hqk", grad_block, values_img, preferred_element_type=jnp.float32
            )
            row_inner = jnp.sum(shares * grad_shares, axis=2, keepdims=True)
            grad_logits = (shares * (grad_shares - row_inner)).astype(jnp.bfloat16)
            query_parts.append(
                (
                    jnp.einsum(
                        "hqk,khe->qhe", grad_logits, keys_img, preferred_element_type=jnp.float32
                    )
                    * head_scale
                ).astype(jnp.bfloat16)
            )
            grad_keys_img = (
                grad_keys_img
                + jnp.einsum(
                    "hqk,qhe->khe", grad_logits, query_block, preferred_element_type=jnp.float32
                )
                * head_scale
            )
            grad_values_img = grad_values_img + jnp.einsum(
                "hqk,qhe->khe",
                shares.astype(jnp.bfloat16),
                grad_block,
                preferred_element_type=jnp.float32,
            )
        return (
            jnp.concatenate(query_parts, 0),
            grad_keys_img.astype(jnp.bfloat16),
            grad_values_img.astype(jnp.bfloat16),
        )

    grad_queries, grad_keys, grad_values = lax.map(
        attend_back,
        (
            by_head(queries),
            by_head(key_rows),
            by_head(value_rows),
            by_head(grad_attended),
            log_totals,
        ),
    )
    grad_queries = grad_queries.reshape(row_count, local_width)
    grad_keys = grad_keys.reshape(row_count, local_width)
    grad_values = grad_values.reshape(row_count, local_width)
    grad_query_bias = jnp.sum(grad_queries, axis=0, dtype=jnp.float32)
    grad_value_bias = jnp.sum(grad_values, axis=0, dtype=jnp.float32)
    grad_query_weight = inner_rows(flat_attn, grad_queries)
    grad_key_weight = inner_rows(flat_attn, grad_keys)
    grad_value_weight = inner_rows(flat_attn, grad_values)
    partial_normed = (
        against(grad_queries, back_query)
        + against(grad_keys, back_key)
        + against(grad_values, back_value)
    )
    grad_normed_attn = fold_grads(partial_normed.reshape(images, length, model_width))
    _, attn_pull = jax.vjp(modulate_images, inputs, shift_attn, scale_attn)
    grad_inputs, grad_shift_attn, grad_scale_attn = attn_pull(grad_normed_attn)
    grad_tokens = grad_after + grad_inputs
    modulation_terms = jnp.concatenate(
        [
            grad_shift_attn,
            grad_scale_attn,
            grad_gate_attn,
            grad_shift_mlp,
            grad_scale_mlp,
            grad_gate_mlp,
        ],
        axis=1,
    )
    grad_modulation = lax.psum_scatter(
        modulation_terms, "tensor", scatter_dimension=1, tiled=True
    ).astype(jnp.bfloat16)
    grad_ada_bias = jnp.sum(grad_modulation, axis=0, dtype=jnp.float32)
    grad_ada_weight = inner_rows(lifted_low, grad_modulation)
    grad_lifted = lax.psum(against(grad_modulation, back_ada), "tensor")
    _, silu_pull = jax.vjp(jax.nn.silu, conditioning)
    grad_conditioning = silu_pull(grad_lifted)[0]
    weight_grads = (
        lax.psum_scatter(grad_query_weight, "dp", scatter_dimension=0, tiled=True),
        lax.psum_scatter(grad_key_weight, "dp", scatter_dimension=0, tiled=True),
        lax.psum_scatter(grad_value_weight, "dp", scatter_dimension=0, tiled=True),
        lax.psum_scatter(grad_out_weight, "dp", scatter_dimension=1, tiled=True),
        lax.psum_scatter(grad_up_weight, "dp", scatter_dimension=0, tiled=True),
        lax.psum_scatter(grad_down_weight, "dp", scatter_dimension=1, tiled=True),
        lax.psum_scatter(grad_ada_weight, "dp", scatter_dimension=0, tiled=True),
    )
    bias_grads = lax.psum(
        (
            grad_query_bias,
            grad_value_bias,
            grad_out_bias,
            grad_up_bias,
            grad_down_bias,
            grad_ada_bias,
        ),
        "dp",
    )
    limit = threshold[0]
    factor = jnp.sqrt(limit / jnp.maximum(peaks, limit))
    column_factor = jnp.repeat(factor, HEAD_DIM)
    query_clipped = (query_weight.astype(jnp.float32) * column_factor).astype(jnp.bfloat16)
    key_clipped = (key_weight.astype(jnp.float32) * column_factor).astype(jnp.bfloat16)
    query_bias_clipped = query_bias * column_factor
    return (
        block_out,
        grad_tokens,
        grad_conditioning,
        weight_grads[0],
        weight_grads[1],
        weight_grads[2],
        weight_grads[3],
        weight_grads[4],
        weight_grads[5],
        weight_grads[6],
        bias_grads[0],
        bias_grads[1],
        bias_grads[2],
        bias_grads[3],
        bias_grads[4],
        bias_grads[5],
        query_clipped,
        key_clipped,
        query_bias_clipped,
    )


def one_image_per_chip(
    tokens, conditioning, cotangent, query_weight, key_weight, value_weight, out_weight, up_weight,
    down_weight, ada_weight, query_bias, value_bias, out_bias, up_bias, down_bias, ada_bias, threshold,
):
    y, x, c, z = (lax.axis_index(a) for a in AXES)
    batch = 4 * y + 2 * x + c
    first = jnp.concatenate([query_weight, key_weight, value_weight, out_weight.T], axis=1)
    shard = jnp.stack([first, up_weight, down_weight.T])
    lift_own = jnp.pad(jax.nn.silu(conditioning).astype(bf).astype(f32), ((0, 6), (0, 0)))
    z_bias = jnp.concatenate([query_bias, value_bias, up_bias])[None]
    (
        full, own_tokens, own_cotangent, lifted_rows, vectors, biases, normed_attn, qkv, mate_kv, attended, totals,
        peak, branch_attn, normed_mlp, active, slope, grad_down,
    ) = forward(shard, tokens, cotangent, lift_own, ada_weight, ada_bias[None], z_bias, out_bias[None])
    sums, block_rows, token_rows, _, _, _, grad_ada_weight, grad_ada_bias, lifted, totals = backward(
        full, own_tokens, own_cotangent, normed_attn, normed_mlp, qkv, mate_kv, attended, totals, peak, branch_attn,
        active, slope, grad_down, vectors, lifted_rows, ada_weight, down_bias[None],
    )
    own_lifted = lax.dynamic_slice(lifted.reshape(8, 16, ROWS), (0, 2 * batch, 0), (8, 2, ROWS))
    own_lifted = jnp.swapaxes(own_lifted, 0, 1).reshape(2, 8 * ROWS)
    _, silu_pull = jax.vjp(jax.nn.silu, conditioning)
    grad_conditioning = silu_pull(own_lifted)[0]
    first_bias = lax.dynamic_slice(totals, (z, 0), (1, COLS))[0]
    grad_query_bias = first_bias[:HS]
    grad_value_bias = first_bias[2 * HS : 3 * HS]
    grad_up_bias = lax.dynamic_slice(totals, (4 + z, 0), (1, COLS))[0]
    grad_out_bias = totals[8, :COLS]
    grad_down_bias = totals[9, :COLS]
    grad_ada_bias = grad_ada_bias[0]
    limit = threshold[0]
    peaks = lax.dynamic_slice(totals[:, COLS], (4 * z,), (4,))
    factor = jnp.sqrt(limit / jnp.maximum(peaks, limit))
    column_factor = jnp.repeat(factor, HEAD_DIM)
    query_clipped = (query_weight.astype(f32) * column_factor).astype(bf)
    key_clipped = (key_weight.astype(f32) * column_factor).astype(bf)
    return (
        block_rows,
        token_rows.astype(f32),
        grad_conditioning,
        sums[0, :, :HS],
        sums[0, :, HS : 2 * HS],
        sums[0, :, 2 * HS : 3 * HS],
        sums[0, :, 3 * HS :].T,
        sums[1],
        sums[2].T,
        grad_ada_weight,
        grad_query_bias,
        grad_value_bias,
        grad_out_bias,
        grad_up_bias,
        grad_down_bias,
        grad_ada_bias,
        query_clipped,
        key_clipped,
        query_bias * column_factor,
    )


def solution(mesh):
    if dict(mesh.shape) == {"dp": 8, "tensor": 4}:
        mesh = Mesh(mesh.devices.reshape(2, 2, 2, 4), AXES)
        split, heads, body = ("y", "x", "core"), "z", one_image_per_chip
    else:
        split, heads, body = "dp", "tensor", local
    weight, turned, bias = P(split, heads), P(heads, split), P(heads)
    rows = P(split, heads, None)
    in_specs = (
        rows, P(split, None), rows, weight, weight, weight, turned, weight, turned, weight,
        bias, bias, P(), bias, P(), bias, P(),
    )
    out_specs = (
        rows, rows, P(split, None), weight, weight, weight, turned, weight, turned, weight,
        bias, bias, P(), bias, P(), bias, weight, weight, bias,
    )
    return jax.shard_map(body, mesh=mesh, in_specs=in_specs, out_specs=out_specs, check_vma=False)
```

```python
from functools import partial

import jax
import jax.numpy as jnp
from jax import lax
from jax.experimental import pallas as pl
from jax.experimental.pallas import tpu as pltpu
from jax.sharding import Mesh, PartitionSpec as P

HEAD_DIM=72
epsilon=1e-06
MESH = pl.DeviceIdType.MESH
AXES = ("y", "x", "core", "z")
ROWS, COLS, TOK = 144, 1152, 512
HS, KV0, KVW, AT0, ATW, ADA = 288, 256, 640, 768, 384, 1728
C = HEAD_DIM**-0.5
LOG2E = 1.4426950408889634
bf = jnp.bfloat16
f32 = jnp.float32
VM = pl.BlockSpec(memory_space=pltpu.VMEM)
HB = pl.BlockSpec(memory_space=pl.ANY)
S = jax.ShapeDtypeStruct
D = pltpu.SemaphoreType.DMA
V = pltpu.VMEM


def dg(a, b, ca, cb):
    return lax.dot_general(a, b, (((ca,), (cb,)), ((), ())), preferred_element_type=f32)


class Net:
    def __init__(self):
        self.y, self.x, self.c, self.z = (lax.axis_index(a) for a in AXES)
        y, x, c, z = self.y, self.x, self.c, self.z
        self.up, self.down = lax.rem(z + 1, 4), lax.rem(z + 3, 4)
        self.xn, self.yn, self.dn = (y, 1 - x, c, z), (1 - y, x, c, z), (1 - y, 1 - x, c, z)
        self.cn = (y, x, 1 - c, z)
        self.zpn, self.zmn = (y, x, c, self.up), (y, x, c, self.down)
        self.f, self.n = self.place(y, x)
        self.far = self.device(1 - self.f, self.n)
        self.near = self.device(self.f, 1 - self.n)

    def place(self, a, b):
        return (1 - self.c) * a + self.c * b, (1 - self.c) * b + self.c * a

    def device(self, f, n):
        y, x = self.place(f, n)
        return (y, x, self.c, self.z)

    def along_z(self, step):
        return (self.y, self.x, self.c, lax.rem(self.z + step, 4))

    def greet(self):
        bar = pltpu.get_barrier_semaphore()
        others = [self.xn, self.yn, self.dn]
        for dc in range(2):
            for dz in range(4):
                if dc or dz:
                    others.append((self.y, self.x, lax.rem(self.c + dc, 2), lax.rem(self.z + dz, 4)))
        for o in others:
            pl.semaphore_signal(bar, inc=1, device_id=o, device_id_type=MESH)
        pl.semaphore_wait(bar, len(others))


def remote(src, dst, send, recv, device):
    return pltpu.make_async_remote_copy(
        src_ref=src, dst_ref=dst, send_sem=send, recv_sem=recv, device_id=device, device_id_type=MESH
    )


def landed(ref, sem):
    pltpu.make_async_copy(ref, ref, sem).wait()


def gelu_pair(u):
    k = 0.7978845608028654
    u2 = u * u
    t = jnp.tanh(k * u * (1.0 + 0.044715 * u2))
    h = 0.5 * (1.0 + t)
    return u * h, h + 0.5 * u * (1.0 - t * t) * (k * (1.0 + 3.0 * 0.044715 * u2))


class Gather:
    def __init__(self, net, g, shard, send, zsend, recv):
        self.net, self.g, self.shard, self.send, self.zsend, self.recv = net, g, shard, send, zsend, recv

    def slot(self, t, f, n, c, z):
        y, x = self.net.place(f, n)
        row = pl.multiple_of((4 * y + 2 * x + c) * ROWS, 16)
        return self.g.at[t, pl.ds(row, ROWS), pl.ds(pl.multiple_of(z * COLS, 128), COLS)]

    def sem(self, t, f, n, c, z):
        y, x = self.net.place(f, n)
        return self.recv.at[t, 4 * y + 2 * x + c, z]

    def put(self, u, k, device, f, n, z, own=False):
        t = lax.div(u, 4)
        s = self.slot(t, f, n, self.net.c, z)
        return remote(self.shard.at[t] if own else s, s, self.send.at[u, k], self.sem(t, f, n, self.net.c, z), device)

    def arrived(self, t, f, n, c, z):
        landed(self.slot(t, f, n, c, z), self.sem(t, f, n, c, z))

    def nth(self, k):
        z = self.net.z
        after = ((0, 1, 2, 3), (1, 0, 2, 3), (2, 3, 1, 0), (3, 2, 1, 0))
        return sum(
            jnp.where(jnp.logical_and(z == i, k == j), after[i][j], 0)
            for i in range(4) for j in range(4)
        )

    def onward(self, t, k, zz, act, own=False):
        net = self.net
        s = self.slot(t, net.f, net.n, net.c, zz)
        src = self.shard.at[t] if own else s
        sem = self.sem(t, net.f, net.n, net.c, zz)
        up = jnp.logical_and(zz <= net.z, net.z < 3)
        down = jnp.logical_and(zz >= net.z, net.z > 0)

        @pl.when(up)
        def _():
            act(remote(src, s, self.zsend.at[t, k, 0], sem, net.zpn))

        @pl.when(down)
        def _():
            act(remote(src, s, self.zsend.at[t, k, 1], sem, net.zmn))

    def copies(self, u, own=False):
        net = self.net
        zz = net.z if own else self.nth(lax.rem(u, 4))
        f, n = net.f, net.n
        return (
            [self.put(u, 0, net.near, f, n, zz, own), self.put(u, 1, net.far, f, n, zz, own), self.put(u, 2, net.cn, f, n, zz, own)],
            [self.put(u, 3, net.far, f, 1 - n, zz), self.put(u, 4, net.cn, f, 1 - n, zz), self.put(u, 5, net.cn, 1 - f, n, zz)],
            [self.put(u, 6, net.cn, 1 - f, 1 - n, zz)],
        )

    def line(self, u):
        t, k = lax.div(u, 4), lax.rem(u, 4)
        pl.when(k == 0)(lambda: self.onward(t, k, self.net.z, lambda cp: cp.start(), True))

        @pl.when(k > 0)
        def _():
            zz = self.nth(k)
            self.arrived(t, self.net.f, self.net.n, self.net.c, zz)
            self.onward(t, k, zz, lambda cp: cp.start())

    def tok(self, p):
        self.token_rows.piece(p)

    def cot(self, p):
        self.cot_rows.piece(p)

    def mid(self, u):
        pl.when(jnp.logical_and(self.net.z > 0, self.net.z < 3))(lambda: self.line(u))

    def end(self, u):
        pl.when(lax.rem(self.net.z, 3) == 0)(lambda: self.line(u))

    def spread(self, u):
        k = lax.rem(u, 4)

        @pl.when(k == 0)
        def _():
            for cp in self.copies(u, True)[0]:
                cp.start()

        @pl.when(k > 0)
        def _():
            for cp in self.copies(u)[0]:
                cp.start()

    def across(self, u):
        net, t = self.net, lax.div(u, 4)
        zz = self.nth(lax.rem(u, 4))
        a, b, d = self.copies(u)[1]
        self.arrived(t, net.f, 1 - net.n, net.c, zz)
        a.start()
        b.start()
        self.arrived(t, 1 - net.f, net.n, net.c, zz)
        d.start()

    def corner(self, u):
        net, t = self.net, lax.div(u, 4)
        self.arrived(t, 1 - net.f, 1 - net.n, net.c, self.nth(lax.rem(u, 4)))
        self.copies(u)[2][0].start()

    def do(self, *steps):
        for step, u in steps:
            step(self, u if step in (Gather.tok, Gather.cot) else jnp.int32(u))

    def at(self, point, table):
        for p, steps in enumerate(table):
            if steps:
                pl.when(point == p)(lambda: self.do(*steps))

    def from_mate(self, t):
        def one(i, _):
            self.arrived(t, lax.div(i, 8), lax.rem(lax.div(i, 4), 2), 1 - self.net.c, lax.rem(i, 4))
            return 0

        lax.fori_loop(0, 16, one, 0)

    def finish(self):
        def one(u, _):
            for group in self.copies(u):
                for cp in group:
                    cp.wait_send()
            t, k = lax.div(u, 4), lax.rem(u, 4)
            self.onward(t, k, self.nth(k), lambda cp: cp.wait_send())
            return 0

        lax.fori_loop(0, 12, one, 0)


def rows_out(net, i):
    dc, dz = lax.div(net.z, 2), 2 * net.c + i
    here = jnp.logical_and(dc == net.c, dz == net.z)
    return (net.y, net.x, dc, dz), pl.multiple_of(lax.rem(net.z, 2) * 256, 256), here


class Rows:
    def __init__(self, net, src, dst, send, recv):
        self.net, self.src, self.dst, self.send, self.recv = net, src, dst, send, recv

    def local(self):
        for i in range(2):
            _, row, here = rows_out(self.net, i)

            @pl.when(here)
            def _():
                self.dst[pl.ds(row, 256)] = self.src[i]

    def copy(self, i, first, count):
        device, row, here = rows_out(self.net, i)
        return remote(
            self.src.at[i, pl.ds(first, count)], self.dst.at[pl.ds(row + first, count)],
            self.send.at[i], self.recv.at[lax.rem(self.net.z, 2)], device,
        ), jnp.logical_not(here)

    def piece(self, p):
        cp, cond = self.copy(p % 2, p // 2 * 64, 64)
        pl.when(cond)(cp.start)

    def sent(self):
        for i in range(2):
            cp, cond = self.copy(i, 0, 256)
            pl.when(cond)(cp.wait_send)

    def arrivals(self):
        net = self.net
        for k in range(2):
            here = jnp.logical_and(lax.div(net.z, 2) == net.c, 2 * net.c + k == net.z)
            pl.when(jnp.logical_not(here))(lambda: landed(self.dst.at[pl.ds(k * 256, 256)], self.recv.at[k]))


def normalize(v):
    mean = jnp.mean(v, axis=-1, keepdims=True)
    centred = v - mean
    r = lax.rsqrt(jnp.mean(centred * centred, axis=-1, keepdims=True) + epsilon)
    return centred * r, r


def by_rows(step, body):
    def one(i, _):
        body(pl.ds(pl.multiple_of(i * step, step), step))
        return 0

    lax.fori_loop(0, TOK // step, one, 0)


TABLE = (
    ((Gather.across, 5),),
    ((Gather.end, 7), (Gather.spread, 7)),
    ((Gather.mid, 9), (Gather.mid, 10), (Gather.corner, 8)),
    ((Gather.across, 6), (Gather.end, 9), (Gather.spread, 9)),
    ((Gather.mid, 11), (Gather.corner, 5)),
    ((Gather.across, 7), (Gather.end, 10), (Gather.spread, 10), (Gather.cot, 0), (Gather.cot, 1)),
    ((Gather.end, 11), (Gather.spread, 11), (Gather.corner, 6), (Gather.cot, 2)),
    ((Gather.across, 9), (Gather.cot, 3)),
    ((Gather.across, 10), (Gather.cot, 4), (Gather.cot, 5)),
    ((Gather.cot, 6),),
    ((Gather.across, 11), (Gather.corner, 9), (Gather.cot, 7)),
    (),
    ((Gather.corner, 10),),
    (),
    ((Gather.corner, 11),),
)


def forward_kernel(
    shard, tokens, cotangent, lift_own, ada, ada_bias, z_bias, out_bias,
    g, tok, cot, lift_rows, vectors, biases, x_out, qkv_out, kvo_out, att_out, lse, peak, branch_out, nm_out, act_out, gd_out, d2,
    tok_v, cot_v, lift, part, part_in, four, four_in, zall, x_ref, w, qkv, kvo, att, branch, qh, kh, vh, oh, gbt, act_buf, gd_buf, dbuf,
    gsend, gzsend, grecv, lsem, rsend, rrecv, small_send, small_recv, wsem, ksend, krecv, osem, asem, gdsem, dsem,
):
    net = Net()
    y, x, c, z = net.y, net.x, net.c, net.z
    plane = 2 * y + x
    net.greet()
    flow = Gather(net, g, shard, gsend, gzsend, grecv)
    lift[plane, c] = lift_own[...]
    small = [remote(lift.at[plane, c], lift.at[plane, c], small_send.at[0], small_recv.at[0], net.cn)]
    small[0].start()
    token_rows = Rows(net, tokens, tok_v, rsend.at[0], rrecv.at[0])
    cot_rows = Rows(net, cotangent, cot_v, rsend.at[1], rrecv.at[1])
    flow.token_rows, flow.cot_rows = token_rows, cot_rows
    flow.do((Gather.line, 0))
    own = [pltpu.make_async_copy(shard.at[t], flow.slot(t, net.f, net.n, c, z), lsem.at[t]) for t in range(3)]
    for cp in own:
        cp.start()

    landed(lift.at[plane, 1 - c], small_recv.at[0])
    peers = ((net.xn, 2 * y + 1 - x), (net.yn, 2 - 2 * y + x), (net.dn, 3 - plane))
    for k, (dev, _) in enumerate(peers):
        cp = remote(lift.at[plane], lift.at[plane], small_send.at[1 + k], small_recv.at[1 + k], dev)
        cp.start()
        small.append(cp)
    flow.do((Gather.spread, 0), (Gather.spread, 4), (Gather.line, 1))
    for k, (_, p) in enumerate(peers):
        landed(lift.at[p], small_recv.at[1 + k])
    every = jnp.concatenate([lift[p, k, 0:2] for p in range(4) for k in range(2)], axis=0).astype(bf)
    batch = 4 * y + 2 * x + c
    pick = lax.broadcasted_iota(jnp.int32, (COLS, ROWS), 0) == lax.broadcasted_iota(jnp.int32, (COLS, ROWS), 1) + batch * ROWS
    rows = dg(every, jnp.where(pick, 1.0, 0.0).astype(bf), 1, 0)
    lift_rows[...] = rows
    partial = dg(rows.astype(bf), ada[...], 1, 0)
    part[...] = jnp.zeros_like(part)
    for p in range(4):
        part[p, 0:4] = partial[4 * p : 4 * p + 4]
    for k, (dev, p) in enumerate(peers):
        cp = remote(part.at[p], part_in.at[k], small_send.at[4 + k], small_recv.at[4 + k], dev)
        cp.start()
        small.append(cp)
    flow.do((Gather.spread, 1), (Gather.line, 2), (Gather.across, 0), (Gather.spread, 2), (Gather.line, 3), (Gather.spread, 3))
    for k in range(3):
        landed(part_in.at[k], small_recv.at[4 + k])
    four[...] = part[plane] + part_in[0] + part_in[1] + part_in[2]
    cp = remote(four, four_in, small_send.at[7], small_recv.at[7], net.cn)
    cp.start()
    small.append(cp)
    landed(four_in, small_recv.at[7])
    zall[z] = four[...] + four_in[...] + ada_bias[...]
    zall[z, 4:5] = z_bias[...]
    for k in range(3):
        cp = remote(zall.at[z], zall.at[z], small_send.at[8 + k], small_recv.at[8 + k], net.along_z(k + 1))
        cp.start()
        small.append(cp)
    flow.do(
        (Gather.across, 4), (Gather.tok, 0), (Gather.tok, 1), (Gather.across, 1), (Gather.tok, 2), (Gather.tok, 3), (Gather.across, 2), (Gather.tok, 4), (Gather.tok, 5),
        (Gather.across, 3), (Gather.spread, 8), (Gather.tok, 6), (Gather.tok, 7), (Gather.line, 4),
    )
    token_rows.local()
    cot_rows.local()
    for k in range(3):
        landed(zall.at[lax.rem(z + 3 - k, 4)], small_recv.at[8 + k])
    pieces = [zall[k, pl.ds(z, 1)] for k in range(4)]
    half = COLS // 2
    vectors[0:1] = pieces[0][:, :COLS]
    vectors[1:2] = jnp.concatenate([pieces[0][:, COLS:], pieces[1][:, :half]], axis=1)
    vectors[2:3] = pieces[1][:, half:]
    vectors[3:4] = pieces[2][:, :COLS]
    vectors[4:5] = jnp.concatenate([pieces[2][:, COLS:], pieces[3][:, :half]], axis=1)
    vectors[5:6] = pieces[3][:, half:]
    vectors[6:8] = jnp.zeros((2, COLS), f32)
    nothing = jnp.zeros((1, HS), f32)
    for k in range(4):
        b = zall[k, 4:5]
        biases[k, 0:1] = jnp.concatenate([b[:, :HS], nothing, b[:, HS : 2 * HS], nothing], axis=1)
        biases[k, 1:2] = b[:, 2 * HS :]

    flow.do((Gather.corner, 0), (Gather.corner, 4), (Gather.corner, 1), (Gather.corner, 2))
    token_rows.arrivals()

    def first_norm(r):
        n, _ = normalize(tok_v[r].astype(f32))
        x_ref[r] = (n * (1.0 + vectors[1:2]) + vectors[0:1]).astype(bf)

    by_rows(64, first_norm)
    outs = [pltpu.make_async_copy(x_ref, x_out, osem.at[1]), pltpu.make_async_copy(tok_v, tok, osem.at[0])]
    for cp in outs:
        cp.start()
    flow.do((Gather.line, 5), (Gather.spread, 5), (Gather.mid, 6), (Gather.corner, 3))
    flow.from_mate(0)

    def load_w(t, k):
        return pltpu.make_async_copy(g.at[t, :, pl.ds(k * COLS, COLS)], w.at[k], wsem.at[k])

    own[0].wait()
    for k in range(4):
        load_w(0, k).start()

    def kv(k):
        return remote(qkv.at[k, :, pl.ds(KV0, KVW)], kvo.at[k], ksend.at[k], krecv.at[k], net.cn)

    for k in range(4):
        load_w(0, k).wait()
        qkv[k] = (dg(x_ref[...], w[k], 1, 0) + biases[k, 0:1]).astype(bf)
        kv(k).start()
        flow.do(*((), ((Gather.end, 6), (Gather.spread, 6), (Gather.across, 8)), ((Gather.mid, 7), (Gather.line, 8)), ())[k])
    cp = pltpu.make_async_copy(qkv, qkv_out, osem.at[2])
    cp.start()
    outs.append(cp)
    branch[...] = jnp.broadcast_to(out_bias[...], (TOK, COLS))


    def chunk(k, _):
        flow.at(2 * k, TABLE)
        kv(k).wait_recv()
        for j in range(4):
            a = j * HEAD_DIM
            qh[j] = qkv[k, :, a : a + HEAD_DIM]
            kh[j, :TOK] = qkv[k, :, HS + a : HS + a + HEAD_DIM]
            vh[j, :TOK] = qkv[k, :, 2 * HS + a : 2 * HS + a + HEAD_DIM]
            kh[j, TOK:] = kvo[k, :, HS - KV0 + a : HS - KV0 + a + HEAD_DIM]
            vh[j, TOK:] = kvo[k, :, 2 * HS - KV0 + a : 2 * HS - KV0 + a + HEAD_DIM]

        def head(j, _):
            h = k * 4 + j
            s = dg(kh[j], qh[j], 1, 1)
            m = jnp.max(s, axis=0, keepdims=True)
            p = jnp.exp2((s - m) * (C * LOG2E))
            l = jnp.sum(p, axis=0, keepdims=True)
            o = dg(vh[j], p.astype(bf), 0, 0) / l
            oh[j] = o.T.astype(bf)
            lse[h] = m * (C * LOG2E) + jnp.log2(l)
            peak[h] = jnp.broadcast_to(jnp.max(m, axis=1, keepdims=True) * C, (1, 128))
            pl.when(j == 1)(lambda: flow.at(2 * k + 1, TABLE))
            return 0

        lax.fori_loop(0, 4, head, 0)
        att[k] = jnp.concatenate([jnp.zeros((TOK, ATW - HS), bf)] + [oh[j] for j in range(4)], axis=1)
        branch[...] += dg(att[k], w[k, :, AT0:], 1, 1)
        return 0

    lax.fori_loop(0, 4, chunk, 0)
    for src, dst, k in ((kvo, kvo_out, 3), (att, att_out, 4), (branch, branch_out, 5)):
        cp = pltpu.make_async_copy(src, dst, osem.at[k])
        cp.start()
        outs.append(cp)
    outs[0].wait()

    def second_norm(r):
        after = tok_v[r].astype(f32) + vectors[2:3] * branch[r]
        n, _ = normalize(after)
        x_ref[r] = (n * (1.0 + vectors[4:5]) + vectors[3:4]).astype(bf)

    by_rows(64, second_norm)
    cp = pltpu.make_async_copy(x_ref, nm_out, osem.at[6])
    cp.start()
    outs[0] = cp
    flow.do((Gather.corner, 7),)
    flow.from_mate(1)
    own[1].wait()
    for k in range(4):
        load_w(1, k).start()

    def slope_store(k):
        i = lax.rem(k, 2)
        return pltpu.make_async_copy(gd_buf.at[i], gd_out.at[k], gdsem.at[i])

    def hidden(k, _):
        i = lax.rem(k, 2)
        pltpu.make_async_copy(g.at[1, :, pl.ds(pl.multiple_of(k * COLS, 128), COLS)], w.at[k], wsem.at[k]).wait()
        pl.when(k >= 2)(lambda: slope_store(k - 2).wait())
        gd_buf[i] = dg(x_ref[...], w[k], 1, 0)

        def activate(r):
            a, d = gelu_pair(gd_buf[i, r] + biases[k, 1:2])
            act_buf[k, r] = a.astype(bf)
            gd_buf[i, r] = d

        by_rows(64, activate)
        slope_store(k).start()
        pltpu.make_async_copy(act_buf.at[k], act_out.at[k], asem.at[k]).start()
        flow.at(8 + k, TABLE)
        return 0

    lax.fori_loop(0, 4, hidden, 0)
    cot_rows.arrivals()
    cp = pltpu.make_async_copy(cot_v, cot, osem.at[1])
    cp.start()
    outs.append(cp)

    def gated(r):
        x_ref[r] = (vectors[5:6] * cot_v[r].astype(f32)).astype(bf)

    outs[0].wait()
    by_rows(64, gated)
    gbt[...] = x_ref[...].T

    def down_store(k):
        i = lax.rem(k, 2)
        return pltpu.make_async_copy(dbuf.at[i], d2.at[:, pl.ds(pl.multiple_of(k * COLS, 128), COLS)], dsem.at[i])

    def down(k, _):
        i = lax.rem(k, 2)
        pl.when(k >= 2)(lambda: down_store(k - 2).wait())
        dbuf[i] = dg(gbt[...], act_buf[k], 1, 0).astype(bf)
        down_store(k).start()
        flow.at(12 + k, TABLE)
        return 0

    lax.fori_loop(0, 4, down, 0)
    for k in (2, 3):
        slope_store(k).wait()
        down_store(k).wait()
    for k in range(4):
        pltpu.make_async_copy(act_buf.at[k], act_out.at[k], asem.at[k]).wait()
    flow.from_mate(2)
    flow.finish()
    for cp in outs[1:]:
        cp.wait()
    for k in range(4):
        kv(k).wait_send()
    for cp in small:
        cp.wait_send()
    own[2].wait()
    token_rows.sent()
    cot_rows.sent()


def forward(shard, tokens, cotangent, lift_own, ada, ada_bias, z_bias, out_bias):
    rows = S((TOK, COLS), bf)
    wide = S((TOK, COLS), f32)
    return pl.pallas_call(
        forward_kernel,
        name="forward",
        out_shape=(
            S((3, 8 * ROWS, 4 * COLS), bf), rows, rows, S((16, ROWS), f32), S((8, COLS), f32), S((4, 2, COLS), f32),
            rows, S((4, TOK, COLS), bf), S((4, TOK, KVW), bf), S((4, TOK, ATW), bf), S((16, 1, TOK), f32),
            S((16, 1, 128), f32), wide, rows, S((4, TOK, COLS), bf), S((4, TOK, COLS), f32), S((8 * ROWS, 4 * COLS), bf),
        ),
        in_specs=[VM] * 8,
        out_specs=(HB, HB, HB, VM, VM, VM, HB, HB, HB, HB, VM, VM, HB, HB, HB, HB, HB),
        scratch_shapes=[
            V((TOK, COLS), bf), V((TOK, COLS), bf), V((4, 2, 8, COLS), f32), V((4, 8, ADA), f32), V((3, 8, ADA), f32),
            V((8, ADA), f32), V((8, ADA), f32), V((4, 8, ADA), f32), V((TOK, COLS), bf), V((4, COLS, COLS), bf),
            V((4, TOK, COLS), bf), V((4, TOK, KVW), bf), V((4, TOK, ATW), bf), V((TOK, COLS), f32),
            V((4, TOK, HEAD_DIM), bf), V((4, 2 * TOK, HEAD_DIM), bf), V((4, 2 * TOK, HEAD_DIM), bf), V((4, TOK, HEAD_DIM), bf),
            V((COLS, TOK), bf), V((4, TOK, COLS), bf), V((2, TOK, COLS), f32), V((2, COLS, COLS), bf),
            D((12, 7)), D((3, 4, 2)), D((3, 8, 4)), D((3,)), D((2, 2)), D((2, 2)), D((11,)), D((11,)), D((4,)), D((4,)), D((4,)),
            D((7,)), D((4,)), D((2,)), D((2,)),
        ],
        compiler_params=pltpu.CompilerParams(collective_id=1, has_side_effects=True, vmem_limit_bytes=60 * 2**20),
    )(shard, tokens, cotangent, lift_own, ada, ada_bias, z_bias, out_bias)


LINE = (0, 3, 1, 2)


class Scatter:
    def __init__(self, net, source, out, stage, out_sem, rc, far_in, near_in, line_in, side_in, acc, ctmp, ftmp,
                 csend, crecv, own_sem, ctmp_sem, fsend, frecv, ftmp_sem, nsend, nrecv, lsend, lrecv, srecv):
        self.__dict__.update(locals())

    def block(self, v, yy, xx, c):
        row = pl.multiple_of((4 * yy + 2 * xx + c) * ROWS, 16)
        return self.source(v).at[pl.ds(row, ROWS), pl.ds(LINE[v % 4] * COLS, COLS)]

    def places(self):
        return [(yy, xx) for yy in range(2) for xx in range(2)]

    def to_mate(self, v, yy, xx):
        return remote(
            self.block(v, yy, xx, 1 - self.net.c), self.rc.at[v, yy, xx],
            self.csend.at[v, yy, xx], self.crecv.at[v, yy, xx], self.net.cn,
        )

    def begin(self, v):
        for yy, xx in self.places():
            self.to_mate(v, yy, xx).start()

    def to_far(self, v, n):
        yy, xx = self.net.place(1 - self.net.f, n)
        return remote(self.acc.at[v % 4, yy, xx], self.far_in.at[v, n], self.fsend.at[v, n], self.frecv.at[v, n], self.net.far)

    def to_near(self, v):
        yy, xx = self.net.place(self.net.f, 1 - self.net.n)
        return remote(self.acc.at[v % 4, yy, xx], self.near_in.at[v], self.nsend.at[v], self.nrecv.at[v], self.net.near)

    def own_loads(self, v):
        return [
            pltpu.make_async_copy(self.block(v, yy, xx, self.net.c), self.acc.at[v % 4, yy, xx], self.own_sem.at[yy, xx])
            for yy, xx in self.places()
        ]

    def mate_loads(self, v, f):
        for n in range(2):
            yy, xx = self.net.place(f, n)
            yield pltpu.make_async_copy(self.rc.at[v, yy, xx], self.ctmp.at[f, n], self.ctmp_sem.at[f, n])

    def add(self, a, b):
        def one(i, _):
            r = pl.ds(pl.multiple_of(i * 48, 16), 48)
            a[r] = a[r] + b[r]
            return 0

        lax.fori_loop(0, ROWS // 48, one, 0)

    def fetch(self, v):
        if v >= 4:
            for n in range(2):
                self.to_far(v - 4, n).wait_send()
            self.to_near(v - 4).wait_send()
        for cp in self.own_loads(v):
            cp.start()
        for yy, xx in self.places():
            landed(self.rc.at[v, yy, xx], self.crecv.at[v, yy, xx])
        for f in (1 - self.net.f, self.net.f):
            for cp in self.mate_loads(v, f):
                cp.start()

    def core(self, v):
        for cp in self.own_loads(v):
            cp.wait()
        for f in (1 - self.net.f, self.net.f):
            for n, cp in enumerate(self.mate_loads(v, f)):
                cp.wait()
                yy, xx = self.net.place(f, n)
                self.add(self.acc.at[v % 4, yy, xx], self.ctmp.at[f, n])
                if f is not self.net.f:
                    self.to_far(v, n).start()

    def far_loads(self, v):
        return [pltpu.make_async_copy(self.far_in.at[v, n], self.ftmp.at[n], self.ftmp_sem.at[n]) for n in range(2)]

    def bring(self, v):
        for n, cp in enumerate(self.far_loads(v)):
            landed(self.far_in.at[v, n], self.frecv.at[v, n])
            cp.start()

    def far(self, v):
        for cp in self.far_loads(v):
            cp.wait()
        for n in (1 - self.net.n, self.net.n):
            yy, xx = self.net.place(self.net.f, n)
            self.add(self.acc.at[v % 4, yy, xx], self.ftmp.at[n])
            if n is not self.net.n:
                self.to_near(v).start()

    def near(self, v):
        landed(self.near_in.at[v], self.nrecv.at[v])
        self.add(self.near_in.at[v], self.acc.at[v % 4, self.net.y, self.net.x])

    def hop(self, v, h, act):
        net, zz = self.net, LINE[v % 4]
        if h < zz:

            @pl.when(net.z == h)
            def _():
                act(v, h, remote(self.near_in.at[v], self.line_in.at[v], self.lsend.at[v], self.lrecv.at[v], net.zpn))

        if 3 - h > zz:

            @pl.when(net.z == 3 - h)
            def _():
                side = 3 - h - 1 == zz
                dst = self.side_in.at[v // 4] if side else self.line_in.at[v]
                sem = self.srecv.at[v // 4] if side else self.lrecv.at[v]
                act(v, h, remote(self.near_in.at[v], dst, self.lsend.at[v], sem, net.zmn))

    def pass_on(self, v, h, cp):
        if h:
            landed(self.line_in.at[v], self.lrecv.at[v])
            self.add(self.near_in.at[v], self.line_in.at[v])
        cp.start()

    def line0(self, v):
        self.hop(v, 0, self.pass_on)

    def line1(self, v):
        self.hop(v, 1, self.pass_on)

    def line2(self, v):
        self.hop(v, 2, self.pass_on)

    def keep(self, t):
        return pltpu.make_async_copy(self.stage, self.out.at[t], self.out_sem)

    def last(self, v):
        t, zz = 2 - v // 4, LINE[v % 4]

        @pl.when(self.net.z == zz)
        def _():
            if zz > 0:
                landed(self.line_in.at[v], self.lrecv.at[v])
            if zz < 3:
                landed(self.side_in.at[v // 4], self.srecv.at[v // 4])
            if t < 2:
                self.keep(t + 1).wait()

            def one(i, _):
                r = pl.ds(pl.multiple_of(i * 16, 16), 16)
                total = self.near_in[v, r].astype(f32)
                if zz > 0:
                    total = total + self.line_in[v, r].astype(f32)
                if zz < 3:
                    total = total + self.side_in[v // 4, r].astype(f32)
                self.stage[r] = total
                return 0

            lax.fori_loop(0, ROWS // 16, one, 0)
            self.keep(t).start()

    def rows(self, p):
        self.block_back.piece(p)

    def toks(self, p):
        self.token_back.piece(p)

    def do(self, *steps):
        for step, v in steps:
            step(self, v)

    def at(self, point, table, base=0):
        for p, steps in enumerate(table):
            if steps:
                pl.when(point == base + p)(lambda: self.do(*steps))

    def finish(self):
        self.keep(0).wait()
        for v in range(12):
            for yy, xx in self.places():
                self.to_mate(v, yy, xx).wait_send()
            if v >= 8:
                for n in range(2):
                    self.to_far(v, n).wait_send()
                self.to_near(v).wait_send()
            for h in range(3):
                self.hop(v, h, lambda v, h, cp: cp.wait_send())


HIDDEN = (
    ((Scatter.core, 2), (Scatter.fetch, 3)),
    ((Scatter.bring, 0), (Scatter.far, 0), (Scatter.core, 3)),
    ((Scatter.begin, 4),),
    ((Scatter.bring, 1), (Scatter.far, 1)),
    ((Scatter.begin, 5),),
    ((Scatter.near, 0), (Scatter.line0, 0), (Scatter.fetch, 4), (Scatter.bring, 2)),
    ((Scatter.core, 4), (Scatter.far, 2), (Scatter.begin, 6)),
    ((Scatter.near, 1), (Scatter.line0, 1), (Scatter.fetch, 5)),
)
HEADS = (
    ((Scatter.far, 4), (Scatter.core, 7), (Scatter.rows, 0)),
    ((Scatter.bring, 5), (Scatter.rows, 1)),
    ((Scatter.far, 5), (Scatter.rows, 2)),
    ((Scatter.rows, 3),),
    ((Scatter.near, 4), (Scatter.line0, 4), (Scatter.rows, 4)),
    ((Scatter.bring, 6), (Scatter.far, 6), (Scatter.rows, 5)),
    ((Scatter.begin, 8), (Scatter.near, 5), (Scatter.line0, 5), (Scatter.rows, 6)),
    ((Scatter.bring, 7), (Scatter.far, 7), (Scatter.fetch, 8), (Scatter.line1, 0), (Scatter.line1, 1), (Scatter.rows, 7)),
    ((Scatter.core, 8), (Scatter.line1, 2), (Scatter.line1, 3)),
    ((Scatter.near, 6), (Scatter.line0, 6), (Scatter.line1, 4)),
    ((Scatter.begin, 9), (Scatter.line2, 0), (Scatter.line2, 1)),
    ((Scatter.fetch, 9), (Scatter.line2, 2), (Scatter.line2, 3), (Scatter.line1, 5)),
    ((Scatter.core, 9), (Scatter.near, 7), (Scatter.line0, 7), (Scatter.line2, 4)),
    ((Scatter.bring, 8), (Scatter.far, 8), (Scatter.line1, 6)),
    ((Scatter.begin, 10), (Scatter.last, 0), (Scatter.last, 1), (Scatter.line2, 5)),
    ((Scatter.fetch, 10), (Scatter.last, 2), (Scatter.last, 3), (Scatter.line1, 7)),
)


class Back:
    def __init__(self, net, src, dst, send, recv):
        self.net, self.src, self.dst, self.send, self.recv = net, src, dst, send, recv

    def copy(self, k, first, count):
        net = self.net
        dc, dz = lax.div(net.z, 2), 2 * net.c + k
        here = jnp.logical_and(dc == net.c, dz == net.z)
        rows, image = self.src.at[pl.ds(k * 256 + first, count)], self.dst.at[lax.rem(net.z, 2), pl.ds(first, count)]
        sem = self.recv.at[lax.rem(net.z, 2)]
        return remote(rows, image, self.send.at[k], sem, (net.y, net.x, dc, dz)), pltpu.make_async_copy(rows, image, sem), here

    def piece(self, p):
        cp, local, here = self.copy(p % 2, p // 2 * 64, 64)
        pl.when(jnp.logical_not(here))(cp.start)
        pl.when(here)(local.start)

    def sent(self):
        for k in range(2):
            cp, _, here = self.copy(k, 0, 256)
            pl.when(jnp.logical_not(here))(cp.wait_send)

    def arrivals(self):
        for i in range(2):
            landed(self.dst.at[i], self.recv.at[i])


def column_sum(v):
    return jnp.sum(v.astype(f32), axis=0, keepdims=True)


def backward_kernel(
    g, tok_in, cot_in, x_in, nm_in, qkv_in, kvo_in, att_in, lse, peak, branch_in, act_in, gd_in, d2, vectors, lift_rows, ada, down_bias,
    sums, block_rows, token_rows, d, rc, far_in, ada_grad, ada_bias_grad, lifted, totals,
    tok, cot, branch, gn, br, gb, gub, xt, gt, w1, act, dbuf, near_in, line_in, side_in, acc, ctmp, ftmp, mate_in,
    stage, bias, bias_in, terms, terms_in, image, pgl, pgl_in, four,
    out_sem, csend, crecv, own_sem, ctmp_sem, fsend, frecv, ftmp_sem, nsend, nrecv, lsend, lrecv, srecv,
    bsend, brecv, isem, w1_sem, w2_sem, act_sem, gd_sem, dsem, msend, mrecv, kvsem, small_send, small_recv,
):
    net = Net()
    y, x, c, z = net.y, net.x, net.c, net.z
    plane = 2 * y + x

    def fetch(src, dst, k):
        cp = pltpu.make_async_copy(src, dst, isem.at[k])
        cp.start()
        return cp

    first = [fetch(cot_in, cot, 0), fetch(nm_in, gub, 1), fetch(tok_in, tok, 2), fetch(branch_in, branch, 3)]

    def cols(ref, k):
        return ref.at[:, pl.ds(pl.multiple_of(zs(k) * COLS, 128), COLS)]

    def zs(k):
        return jnp.where(k == 0, 0, jnp.where(k == 1, 3, k - 1))

    def load_first(t, k):
        return pltpu.make_async_copy(cols(g.at[t], k), w1.at[lax.rem(k, 2)], w1_sem.at[lax.rem(k, 2)])

    def d_store(t, k):
        return pltpu.make_async_copy(dbuf, cols(d.at[t], k), dsem)

    load_first(1, jnp.int32(0)).start()
    net.greet()
    flow = Scatter(
        net, lambda v: d2 if v < 4 else d.at[2 - v // 4], sums, stage, out_sem, rc, far_in, near_in, line_in, side_in, acc, ctmp, ftmp,
        csend, crecv, own_sem, ctmp_sem, fsend, frecv, ftmp_sem, nsend, nrecv, lsend, lrecv, srecv,
    )
    for v in range(4):
        flow.begin(v)
    shift_attn, scale_attn, gate_attn, shift_mlp, scale_mlp, gate_mlp = [vectors[i : i + 1] for i in range(6)]
    terms[...] = jnp.zeros_like(terms)
    bias[...] = jnp.zeros_like(bias)
    for h in range(16):
        bias[h : h + 1, COLS:] = peak[h]
    gn[...] = jnp.zeros_like(gn)
    br[...] = jnp.zeros_like(br)
    first[0].wait()

    def gated(r):
        gb[r] = (gate_mlp * cot[r].astype(f32)).astype(bf)

    by_rows(64, gated)
    first[1].wait()
    xt[...] = gub[...].T

    def mlp(w2, gd):
        def loads(k):
            i = lax.rem(k, 2)
            return (
                load_first(1, k),
                pltpu.make_async_copy(cols(g.at[2], k), w2.at[i], w2_sem.at[i]),
                pltpu.make_async_copy(act_in.at[zs(k)], act.at[i], act_sem.at[i]),
                pltpu.make_async_copy(gd_in.at[zs(k)], gd.at[i], gd_sem.at[i]),
            )

        for cp in loads(jnp.int32(0))[1:]:
            cp.start()
        flow.do((Scatter.fetch, 0), (Scatter.core, 0), (Scatter.fetch, 1), (Scatter.core, 1), (Scatter.fetch, 2))

        def hidden(k, _):
            i = lax.rem(k, 2)
            for cp in loads(k):
                cp.wait()

            @pl.when(k < 3)
            def _():
                for cp in loads(k + 1):
                    cp.start()

            gub[...] = (dg(gb[...], w2[i], 1, 0) * gd[i]).astype(bf)
            bias[pl.ds(4 + zs(k), 1), :COLS] = column_sum(gub[...])
            br[...] += dg(act[i], w2[i], 1, 1)
            pl.when(k > 0)(lambda: d_store(1, k - 1).wait())
            flow.at(2 * k, HIDDEN)
            dbuf[...] = dg(xt[...], gub[...], 1, 0).astype(bf)
            d_store(1, k).start()
            gn[...] += dg(gub[...], w1[i], 1, 1)
            flow.at(2 * k + 1, HIDDEN)
            return 0

        lax.fori_loop(0, 4, hidden, 0)

    pl.run_scoped(mlp, V((2, COLS, COLS), bf), V((2, TOK, COLS), f32))
    load_first(0, jnp.int32(0)).start()
    d_store(1, jnp.int32(3)).wait()
    flow.do((Scatter.begin, 7), (Scatter.core, 5), (Scatter.bring, 3), (Scatter.far, 3))
    first[2].wait()
    first[3].wait()

    def second_norm(r):
        after = tok[r].astype(f32) + gate_attn * branch[r]
        n, s = normalize(after)
        mlp_out = br[r] + down_bias[...]
        gub[r] = (after + gate_mlp * mlp_out).astype(bf)
        go = cot[r].astype(f32)
        terms[5:6] += column_sum(go * mlp_out)
        gr = gn[r]
        terms[3:4] += column_sum(gr)
        terms[4:5] += column_sum(gr * n)
        e = gr * (1.0 + scale_mlp)
        ga = go + s * (e - jnp.mean(e, axis=-1, keepdims=True) - n * jnp.mean(e * n, axis=-1, keepdims=True))
        br[r] = ga
        terms[2:3] += column_sum(ga * branch[r])
        bias[9:10, :COLS] += column_sum(gb[r])
        low = (gate_attn * ga).astype(bf)
        bias[8:9, :COLS] += column_sum(low)
        gb[r] = low

    by_rows(64, second_norm)
    block_back = Back(net, gub, block_rows, bsend.at[0], brecv.at[0])
    flow.do((Scatter.near, 2), (Scatter.line0, 2), (Scatter.fetch, 6))
    flow.block_back = block_back
    flow.do((Scatter.core, 6),)
    load = fetch(x_in, cot, 0)
    gt[...] = gb[...].T
    flow.do((Scatter.near, 3), (Scatter.line0, 3), (Scatter.fetch, 7), (Scatter.bring, 4))
    gn[...] = jnp.zeros_like(gn)
    load.wait()
    xt[...] = cot[...].T

    def attention(kvo, att, qh, kh, vh, gh, dqh, dkh, dvh, dkm, dvm, mate_out):
        pack = cot

        def loads(k):
            i = lax.rem(k, 2)
            return (
                load_first(0, k),
                pltpu.make_async_copy(qkv_in.at[zs(k)], act.at[i], act_sem.at[i]),
                pltpu.make_async_copy(kvo_in.at[zs(k)], kvo, kvsem.at[0, i]),
                pltpu.make_async_copy(att_in.at[zs(k)], att.at[i], kvsem.at[1, i]),
            )

        for cp in loads(jnp.int32(0))[1:]:
            cp.start()

        def to_mate(k):
            return remote(mate_out, mate_in.at[lax.rem(k, 2)], msend, mrecv.at[k], net.cn)

        def complete(k):
            i = lax.rem(k, 2)
            to_mate(k).wait_send()
            landed(mate_in.at[i], mrecv.at[k])
            both = (branch[:, : 2 * HS] + mate_in[i, :, : 2 * HS].astype(f32)).astype(bf)
            pack[:, HS:] = jnp.concatenate([both, jnp.zeros((TOK, HS), bf)], axis=1)
            bias[pl.ds(zs(k), 1), :COLS] = column_sum(pack[...])
            gn[...] += dg(pack[...], w1[i], 1, 1)
            d1 = dg(xt[...], pack[:, :896], 1, 0)
            d2_ = dg(gt[...], att[i], 1, 0)
            dbuf[:, :AT0] = d1[:, :AT0].astype(bf)
            dbuf[:, AT0:896] = (d1[:, AT0:] + d2_[:, :128]).astype(bf)
            dbuf[:, 896:] = d2_[:, 128:].astype(bf)
            d_store(0, k).start()

        def chunk(k, _):
            i = lax.rem(k, 2)
            for cp in loads(k):
                cp.wait()
            ga = dg(gb[...], w1[i, :, AT0:], 1, 0).astype(bf)
            for j in range(4):
                a = j * HEAD_DIM
                gh[j] = ga[:, ATW - HS + a : ATW - HS + a + HEAD_DIM]
                qh[j] = act[i, :, a : a + HEAD_DIM]
                kh[j, :TOK] = act[i, :, HS + a : HS + a + HEAD_DIM]
                vh[j, :TOK] = act[i, :, 2 * HS + a : 2 * HS + a + HEAD_DIM]
                kh[j, TOK:] = kvo[:, HS - KV0 + a : HS - KV0 + a + HEAD_DIM]
                vh[j, TOK:] = kvo[:, 2 * HS - KV0 + a : 2 * HS - KV0 + a + HEAD_DIM]

            def head(j, _):
                kk, q, gg = kh[j], qh[j], gh[j]
                p = jnp.exp2(dg(kk, q, 1, 1) * (C * LOG2E) - lse[zs(k) * 4 + j])
                t = p * dg(vh[j], gg, 1, 1)
                inner = jnp.sum(t, axis=0, keepdims=True)
                ds = (t - p * inner).astype(bf)
                dv = dg(p.astype(bf), gg, 1, 0)
                dvh[j], dvm[j] = dv[:TOK], dv[TOK:].astype(bf)
                dk = dg(ds, q, 1, 0) * C
                dkh[j], dkm[j] = dk[:TOK], dk[TOK:].astype(bf)
                dqh[j] = (dg(kk, ds, 0, 0) * C).T.astype(bf)
                pl.when(jnp.logical_and(j == 1, k > 0))(lambda: complete(k - 1))

                @pl.when(jnp.logical_and(j == 1, k < 3))
                def _():
                    for cp in loads(k + 1):
                        cp.start()

                pl.when(jnp.logical_and(j == 2, k > 0))(lambda: d_store(0, k - 1).wait())
                flow.at(4 * k + j, HEADS)
                return 0

            lax.fori_loop(0, 4, head, 0)
            mate_out[...] = jnp.concatenate(
                [dkm[j] for j in range(4)] + [dvm[j] for j in range(4)] + [jnp.zeros((TOK, KVW - 2 * HS), bf)], axis=1,
            )
            to_mate(k).start()
            branch[:, : 2 * HS] = jnp.concatenate([dkh[j] for j in range(4)] + [dvh[j] for j in range(4)], axis=1)
            pack[:, :HS] = jnp.concatenate([dqh[j] for j in range(4)], axis=1)
            return 0

        lax.fori_loop(0, 4, chunk, 0)
        flow.do((Scatter.core, 10), (Scatter.bring, 9))
        complete(jnp.int32(3))
        flow.do((Scatter.far, 9), (Scatter.near, 8), (Scatter.line0, 8), (Scatter.last, 4), (Scatter.line2, 6), (Scatter.line2, 7))

    T = (4, TOK, HEAD_DIM)
    T2 = (4, 2 * TOK, HEAD_DIM)
    pl.run_scoped(
        attention, V((TOK, KVW), bf), V((2, TOK, ATW), bf), V(T, bf), V(T2, bf), V(T2, bf), V(T, bf), V(T, bf), V(T, f32), V(T, f32),
        V(T, bf), V(T, bf), V((TOK, KVW), bf),
    )

    def first_norm(r):
        n, s = normalize(tok[r].astype(f32))
        gr = gn[r]
        terms[0:1] += column_sum(gr)
        terms[1:2] += column_sum(gr * n)
        e = gr * (1.0 + scale_attn)
        gr = s * (e - jnp.mean(e, axis=-1, keepdims=True) - n * jnp.mean(e * n, axis=-1, keepdims=True))
        tok[r] = (br[r] + gr).astype(bf)

    by_rows(64, first_norm)
    token_back = Back(net, tok, token_rows, bsend.at[1], brecv.at[1])
    flow.token_back = token_back

    small = []

    def exchange(k, src, dst, dev):
        cp = remote(src, dst, small_send.at[k], small_recv.at[k], dev)
        cp.start()
        small.append(cp)

    def combine(k):
        bias[:, :COLS] += bias_in[k, :, :COLS]
        bias[:, COLS:] = jnp.maximum(bias[:, COLS:], bias_in[k, :, COLS:])

    peers = ((net.xn, 2 * y + 1 - x), (net.yn, 2 - 2 * y + x), (net.dn, 3 - plane))
    exchange(0, terms, terms_in, net.cn)
    four[0] = bias[...]
    exchange(1, four.at[0], bias_in.at[0], net.cn)
    d_store(0, jnp.int32(3)).wait()
    flow.begin(11)
    landed(terms_in, small_recv.at[0])
    image[plane, z] = (terms[...] + terms_in[...]).astype(bf).astype(f32)
    for k in range(3):
        exchange(2 + k, image.at[plane, z], image.at[plane, z], net.along_z(k + 1))
    landed(bias_in.at[0], small_recv.at[1])
    combine(0)
    four[1] = bias[...]
    for k in range(3):
        exchange(5 + k, four.at[1], bias_in.at[1 + k], net.along_z(k + 1))
    flow.do((Scatter.fetch, 11), (Scatter.near, 9), (Scatter.line0, 9), (Scatter.core, 11), (Scatter.bring, 10), (Scatter.far, 10), (Scatter.toks, 0), (Scatter.toks, 1))
    for k in range(3):
        landed(image.at[plane, lax.rem(z + 3 - k, 4)], small_recv.at[2 + k])
    for k, (dev, _) in enumerate(peers):
        exchange(8 + k, image.at[plane], image.at[plane], dev)
    flow.do((Scatter.bring, 11), (Scatter.far, 11), (Scatter.near, 10), (Scatter.line0, 10), (Scatter.line1, 8), (Scatter.toks, 2))
    for k, (_, p) in enumerate(peers):
        landed(image.at[p], small_recv.at[8 + k])
    every = [jnp.concatenate([image[p, q, i : i + 1] for p in range(4) for q in range(4)], axis=0) for i in range(6)]
    half = COLS // 2
    options = (
        (every[0], every[1][:, :half]), (every[1][:, half:], every[2]),
        (every[3], every[4][:, :half]), (every[4][:, half:], every[5]),
    )
    grad = sum(jnp.where(z == k, jnp.concatenate(o, axis=1), 0.0) for k, o in enumerate(options))
    low = grad.astype(bf)
    pgl[0] = dg(low, ada[...], 1, 1)
    for k in range(3):
        exchange(14 + k, pgl.at[0], pgl_in.at[k], net.along_z(k + 1))
    flow.do((Scatter.toks, 3), (Scatter.near, 11), (Scatter.line0, 11), (Scatter.toks, 4))
    ada_bias_grad[...] = column_sum(grad)
    ada_grad[...] = dg(lift_rows[...].astype(bf), low, 0, 0)
    for k in range(3):
        landed(bias_in.at[1 + k], small_recv.at[5 + k])
        combine(1 + k)
    four[2] = bias[...]
    for k, (dev, _) in enumerate(peers):
        exchange(11 + k, four.at[2], bias_in.at[4 + k], dev)
    flow.do((Scatter.line1, 9), (Scatter.toks, 5), (Scatter.line2, 8), (Scatter.line1, 10), (Scatter.toks, 6))
    for k in range(3):
        landed(pgl_in.at[k], small_recv.at[14 + k])
    lifted[plane, c] = pgl[0] + pgl_in[0] + pgl_in[1] + pgl_in[2]
    exchange(17, lifted.at[plane, c], lifted.at[plane, c], net.cn)
    flow.do((Scatter.line1, 11), (Scatter.line2, 9), (Scatter.toks, 7))
    landed(lifted.at[plane, 1 - c], small_recv.at[17])
    for k, (dev, _) in enumerate(peers):
        exchange(18 + k, lifted.at[plane], lifted.at[plane], dev)
    for k in range(3):
        landed(bias_in.at[4 + k], small_recv.at[11 + k])
        combine(4 + k)
    totals[...] = bias[...]
    flow.do((Scatter.last, 5), (Scatter.last, 6), (Scatter.last, 7), (Scatter.last, 8), (Scatter.line2, 10), (Scatter.last, 9), (Scatter.line2, 11), (Scatter.last, 10), (Scatter.last, 11))
    for k, (_, p) in enumerate(peers):
        landed(lifted.at[p], small_recv.at[18 + k])
    block_back.arrivals()
    token_back.arrivals()
    flow.finish()
    for cp in small:
        cp.wait_send()
    block_back.sent()
    token_back.sent()


def backward(*args):
    B = (ROWS, COLS)
    wide, rows = (TOK, COLS), (2, 256, COLS)
    pair = D((2,))
    return pl.pallas_call(
        backward_kernel,
        name="backward",
        out_shape=(
            S((3,) + B, f32), S(rows, bf), S(rows, bf), S((2, 8 * ROWS, 4 * COLS), bf), S((12, 2, 2) + B, bf), S((12, 2) + B, bf),
            S((ROWS, ADA), f32), S((1, ADA), f32), S((4, 2, 16, ROWS), f32), S((16, COLS + 128), f32),
        ),
        in_specs=[HB] * 8 + [VM, VM] + [HB] * 4 + [VM] * 4,
        out_specs=(HB,) * 6 + (VM,) * 4,
        scratch_shapes=[
            V(wide, bf), V(wide, bf), V(wide, f32), V(wide, f32), V(wide, f32), V(wide, bf), V(wide, bf), V((COLS, TOK), bf), V((COLS, TOK), bf),
            V((2, COLS, COLS), bf), V((2, TOK, COLS), bf), V((COLS, COLS), bf),
            V((12,) + B, bf), V((12,) + B, bf), V((3,) + B, bf), V((4, 2, 2) + B, bf), V((2, 2) + B, bf), V((2,) + B, bf), V((2, TOK, KVW), bf),
            V(B, f32), V((16, COLS + 128), f32), V((7, 16, COLS + 128), f32), V((8, COLS), f32), V((8, COLS), f32), V((4, 4, 8, COLS), f32),
            V((1, 16, ROWS), f32), V((3, 16, ROWS), f32), V((3, 16, COLS + 128), f32),
            D, D((12, 2, 2)), D((12, 2, 2)), D((2, 2)), D((2, 2)), D((12, 2)), D((12, 2)), pair, D((12,)), D((12,)), D((12,)), D((12,)), D((3,)),
            D((2, 2)), D((2, 2)), D((4,)), pair, pair, pair, pair, D, D, D((4,)), D((2, 2)), D((21,)), D((21,)),
        ],
        compiler_params=pltpu.CompilerParams(collective_id=2, has_side_effects=True, vmem_limit_bytes=62 * 2**20),
    )(*args)


def modulate_images(values, shift, scale):
    average = jnp.mean(values, axis=-1, keepdims=True)
    centred = values - average
    spread = jnp.mean(centred * centred, axis=-1, keepdims=True)
    return centred * lax.rsqrt(spread + epsilon) * (1.0 + scale[:, None, :]) + shift[:, None, :]


def product(left, right):
    return jnp.dot(left, right, preferred_element_type=jnp.float32)


def inner_rows(left, right):
    return lax.dot_general(
        left, right, (((0,), (0,)), ((), ())), preferred_element_type=jnp.float32
    )


def against(left, right):
    return lax.dot_general(
        left, right, (((1,), (1,)), ((), ())), preferred_element_type=jnp.float32
    )


def spread_rows(values):
    return lax.all_gather(values, "tensor", axis=1, tiled=True)


def fold_rows(values):
    return lax.psum_scatter(values, "tensor", scatter_dimension=1, tiled=True)


def spread_grads(values):
    return lax.all_gather(values, "tensor", axis=1, tiled=True)


def fold_grads(values):
    return lax.psum_scatter(values, "tensor", scatter_dimension=1, tiled=True)


def local(
    tokens,
    conditioning,
    cotangent,
    query_weight,
    key_weight,
    value_weight,
    out_weight,
    up_weight,
    down_weight,
    ada_weight,
    query_bias,
    value_bias,
    out_bias,
    up_bias,
    down_bias,
    ada_bias,
    threshold,
):
    images = tokens.shape[0]
    model_width = tokens.shape[2]
    gathered = (
        lax.all_gather(query_weight, "dp", axis=0, tiled=True),
        lax.all_gather(key_weight, "dp", axis=0, tiled=True),
        lax.all_gather(value_weight, "dp", axis=0, tiled=True),
        lax.all_gather(out_weight, "dp", axis=1, tiled=True),
        lax.all_gather(up_weight, "dp", axis=0, tiled=True),
        lax.all_gather(down_weight, "dp", axis=1, tiled=True),
        lax.all_gather(ada_weight, "dp", axis=0, tiled=True),
    )
    full_query, full_key, full_value, full_out, full_up, full_down, full_ada = gathered
    lifted_low = jax.nn.silu(conditioning).astype(jnp.bfloat16)
    own_columns = product(lifted_low, full_ada) + ada_bias
    modulation = lax.all_gather(own_columns, "tensor", axis=1, tiled=True)
    pieces = [
        modulation[:, piece_index * model_width : (piece_index + 1) * model_width]
        for piece_index in range(6)
    ]
    shift_attn, scale_attn, gate_attn, shift_mlp, scale_mlp, gate_mlp = pieces
    inputs = tokens.astype(jnp.float32)
    normed_attn = spread_rows(modulate_images(inputs, shift_attn, scale_attn).astype(jnp.bfloat16))
    length = normed_attn.shape[1]
    row_count = images * length
    flat_attn = normed_attn.reshape(row_count, model_width)
    local_width = full_query.shape[1]
    heads_here = local_width // HEAD_DIM
    queries = (product(flat_attn, full_query) + query_bias).astype(jnp.bfloat16)
    key_rows = product(flat_attn, full_key).astype(jnp.bfloat16)
    value_rows = (product(flat_attn, full_value) + value_bias).astype(jnp.bfloat16)
    block_rows = min(512, length)
    head_scale = HEAD_DIM ** (-0.5)

    def by_head(matrix):
        return matrix.reshape(images, length, heads_here, HEAD_DIM)

    def attend_image(bundle):
        queries_img, keys_img, values_img = bundle
        outputs, totals, highest = ([], [], [])
        for offset in range(0, length, block_rows):
            logits = (
                jnp.einsum(
                    "qhe,khe->hqk",
                    queries_img[offset : offset + block_rows],
                    keys_img,
                    preferred_element_type=jnp.float32,
                )
                * head_scale
            )
            row_top = jnp.max(logits, axis=2, keepdims=True)
            raised = jnp.exp(logits - row_top)
            summed = jnp.sum(raised, axis=2, keepdims=True)
            shares = (raised / summed).astype(jnp.bfloat16)
            outputs.append(
                jnp.einsum(
                    "hqk,khe->qhe", shares, values_img, preferred_element_type=jnp.float32
                ).astype(jnp.bfloat16)
            )
            totals.append(row_top[:, :, 0] + jnp.log(summed[:, :, 0]))
            highest.append(jnp.max(row_top[:, :, 0], axis=1))
        return (
            jnp.concatenate(outputs, 0),
            jnp.concatenate(totals, 1),
            jnp.max(jnp.stack(highest), axis=0),
        )

    attended, log_totals, image_peaks = lax.map(
        attend_image, (by_head(queries), by_head(key_rows), by_head(value_rows))
    )
    flat_attended = attended.reshape(row_count, local_width)
    branch_attn = (
        fold_rows(product(flat_attended, full_out).reshape(images, length, model_width)) + out_bias
    )
    after_attn = inputs + gate_attn[:, None, :] * branch_attn
    normed_mlp = spread_rows(modulate_images(after_attn, shift_mlp, scale_mlp).astype(jnp.bfloat16))
    flat_mlp = normed_mlp.reshape(row_count, model_width)
    upward = product(flat_mlp, full_up) + up_bias
    active = jax.nn.gelu(upward, approximate=True).astype(jnp.bfloat16)
    branch_mlp = (
        fold_rows(product(active, full_down).reshape(images, length, model_width)) + down_bias
    )
    block_out = (after_attn + gate_mlp[:, None, :] * branch_mlp).astype(jnp.bfloat16)
    peaks = lax.pmax(jnp.max(image_peaks, axis=0), "dp")
    again = (
        lax.all_gather(query_weight, "dp", axis=0, tiled=True),
        lax.all_gather(key_weight, "dp", axis=0, tiled=True),
        lax.all_gather(value_weight, "dp", axis=0, tiled=True),
        lax.all_gather(out_weight, "dp", axis=1, tiled=True),
        lax.all_gather(up_weight, "dp", axis=0, tiled=True),
        lax.all_gather(down_weight, "dp", axis=1, tiled=True),
        lax.all_gather(ada_weight, "dp", axis=0, tiled=True),
    )
    back_query, back_key, back_value, back_out, back_up, back_down, back_ada = again
    grad_out = cotangent.astype(jnp.float32)
    grad_branch_mlp = (gate_mlp[:, None, :] * grad_out).astype(jnp.bfloat16)
    grad_gate_mlp = jnp.sum(grad_out * branch_mlp, axis=1)
    flat_grad_mlp = spread_grads(grad_branch_mlp).reshape(row_count, model_width)
    grad_down_bias = jnp.sum(flat_grad_mlp, axis=0, dtype=jnp.float32)
    grad_down_weight = inner_rows(active, flat_grad_mlp)
    grad_active = against(flat_grad_mlp, back_down)
    _, gelu_pull = jax.vjp(partial(jax.nn.gelu, approximate=True), upward)
    grad_upward = gelu_pull(grad_active)[0].astype(jnp.bfloat16)
    grad_up_bias = jnp.sum(grad_upward, axis=0, dtype=jnp.float32)
    grad_up_weight = inner_rows(flat_mlp, grad_upward)
    grad_normed_mlp = fold_grads(against(grad_upward, back_up).reshape(images, length, model_width))
    _, mlp_pull = jax.vjp(modulate_images, after_attn, shift_mlp, scale_mlp)
    grad_after, grad_shift_mlp, grad_scale_mlp = mlp_pull(grad_normed_mlp)
    grad_after = grad_out + grad_after
    grad_branch_attn = (gate_attn[:, None, :] * grad_after).astype(jnp.bfloat16)
    grad_gate_attn = jnp.sum(grad_after * branch_attn, axis=1)
    flat_grad_attn = spread_grads(grad_branch_attn).reshape(row_count, model_width)
    grad_out_bias = jnp.sum(flat_grad_attn, axis=0, dtype=jnp.float32)
    grad_out_weight = inner_rows(flat_attended, flat_grad_attn)
    grad_attended = against(flat_grad_attn, back_out).astype(jnp.bfloat16)

    def attend_back(bundle):
        queries_img, keys_img, values_img, grads_img, totals_img = bundle
        query_parts = []
        grad_keys_img = jnp.zeros(keys_img.shape, jnp.float32)
        grad_values_img = jnp.zeros(values_img.shape, jnp.float32)
        for offset in range(0, length, block_rows):
            query_block = queries_img[offset : offset + block_rows]
            grad_block = grads_img[offset : offset + block_rows]
            logits = (
                jnp.einsum(
                    "qhe,khe->hqk", query_block, keys_img, preferred_element_type=jnp.float32
                )
                * head_scale
            )
            shares = jnp.exp(logits - totals_img[:, offset : offset + block_rows, None])
            grad_shares = jnp.einsum(
                "qhe,khe->hqk", grad_block, values_img, preferred_element_type=jnp.float32
            )
            row_inner = jnp.sum(shares * grad_shares, axis=2, keepdims=True)
            grad_logits = (shares * (grad_shares - row_inner)).astype(jnp.bfloat16)
            query_parts.append(
                (
                    jnp.einsum(
                        "hqk,khe->qhe", grad_logits, keys_img, preferred_element_type=jnp.float32
                    )
                    * head_scale
                ).astype(jnp.bfloat16)
            )
            grad_keys_img = (
                grad_keys_img
                + jnp.einsum(
                    "hqk,qhe->khe", grad_logits, query_block, preferred_element_type=jnp.float32
                )
                * head_scale
            )
            grad_values_img = grad_values_img + jnp.einsum(
                "hqk,qhe->khe",
                shares.astype(jnp.bfloat16),
                grad_block,
                preferred_element_type=jnp.float32,
            )
        return (
            jnp.concatenate(query_parts, 0),
            grad_keys_img.astype(jnp.bfloat16),
            grad_values_img.astype(jnp.bfloat16),
        )

    grad_queries, grad_keys, grad_values = lax.map(
        attend_back,
        (
            by_head(queries),
            by_head(key_rows),
            by_head(value_rows),
            by_head(grad_attended),
            log_totals,
        ),
    )
    grad_queries = grad_queries.reshape(row_count, local_width)
    grad_keys = grad_keys.reshape(row_count, local_width)
    grad_values = grad_values.reshape(row_count, local_width)
    grad_query_bias = jnp.sum(grad_queries, axis=0, dtype=jnp.float32)
    grad_value_bias = jnp.sum(grad_values, axis=0, dtype=jnp.float32)
    grad_query_weight = inner_rows(flat_attn, grad_queries)
    grad_key_weight = inner_rows(flat_attn, grad_keys)
    grad_value_weight = inner_rows(flat_attn, grad_values)
    partial_normed = (
        against(grad_queries, back_query)
        + against(grad_keys, back_key)
        + against(grad_values, back_value)
    )
    grad_normed_attn = fold_grads(partial_normed.reshape(images, length, model_width))
    _, attn_pull = jax.vjp(modulate_images, inputs, shift_attn, scale_attn)
    grad_inputs, grad_shift_attn, grad_scale_attn = attn_pull(grad_normed_attn)
    grad_tokens = grad_after + grad_inputs
    modulation_terms = jnp.concatenate(
        [
            grad_shift_attn,
            grad_scale_attn,
            grad_gate_attn,
            grad_shift_mlp,
            grad_scale_mlp,
            grad_gate_mlp,
        ],
        axis=1,
    )
    grad_modulation = lax.psum_scatter(
        modulation_terms, "tensor", scatter_dimension=1, tiled=True
    ).astype(jnp.bfloat16)
    grad_ada_bias = jnp.sum(grad_modulation, axis=0, dtype=jnp.float32)
    grad_ada_weight = inner_rows(lifted_low, grad_modulation)
    grad_lifted = lax.psum(against(grad_modulation, back_ada), "tensor")
    _, silu_pull = jax.vjp(jax.nn.silu, conditioning)
    grad_conditioning = silu_pull(grad_lifted)[0]
    weight_grads = (
        lax.psum_scatter(grad_query_weight, "dp", scatter_dimension=0, tiled=True),
        lax.psum_scatter(grad_key_weight, "dp", scatter_dimension=0, tiled=True),
        lax.psum_scatter(grad_value_weight, "dp", scatter_dimension=0, tiled=True),
        lax.psum_scatter(grad_out_weight, "dp", scatter_dimension=1, tiled=True),
        lax.psum_scatter(grad_up_weight, "dp", scatter_dimension=0, tiled=True),
        lax.psum_scatter(grad_down_weight, "dp", scatter_dimension=1, tiled=True),
        lax.psum_scatter(grad_ada_weight, "dp", scatter_dimension=0, tiled=True),
    )
    bias_grads = lax.psum(
        (
            grad_query_bias,
            grad_value_bias,
            grad_out_bias,
            grad_up_bias,
            grad_down_bias,
            grad_ada_bias,
        ),
        "dp",
    )
    limit = threshold[0]
    factor = jnp.sqrt(limit / jnp.maximum(peaks, limit))
    column_factor = jnp.repeat(factor, HEAD_DIM)
    query_clipped = (query_weight.astype(jnp.float32) * column_factor).astype(jnp.bfloat16)
    key_clipped = (key_weight.astype(jnp.float32) * column_factor).astype(jnp.bfloat16)
    query_bias_clipped = query_bias * column_factor
    return (
        block_out,
        grad_tokens,
        grad_conditioning,
        weight_grads[0],
        weight_grads[1],
        weight_grads[2],
        weight_grads[3],
        weight_grads[4],
        weight_grads[5],
        weight_grads[6],
        bias_grads[0],
        bias_grads[1],
        bias_grads[2],
        bias_grads[3],
        bias_grads[4],
        bias_grads[5],
        query_clipped,
        key_clipped,
        query_bias_clipped,
    )


def one_image_per_chip(
    tokens, conditioning, cotangent, query_weight, key_weight, value_weight, out_weight, up_weight,
    down_weight, ada_weight, query_bias, value_bias, out_bias, up_bias, down_bias, ada_bias, threshold,
):
    y, x, c, z = (lax.axis_index(a) for a in AXES)
    batch = 4 * y + 2 * x + c
    first = jnp.concatenate([query_weight, key_weight, value_weight, out_weight.T], axis=1)
    shard = jnp.stack([first, up_weight, down_weight.T])
    lift_own = jnp.pad(jax.nn.silu(conditioning).astype(bf).astype(f32), ((0, 6), (0, 0)))
    z_bias = jnp.concatenate([query_bias, value_bias, up_bias])[None]
    (
        full, own_tokens, own_cotangent, lifted_rows, vectors, biases, normed_attn, qkv, mate_kv, attended, totals,
        peak, branch_attn, normed_mlp, active, slope, grad_down,
    ) = forward(shard, tokens, cotangent, lift_own, ada_weight, ada_bias[None], z_bias, out_bias[None])
    sums, block_rows, token_rows, _, _, _, grad_ada_weight, grad_ada_bias, lifted, totals = backward(
        full, own_tokens, own_cotangent, normed_attn, normed_mlp, qkv, mate_kv, attended, totals, peak, branch_attn,
        active, slope, grad_down, vectors, lifted_rows, ada_weight, down_bias[None],
    )
    own_lifted = lax.dynamic_slice(lifted.reshape(8, 16, ROWS), (0, 2 * batch, 0), (8, 2, ROWS))
    own_lifted = jnp.swapaxes(own_lifted, 0, 1).reshape(2, 8 * ROWS)
    _, silu_pull = jax.vjp(jax.nn.silu, conditioning)
    grad_conditioning = silu_pull(own_lifted)[0]
    first_bias = lax.dynamic_slice(totals, (z, 0), (1, COLS))[0]
    grad_query_bias = first_bias[:HS]
    grad_value_bias = first_bias[2 * HS : 3 * HS]
    grad_up_bias = lax.dynamic_slice(totals, (4 + z, 0), (1, COLS))[0]
    grad_out_bias = totals[8, :COLS]
    grad_down_bias = totals[9, :COLS]
    grad_ada_bias = grad_ada_bias[0]
    limit = threshold[0]
    peaks = lax.dynamic_slice(totals[:, COLS], (4 * z,), (4,))
    factor = jnp.sqrt(limit / jnp.maximum(peaks, limit))
    column_factor = jnp.repeat(factor, HEAD_DIM)
    query_clipped = (query_weight.astype(f32) * column_factor).astype(bf)
    key_clipped = (key_weight.astype(f32) * column_factor).astype(bf)
    return (
        block_rows,
        token_rows.astype(f32),
        grad_conditioning,
        sums[0, :, :HS],
        sums[0, :, HS : 2 * HS],
        sums[0, :, 2 * HS : 3 * HS],
        sums[0, :, 3 * HS :].T,
        sums[1],
        sums[2].T,
        grad_ada_weight,
        grad_query_bias,
        grad_value_bias,
        grad_out_bias,
        grad_up_bias,
        grad_down_bias,
        grad_ada_bias,
        query_clipped,
        key_clipped,
        query_bias * column_factor,
    )


def solution(mesh):
    if dict(mesh.shape) == {"dp": 8, "tensor": 4}:
        mesh = Mesh(mesh.devices.reshape(2, 2, 2, 4), AXES)
        split, heads, body = ("y", "x", "core"), "z", one_image_per_chip
    else:
        split, heads, body = "dp", "tensor", local
    weight, turned, bias = P(split, heads), P(heads, split), P(heads)
    rows = P(split, heads, None)
    in_specs = (
        rows, P(split, None), rows, weight, weight, weight, turned, weight, turned, weight,
        bias, bias, P(), bias, P(), bias, P(),
    )
    out_specs = (
        rows, rows, P(split, None), weight, weight, weight, turned, weight, turned, weight,
        bias, bias, P(), bias, P(), bias, weight, weight, bias,
    )
    return jax.shard_map(body, mesh=mesh, in_specs=in_specs, out_specs=out_specs, check_vma=False)
```

```python
from functools import partial

import jax
import jax.numpy as jnp
from jax import lax
from jax.experimental import pallas as pl
from jax.experimental.pallas import tpu as pltpu
from jax.sharding import Mesh, PartitionSpec as P

HEAD_DIM=72
epsilon=1e-06
MESH = pl.DeviceIdType.MESH
AXES = ("y", "x", "core", "z")
ROWS, COLS, TOK = 144, 1152, 512
HS, KV0, KVW, AT0, ATW, ADA = 288, 256, 640, 768, 384, 1728
C = HEAD_DIM**-0.5
LOG2E = 1.4426950408889634
bf = jnp.bfloat16
f32 = jnp.float32
VM = pl.BlockSpec(memory_space=pltpu.VMEM)
HB = pl.BlockSpec(memory_space=pl.ANY)
S = jax.ShapeDtypeStruct
D = pltpu.SemaphoreType.DMA
V = pltpu.VMEM


def dg(a, b, ca, cb):
    return lax.dot_general(a, b, (((ca,), (cb,)), ((), ())), preferred_element_type=f32)


class Net:
    def __init__(self):
        self.y, self.x, self.c, self.z = (lax.axis_index(a) for a in AXES)
        y, x, c, z = self.y, self.x, self.c, self.z
        self.up, self.down = lax.rem(z + 1, 4), lax.rem(z + 3, 4)
        self.xn, self.yn, self.dn = (y, 1 - x, c, z), (1 - y, x, c, z), (1 - y, 1 - x, c, z)
        self.cn = (y, x, 1 - c, z)
        self.zpn, self.zmn = (y, x, c, self.up), (y, x, c, self.down)
        self.f, self.n = self.place(y, x)
        self.far = self.device(1 - self.f, self.n)
        self.near = self.device(self.f, 1 - self.n)

    def place(self, a, b):
        return (1 - self.c) * a + self.c * b, (1 - self.c) * b + self.c * a

    def device(self, f, n):
        y, x = self.place(f, n)
        return (y, x, self.c, self.z)

    def along_z(self, step):
        return (self.y, self.x, self.c, lax.rem(self.z + step, 4))

    def greet(self):
        bar = pltpu.get_barrier_semaphore()
        others = [self.xn, self.yn, self.dn]
        for dc in range(2):
            for dz in range(4):
                if dc or dz:
                    others.append((self.y, self.x, lax.rem(self.c + dc, 2), lax.rem(self.z + dz, 4)))
        for o in others:
            pl.semaphore_signal(bar, inc=1, device_id=o, device_id_type=MESH)
        pl.semaphore_wait(bar, len(others))


def remote(src, dst, send, recv, device):
    return pltpu.make_async_remote_copy(
        src_ref=src, dst_ref=dst, send_sem=send, recv_sem=recv, device_id=device, device_id_type=MESH
    )


def landed(ref, sem):
    pltpu.make_async_copy(ref, ref, sem).wait()


def gelu_pair(u):
    k = 0.7978845608028654
    u2 = u * u
    t = jnp.tanh(k * u * (1.0 + 0.044715 * u2))
    h = 0.5 * (1.0 + t)
    return u * h, h + 0.5 * u * (1.0 - t * t) * (k * (1.0 + 3.0 * 0.044715 * u2))


class Gather:
    def __init__(self, net, g, shard, send, zsend, recv):
        self.net, self.g, self.shard, self.send, self.zsend, self.recv = net, g, shard, send, zsend, recv

    def slot(self, t, f, n, c, z):
        y, x = self.net.place(f, n)
        row = pl.multiple_of((4 * y + 2 * x + c) * ROWS, 16)
        return self.g.at[t, pl.ds(row, ROWS), pl.ds(pl.multiple_of(z * COLS, 128), COLS)]

    def sem(self, t, f, n, c, z):
        y, x = self.net.place(f, n)
        return self.recv.at[t, 4 * y + 2 * x + c, z]

    def put(self, u, k, device, f, n, z, own=False):
        t = lax.div(u, 4)
        s = self.slot(t, f, n, self.net.c, z)
        return remote(self.shard.at[t] if own else s, s, self.send.at[u, k], self.sem(t, f, n, self.net.c, z), device)

    def arrived(self, t, f, n, c, z):
        landed(self.slot(t, f, n, c, z), self.sem(t, f, n, c, z))

    def nth(self, k):
        z = self.net.z
        after = ((0, 1, 2, 3), (1, 0, 2, 3), (2, 3, 1, 0), (3, 2, 1, 0))
        return sum(
            jnp.where(jnp.logical_and(z == i, k == j), after[i][j], 0)
            for i in range(4) for j in range(4)
        )

    def onward(self, t, k, zz, act, own=False):
        net = self.net
        s = self.slot(t, net.f, net.n, net.c, zz)
        src = self.shard.at[t] if own else s
        sem = self.sem(t, net.f, net.n, net.c, zz)
        up = jnp.logical_and(zz <= net.z, net.z < 3)
        down = jnp.logical_and(zz >= net.z, net.z > 0)

        @pl.when(up)
        def _():
            act(remote(src, s, self.zsend.at[t, k, 0], sem, net.zpn))

        @pl.when(down)
        def _():
            act(remote(src, s, self.zsend.at[t, k, 1], sem, net.zmn))

    def copies(self, u, own=False):
        net = self.net
        zz = net.z if own else self.nth(lax.rem(u, 4))
        f, n = net.f, net.n
        return (
            [self.put(u, 0, net.near, f, n, zz, own), self.put(u, 1, net.far, f, n, zz, own), self.put(u, 2, net.cn, f, n, zz, own)],
            [self.put(u, 3, net.far, f, 1 - n, zz), self.put(u, 4, net.cn, f, 1 - n, zz), self.put(u, 5, net.cn, 1 - f, n, zz)],
            [self.put(u, 6, net.cn, 1 - f, 1 - n, zz)],
        )

    def line(self, u):
        t, k = lax.div(u, 4), lax.rem(u, 4)
        pl.when(k == 0)(lambda: self.onward(t, k, self.net.z, lambda cp: cp.start(), True))

        @pl.when(k > 0)
        def _():
            zz = self.nth(k)
            self.arrived(t, self.net.f, self.net.n, self.net.c, zz)
            self.onward(t, k, zz, lambda cp: cp.start())

    def tok(self, p):
        self.token_rows.piece(p)

    def cot(self, p):
        self.cot_rows.piece(p)

    def mid(self, u):
        pl.when(jnp.logical_and(self.net.z > 0, self.net.z < 3))(lambda: self.line(u))

    def end(self, u):
        pl.when(lax.rem(self.net.z, 3) == 0)(lambda: self.line(u))

    def spread(self, u):
        k = lax.rem(u, 4)

        @pl.when(k == 0)
        def _():
            for cp in self.copies(u, True)[0]:
                cp.start()

        @pl.when(k > 0)
        def _():
            for cp in self.copies(u)[0]:
                cp.start()

    def across(self, u):
        net, t = self.net, lax.div(u, 4)
        zz = self.nth(lax.rem(u, 4))
        a, b, d = self.copies(u)[1]
        self.arrived(t, net.f, 1 - net.n, net.c, zz)
        a.start()
        b.start()
        self.arrived(t, 1 - net.f, net.n, net.c, zz)
        d.start()

    def corner(self, u):
        net, t = self.net, lax.div(u, 4)
        self.arrived(t, 1 - net.f, 1 - net.n, net.c, self.nth(lax.rem(u, 4)))
        self.copies(u)[2][0].start()

    def do(self, *steps):
        for step, u in steps:
            step(self, u if step in (Gather.tok, Gather.cot) else jnp.int32(u))

    def at(self, point, table):
        for p, steps in enumerate(table):
            if steps:
                pl.when(point == p)(lambda: self.do(*steps))

    def from_mate(self, t):
        def one(i, _):
            self.arrived(t, lax.div(i, 8), lax.rem(lax.div(i, 4), 2), 1 - self.net.c, lax.rem(i, 4))
            return 0

        lax.fori_loop(0, 16, one, 0)

    def finish(self):
        def one(u, _):
            for group in self.copies(u):
                for cp in group:
                    cp.wait_send()
            t, k = lax.div(u, 4), lax.rem(u, 4)
            self.onward(t, k, self.nth(k), lambda cp: cp.wait_send())
            return 0

        lax.fori_loop(0, 12, one, 0)


def rows_out(net, i):
    dc, dz = lax.div(net.z, 2), 2 * net.c + i
    here = jnp.logical_and(dc == net.c, dz == net.z)
    return (net.y, net.x, dc, dz), pl.multiple_of(lax.rem(net.z, 2) * 256, 256), here


class Rows:
    def __init__(self, net, src, dst, send, recv):
        self.net, self.src, self.dst, self.send, self.recv = net, src, dst, send, recv

    def local(self):
        for i in range(2):
            _, row, here = rows_out(self.net, i)

            @pl.when(here)
            def _():
                self.dst[pl.ds(row, 256)] = self.src[i]

    def copy(self, i, first, count):
        device, row, here = rows_out(self.net, i)
        return remote(
            self.src.at[i, pl.ds(first, count)], self.dst.at[pl.ds(row + first, count)],
            self.send.at[i], self.recv.at[lax.rem(self.net.z, 2)], device,
        ), jnp.logical_not(here)

    def piece(self, p):
        cp, cond = self.copy(p % 2, p // 2 * 64, 64)
        pl.when(cond)(cp.start)

    def sent(self):
        for i in range(2):
            cp, cond = self.copy(i, 0, 256)
            pl.when(cond)(cp.wait_send)

    def arrivals(self):
        net = self.net
        for k in range(2):
            here = jnp.logical_and(lax.div(net.z, 2) == net.c, 2 * net.c + k == net.z)
            pl.when(jnp.logical_not(here))(lambda: landed(self.dst.at[pl.ds(k * 256, 256)], self.recv.at[k]))


def normalize(v):
    mean = jnp.mean(v, axis=-1, keepdims=True)
    centred = v - mean
    r = lax.rsqrt(jnp.mean(centred * centred, axis=-1, keepdims=True) + epsilon)
    return centred * r, r


def by_rows(step, body):
    def one(i, _):
        body(pl.ds(pl.multiple_of(i * step, step), step))
        return 0

    lax.fori_loop(0, TOK // step, one, 0)


TABLE = (
    ((Gather.across, 5),),
    ((Gather.end, 7), (Gather.spread, 7)),
    ((Gather.mid, 9), (Gather.mid, 10), (Gather.corner, 8)),
    ((Gather.across, 6), (Gather.end, 9), (Gather.spread, 9)),
    ((Gather.mid, 11), (Gather.corner, 5)),
    ((Gather.across, 7), (Gather.end, 10), (Gather.spread, 10), (Gather.cot, 0), (Gather.cot, 1)),
    ((Gather.end, 11), (Gather.spread, 11), (Gather.corner, 6), (Gather.cot, 2)),
    ((Gather.across, 9), (Gather.cot, 3)),
    ((Gather.across, 10), (Gather.cot, 4), (Gather.cot, 5)),
    ((Gather.cot, 6),),
    ((Gather.across, 11), (Gather.corner, 9), (Gather.cot, 7)),
    (),
    ((Gather.corner, 10),),
    (),
    ((Gather.corner, 11),),
)


def forward_kernel(
    shard, tokens, cotangent, lift_own, ada, ada_bias, z_bias, out_bias,
    g, tok, cot, lift_rows, vectors, biases, x_out, qkv_out, kvo_out, att_out, lse, peak, branch_out, nm_out, act_out, gd_out, d2,
    tok_v, cot_v, lift, part, part_in, four, four_in, zall, x_ref, w, qkv, kvo, att, branch, qh, kh, vh, oh, gbt, act_buf, gd_buf, dbuf,
    gsend, gzsend, grecv, lsem, rsend, rrecv, small_send, small_recv, wsem, ksend, krecv, osem, asem, gdsem, dsem,
):
    net = Net()
    y, x, c, z = net.y, net.x, net.c, net.z
    plane = 2 * y + x
    net.greet()
    flow = Gather(net, g, shard, gsend, gzsend, grecv)
    lift[plane, c] = lift_own[...]
    small = [remote(lift.at[plane, c], lift.at[plane, c], small_send.at[0], small_recv.at[0], net.cn)]
    small[0].start()
    token_rows = Rows(net, tokens, tok_v, rsend.at[0], rrecv.at[0])
    cot_rows = Rows(net, cotangent, cot_v, rsend.at[1], rrecv.at[1])
    flow.token_rows, flow.cot_rows = token_rows, cot_rows
    flow.do((Gather.line, 0))
    own = [pltpu.make_async_copy(shard.at[t], flow.slot(t, net.f, net.n, c, z), lsem.at[t]) for t in range(3)]
    for cp in own:
        cp.start()

    landed(lift.at[plane, 1 - c], small_recv.at[0])
    peers = ((net.xn, 2 * y + 1 - x), (net.yn, 2 - 2 * y + x), (net.dn, 3 - plane))
    for k, (dev, _) in enumerate(peers):
        cp = remote(lift.at[plane], lift.at[plane], small_send.at[1 + k], small_recv.at[1 + k], dev)
        cp.start()
        small.append(cp)
    flow.do((Gather.spread, 0), (Gather.spread, 4), (Gather.line, 1))
    for k, (_, p) in enumerate(peers):
        landed(lift.at[p], small_recv.at[1 + k])
    every = jnp.concatenate([lift[p, k, 0:2] for p in range(4) for k in range(2)], axis=0).astype(bf)
    batch = 4 * y + 2 * x + c
    pick = lax.broadcasted_iota(jnp.int32, (COLS, ROWS), 0) == lax.broadcasted_iota(jnp.int32, (COLS, ROWS), 1) + batch * ROWS
    rows = dg(every, jnp.where(pick, 1.0, 0.0).astype(bf), 1, 0)
    lift_rows[...] = rows
    partial = dg(rows.astype(bf), ada[...], 1, 0)
    part[...] = jnp.zeros_like(part)
    for p in range(4):
        part[p, 0:4] = partial[4 * p : 4 * p + 4]
    for k, (dev, p) in enumerate(peers):
        cp = remote(part.at[p], part_in.at[k], small_send.at[4 + k], small_recv.at[4 + k], dev)
        cp.start()
        small.append(cp)
    flow.do((Gather.spread, 1), (Gather.line, 2), (Gather.across, 0), (Gather.spread, 2), (Gather.line, 3), (Gather.spread, 3))
    for k in range(3):
        landed(part_in.at[k], small_recv.at[4 + k])
    four[...] = part[plane] + part_in[0] + part_in[1] + part_in[2]
    cp = remote(four, four_in, small_send.at[7], small_recv.at[7], net.cn)
    cp.start()
    small.append(cp)
    landed(four_in, small_recv.at[7])
    zall[z] = four[...] + four_in[...] + ada_bias[...]
    zall[z, 4:5] = z_bias[...]
    for k in range(3):
        cp = remote(zall.at[z], zall.at[z], small_send.at[8 + k], small_recv.at[8 + k], net.along_z(k + 1))
        cp.start()
        small.append(cp)
    flow.do(
        (Gather.across, 4), (Gather.tok, 0), (Gather.tok, 1), (Gather.across, 1), (Gather.tok, 2), (Gather.tok, 3), (Gather.across, 2), (Gather.tok, 4), (Gather.tok, 5),
        (Gather.across, 3), (Gather.spread, 8), (Gather.tok, 6), (Gather.tok, 7), (Gather.line, 4),
    )
    token_rows.local()
    cot_rows.local()
    for k in range(3):
        landed(zall.at[lax.rem(z + 3 - k, 4)], small_recv.at[8 + k])
    pieces = [zall[k, pl.ds(z, 1)] for k in range(4)]
    half = COLS // 2
    vectors[0:1] = pieces[0][:, :COLS]
    vectors[1:2] = jnp.concatenate([pieces[0][:, COLS:], pieces[1][:, :half]], axis=1)
    vectors[2:3] = pieces[1][:, half:]
    vectors[3:4] = pieces[2][:, :COLS]
    vectors[4:5] = jnp.concatenate([pieces[2][:, COLS:], pieces[3][:, :half]], axis=1)
    vectors[5:6] = pieces[3][:, half:]
    vectors[6:8] = jnp.zeros((2, COLS), f32)
    nothing = jnp.zeros((1, HS), f32)
    for k in range(4):
        b = zall[k, 4:5]
        biases[k, 0:1] = jnp.concatenate([b[:, :HS], nothing, b[:, HS : 2 * HS], nothing], axis=1)
        biases[k, 1:2] = b[:, 2 * HS :]

    flow.do((Gather.corner, 0), (Gather.corner, 4), (Gather.corner, 1), (Gather.corner, 2))
    token_rows.arrivals()

    def first_norm(r):
        n, _ = normalize(tok_v[r].astype(f32))
        x_ref[r] = (n * (1.0 + vectors[1:2]) + vectors[0:1]).astype(bf)

    by_rows(64, first_norm)
    outs = [pltpu.make_async_copy(x_ref, x_out, osem.at[1]), pltpu.make_async_copy(tok_v, tok, osem.at[0])]
    for cp in outs:
        cp.start()
    flow.do((Gather.line, 5), (Gather.spread, 5), (Gather.mid, 6), (Gather.corner, 3))
    flow.from_mate(0)

    def load_w(t, k):
        return pltpu.make_async_copy(g.at[t, :, pl.ds(k * COLS, COLS)], w.at[k], wsem.at[k])

    own[0].wait()
    for k in range(4):
        load_w(0, k).start()

    def kv(k):
        return remote(qkv.at[k, :, pl.ds(KV0, KVW)], kvo.at[k], ksend.at[k], krecv.at[k], net.cn)

    for k in range(4):
        load_w(0, k).wait()
        qkv[k] = (dg(x_ref[...], w[k], 1, 0) + biases[k, 0:1]).astype(bf)
        kv(k).start()
        flow.do(*((), ((Gather.end, 6), (Gather.spread, 6), (Gather.across, 8)), ((Gather.mid, 7), (Gather.line, 8)), ())[k])
    cp = pltpu.make_async_copy(qkv, qkv_out, osem.at[2])
    cp.start()
    outs.append(cp)
    branch[...] = jnp.broadcast_to(out_bias[...], (TOK, COLS))


    def chunk(k, _):
        flow.at(2 * k, TABLE)
        kv(k).wait_recv()
        for j in range(4):
            a = j * HEAD_DIM
            qh[j] = qkv[k, :, a : a + HEAD_DIM]
            kh[j, :TOK] = qkv[k, :, HS + a : HS + a + HEAD_DIM]
            vh[j, :TOK] = qkv[k, :, 2 * HS + a : 2 * HS + a + HEAD_DIM]
            kh[j, TOK:] = kvo[k, :, HS - KV0 + a : HS - KV0 + a + HEAD_DIM]
            vh[j, TOK:] = kvo[k, :, 2 * HS - KV0 + a : 2 * HS - KV0 + a + HEAD_DIM]

        def head(j, _):
            h = k * 4 + j
            s = dg(kh[j], qh[j], 1, 1)
            m = jnp.max(s, axis=0, keepdims=True)
            p = jnp.exp2((s - m) * (C * LOG2E))
            l = jnp.sum(p, axis=0, keepdims=True)
            o = dg(vh[j], p.astype(bf), 0, 0) / l
            oh[j] = o.T.astype(bf)
            lse[h] = m * (C * LOG2E) + jnp.log2(l)
            peak[h] = jnp.broadcast_to(jnp.max(m, axis=1, keepdims=True) * C, (1, 128))
            pl.when(j == 1)(lambda: flow.at(2 * k + 1, TABLE))
            return 0

        lax.fori_loop(0, 4, head, 0)
        att[k] = jnp.concatenate([jnp.zeros((TOK, ATW - HS), bf)] + [oh[j] for j in range(4)], axis=1)
        branch[...] += dg(att[k], w[k, :, AT0:], 1, 1)
        return 0

    lax.fori_loop(0, 4, chunk, 0)
    for src, dst, k in ((kvo, kvo_out, 3), (att, att_out, 4), (branch, branch_out, 5)):
        cp = pltpu.make_async_copy(src, dst, osem.at[k])
        cp.start()
        outs.append(cp)
    outs[0].wait()

    def second_norm(r):
        after = tok_v[r].astype(f32) + vectors[2:3] * branch[r]
        n, _ = normalize(after)
        x_ref[r] = (n * (1.0 + vectors[4:5]) + vectors[3:4]).astype(bf)

    by_rows(64, second_norm)
    cp = pltpu.make_async_copy(x_ref, nm_out, osem.at[6])
    cp.start()
    outs[0] = cp
    flow.do((Gather.corner, 7),)
    flow.from_mate(1)
    own[1].wait()
    for k in range(4):
        load_w(1, k).start()

    def slope_store(k):
        i = lax.rem(k, 2)
        return pltpu.make_async_copy(gd_buf.at[i], gd_out.at[k], gdsem.at[i])

    def hidden(k, _):
        i = lax.rem(k, 2)
        pltpu.make_async_copy(g.at[1, :, pl.ds(pl.multiple_of(k * COLS, 128), COLS)], w.at[k], wsem.at[k]).wait()
        pl.when(k >= 2)(lambda: slope_store(k - 2).wait())
        gd_buf[i] = dg(x_ref[...], w[k], 1, 0)

        def activate(r):
            a, d = gelu_pair(gd_buf[i, r] + biases[k, 1:2])
            act_buf[k, r] = a.astype(bf)
            gd_buf[i, r] = d

        by_rows(64, activate)
        slope_store(k).start()
        pltpu.make_async_copy(act_buf.at[k], act_out.at[k], asem.at[k]).start()
        flow.at(8 + k, TABLE)
        return 0

    lax.fori_loop(0, 4, hidden, 0)
    cot_rows.arrivals()
    cp = pltpu.make_async_copy(cot_v, cot, osem.at[1])
    cp.start()
    outs.append(cp)

    def gated(r):
        x_ref[r] = (vectors[5:6] * cot_v[r].astype(f32)).astype(bf)

    outs[0].wait()
    by_rows(64, gated)
    gbt[...] = x_ref[...].T

    def down_store(k):
        i = lax.rem(k, 2)
        return pltpu.make_async_copy(dbuf.at[i], d2.at[:, pl.ds(pl.multiple_of(k * COLS, 128), COLS)], dsem.at[i])

    def down(k, _):
        i = lax.rem(k, 2)
        pl.when(k >= 2)(lambda: down_store(k - 2).wait())
        dbuf[i] = dg(gbt[...], act_buf[k], 1, 0).astype(bf)
        down_store(k).start()
        flow.at(12 + k, TABLE)
        return 0

    lax.fori_loop(0, 4, down, 0)
    for k in (2, 3):
        slope_store(k).wait()
        down_store(k).wait()
    for k in range(4):
        pltpu.make_async_copy(act_buf.at[k], act_out.at[k], asem.at[k]).wait()
    flow.from_mate(2)
    flow.finish()
    for cp in outs[1:]:
        cp.wait()
    for k in range(4):
        kv(k).wait_send()
    for cp in small:
        cp.wait_send()
    own[2].wait()
    token_rows.sent()
    cot_rows.sent()


def forward(shard, tokens, cotangent, lift_own, ada, ada_bias, z_bias, out_bias):
    rows = S((TOK, COLS), bf)
    wide = S((TOK, COLS), f32)
    return pl.pallas_call(
        forward_kernel,
        name="forward",
        out_shape=(
            S((3, 8 * ROWS, 4 * COLS), bf), rows, rows, S((16, ROWS), f32), S((8, COLS), f32), S((4, 2, COLS), f32),
            rows, S((4, TOK, COLS), bf), S((4, TOK, KVW), bf), S((4, TOK, ATW), bf), S((16, 1, TOK), f32),
            S((16, 1, 128), f32), wide, rows, S((4, TOK, COLS), bf), S((4, TOK, COLS), f32), S((8 * ROWS, 4 * COLS), bf),
        ),
        in_specs=[VM] * 8,
        out_specs=(HB, HB, HB, VM, VM, VM, HB, HB, HB, HB, VM, VM, HB, HB, HB, HB, HB),
        scratch_shapes=[
            V((TOK, COLS), bf), V((TOK, COLS), bf), V((4, 2, 8, COLS), f32), V((4, 8, ADA), f32), V((3, 8, ADA), f32),
            V((8, ADA), f32), V((8, ADA), f32), V((4, 8, ADA), f32), V((TOK, COLS), bf), V((4, COLS, COLS), bf),
            V((4, TOK, COLS), bf), V((4, TOK, KVW), bf), V((4, TOK, ATW), bf), V((TOK, COLS), f32),
            V((4, TOK, HEAD_DIM), bf), V((4, 2 * TOK, HEAD_DIM), bf), V((4, 2 * TOK, HEAD_DIM), bf), V((4, TOK, HEAD_DIM), bf),
            V((COLS, TOK), bf), V((4, TOK, COLS), bf), V((2, TOK, COLS), f32), V((2, COLS, COLS), bf),
            D((12, 7)), D((3, 4, 2)), D((3, 8, 4)), D((3,)), D((2, 2)), D((2, 2)), D((11,)), D((11,)), D((4,)), D((4,)), D((4,)),
            D((7,)), D((4,)), D((2,)), D((2,)),
        ],
        compiler_params=pltpu.CompilerParams(collective_id=1, has_side_effects=True, vmem_limit_bytes=60 * 2**20),
    )(shard, tokens, cotangent, lift_own, ada, ada_bias, z_bias, out_bias)


LINE = (0, 3, 1, 2)


class Scatter:
    def __init__(self, net, source, out, stage, out_sem, rc, far_in, near_in, line_in, side_in, acc, ctmp, ftmp,
                 csend, crecv, own_sem, ctmp_sem, fsend, frecv, ftmp_sem, nsend, nrecv, lsend, lrecv, srecv):
        self.__dict__.update(locals())

    def block(self, v, yy, xx, c):
        row = pl.multiple_of((4 * yy + 2 * xx + c) * ROWS, 16)
        return self.source(v).at[pl.ds(row, ROWS), pl.ds(LINE[v % 4] * COLS, COLS)]

    def places(self):
        return [(yy, xx) for yy in range(2) for xx in range(2)]

    def to_mate(self, v, yy, xx):
        return remote(
            self.block(v, yy, xx, 1 - self.net.c), self.rc.at[v, yy, xx],
            self.csend.at[v, yy, xx], self.crecv.at[v, yy, xx], self.net.cn,
        )

    def begin(self, v):
        for yy, xx in self.places():
            self.to_mate(v, yy, xx).start()

    def to_far(self, v, n):
        yy, xx = self.net.place(1 - self.net.f, n)
        return remote(self.acc.at[v % 4, yy, xx], self.far_in.at[v, n], self.fsend.at[v, n], self.frecv.at[v, n], self.net.far)

    def to_near(self, v):
        yy, xx = self.net.place(self.net.f, 1 - self.net.n)
        return remote(self.acc.at[v % 4, yy, xx], self.near_in.at[v], self.nsend.at[v], self.nrecv.at[v], self.net.near)

    def own_loads(self, v):
        return [
            pltpu.make_async_copy(self.block(v, yy, xx, self.net.c), self.acc.at[v % 4, yy, xx], self.own_sem.at[yy, xx])
            for yy, xx in self.places()
        ]

    def mate_loads(self, v, f):
        for n in range(2):
            yy, xx = self.net.place(f, n)
            yield pltpu.make_async_copy(self.rc.at[v, yy, xx], self.ctmp.at[f, n], self.ctmp_sem.at[f, n])

    def add(self, a, b):
        def one(i, _):
            r = pl.ds(pl.multiple_of(i * 48, 16), 48)
            a[r] = a[r] + b[r]
            return 0

        lax.fori_loop(0, ROWS // 48, one, 0)

    def fetch(self, v):
        if v >= 4:
            for n in range(2):
                self.to_far(v - 4, n).wait_send()
            self.to_near(v - 4).wait_send()
        for cp in self.own_loads(v):
            cp.start()
        for yy, xx in self.places():
            landed(self.rc.at[v, yy, xx], self.crecv.at[v, yy, xx])
        for f in (1 - self.net.f, self.net.f):
            for cp in self.mate_loads(v, f):
                cp.start()

    def core(self, v):
        for cp in self.own_loads(v):
            cp.wait()
        for f in (1 - self.net.f, self.net.f):
            for n, cp in enumerate(self.mate_loads(v, f)):
                cp.wait()
                yy, xx = self.net.place(f, n)
                self.add(self.acc.at[v % 4, yy, xx], self.ctmp.at[f, n])
                if f is not self.net.f:
                    self.to_far(v, n).start()

    def far_loads(self, v):
        return [pltpu.make_async_copy(self.far_in.at[v, n], self.ftmp.at[n], self.ftmp_sem.at[n]) for n in range(2)]

    def bring(self, v):
        for n, cp in enumerate(self.far_loads(v)):
            landed(self.far_in.at[v, n], self.frecv.at[v, n])
            cp.start()

    def far(self, v):
        for cp in self.far_loads(v):
            cp.wait()
        for n in (1 - self.net.n, self.net.n):
            yy, xx = self.net.place(self.net.f, n)
            self.add(self.acc.at[v % 4, yy, xx], self.ftmp.at[n])
            if n is not self.net.n:
                self.to_near(v).start()

    def near(self, v):
        landed(self.near_in.at[v], self.nrecv.at[v])
        self.add(self.near_in.at[v], self.acc.at[v % 4, self.net.y, self.net.x])

    def hop(self, v, h, act):
        net, zz = self.net, LINE[v % 4]
        if h < zz:

            @pl.when(net.z == h)
            def _():
                act(v, h, remote(self.near_in.at[v], self.line_in.at[v], self.lsend.at[v], self.lrecv.at[v], net.zpn))

        if 3 - h > zz:

            @pl.when(net.z == 3 - h)
            def _():
                side = 3 - h - 1 == zz
                dst = self.side_in.at[v // 4] if side else self.line_in.at[v]
                sem = self.srecv.at[v // 4] if side else self.lrecv.at[v]
                act(v, h, remote(self.near_in.at[v], dst, self.lsend.at[v], sem, net.zmn))

    def pass_on(self, v, h, cp):
        if h:
            landed(self.line_in.at[v], self.lrecv.at[v])
            self.add(self.near_in.at[v], self.line_in.at[v])
        cp.start()

    def line0(self, v):
        self.hop(v, 0, self.pass_on)

    def line1(self, v):
        self.hop(v, 1, self.pass_on)

    def line2(self, v):
        self.hop(v, 2, self.pass_on)

    def keep(self, t):
        return pltpu.make_async_copy(self.stage, self.out.at[t], self.out_sem)

    def last(self, v):
        t, zz = 2 - v // 4, LINE[v % 4]

        @pl.when(self.net.z == zz)
        def _():
            if zz > 0:
                landed(self.line_in.at[v], self.lrecv.at[v])
            if zz < 3:
                landed(self.side_in.at[v // 4], self.srecv.at[v // 4])
            if t < 2:
                self.keep(t + 1).wait()

            def one(i, _):
                r = pl.ds(pl.multiple_of(i * 16, 16), 16)
                total = self.near_in[v, r].astype(f32)
                if zz > 0:
                    total = total + self.line_in[v, r].astype(f32)
                if zz < 3:
                    total = total + self.side_in[v // 4, r].astype(f32)
                self.stage[r] = total
                return 0

            lax.fori_loop(0, ROWS // 16, one, 0)
            self.keep(t).start()

    def rows(self, p):
        self.block_back.piece(p)

    def toks(self, p):
        self.token_back.piece(p)

    def do(self, *steps):
        for step, v in steps:
            step(self, v)

    def at(self, point, table, base=0):
        for p, steps in enumerate(table):
            if steps:
                pl.when(point == base + p)(lambda: self.do(*steps))

    def finish(self):
        self.keep(0).wait()
        for v in range(12):
            for yy, xx in self.places():
                self.to_mate(v, yy, xx).wait_send()
            if v >= 8:
                for n in range(2):
                    self.to_far(v, n).wait_send()
                self.to_near(v).wait_send()
            for h in range(3):
                self.hop(v, h, lambda v, h, cp: cp.wait_send())


HIDDEN = (
    ((Scatter.core, 2), (Scatter.fetch, 3)),
    ((Scatter.bring, 0), (Scatter.far, 0), (Scatter.core, 3)),
    ((Scatter.begin, 4),),
    ((Scatter.bring, 1), (Scatter.far, 1)),
    ((Scatter.begin, 5),),
    ((Scatter.near, 0), (Scatter.line0, 0), (Scatter.fetch, 4), (Scatter.bring, 2)),
    ((Scatter.core, 4), (Scatter.far, 2), (Scatter.begin, 6)),
    ((Scatter.near, 1), (Scatter.line0, 1), (Scatter.fetch, 5)),
)
HEADS = (
    ((Scatter.bring, 4), (Scatter.near, 3), (Scatter.line0, 3), (Scatter.fetch, 7), (Scatter.rows, 0)),
    ((Scatter.far, 4), (Scatter.core, 7), (Scatter.rows, 1)),
    ((Scatter.bring, 5), (Scatter.rows, 2)),
    ((Scatter.far, 5), (Scatter.rows, 3)),
    ((Scatter.rows, 4),),
    ((Scatter.near, 4), (Scatter.line0, 4), (Scatter.bring, 6), (Scatter.rows, 5)),
    ((Scatter.begin, 8), (Scatter.far, 6), (Scatter.rows, 6)),
    ((Scatter.near, 5), (Scatter.line0, 5), (Scatter.fetch, 8), (Scatter.line1, 0), (Scatter.line1, 1), (Scatter.rows, 7)),
    ((Scatter.bring, 7), (Scatter.core, 8), (Scatter.far, 7), (Scatter.line1, 2), (Scatter.line1, 3)),
    ((Scatter.line1, 4),),
    ((Scatter.begin, 9), (Scatter.near, 6), (Scatter.line0, 6), (Scatter.line2, 0), (Scatter.line2, 1)),
    ((Scatter.fetch, 9), (Scatter.line2, 2), (Scatter.line2, 3), (Scatter.line1, 5)),
    ((Scatter.core, 9), (Scatter.near, 7), (Scatter.line0, 7)),
    ((Scatter.bring, 8), (Scatter.far, 8), (Scatter.line1, 6), (Scatter.line2, 4)),
    ((Scatter.begin, 10), (Scatter.last, 0), (Scatter.last, 1), (Scatter.line2, 5)),
    ((Scatter.fetch, 10), (Scatter.last, 2), (Scatter.last, 3), (Scatter.line1, 7)),
)


class Back:
    def __init__(self, net, src, dst, send, recv):
        self.net, self.src, self.dst, self.send, self.recv = net, src, dst, send, recv

    def copy(self, k, first, count):
        net = self.net
        dc, dz = lax.div(net.z, 2), 2 * net.c + k
        here = jnp.logical_and(dc == net.c, dz == net.z)
        rows, image = self.src.at[pl.ds(k * 256 + first, count)], self.dst.at[lax.rem(net.z, 2), pl.ds(first, count)]
        sem = self.recv.at[lax.rem(net.z, 2)]
        return remote(rows, image, self.send.at[k], sem, (net.y, net.x, dc, dz)), pltpu.make_async_copy(rows, image, sem), here

    def piece(self, p):
        cp, local, here = self.copy(p % 2, p // 2 * 64, 64)
        pl.when(jnp.logical_not(here))(cp.start)
        pl.when(here)(local.start)

    def sent(self):
        for k in range(2):
            cp, _, here = self.copy(k, 0, 256)
            pl.when(jnp.logical_not(here))(cp.wait_send)

    def arrivals(self):
        for i in range(2):
            landed(self.dst.at[i], self.recv.at[i])


def column_sum(v):
    return jnp.sum(v.astype(f32), axis=0, keepdims=True)


def backward_kernel(
    g, tok_in, cot_in, x_in, nm_in, qkv_in, kvo_in, att_in, lse, peak, branch_in, act_in, gd_in, d2, vectors, lift_rows, ada, down_bias,
    sums, block_rows, token_rows, d, rc, far_in, ada_grad, ada_bias_grad, lifted, totals,
    tok, cot, branch, gn, br, gb, gub, xt, gt, w1, act, dbuf, near_in, line_in, side_in, acc, ctmp, ftmp, mate_in,
    stage, bias, bias_in, terms, terms_in, image, pgl, pgl_in, four,
    out_sem, csend, crecv, own_sem, ctmp_sem, fsend, frecv, ftmp_sem, nsend, nrecv, lsend, lrecv, srecv,
    bsend, brecv, isem, w1_sem, w2_sem, act_sem, gd_sem, dsem, msend, mrecv, kvsem, small_send, small_recv,
):
    net = Net()
    y, x, c, z = net.y, net.x, net.c, net.z
    plane = 2 * y + x

    def fetch(src, dst, k):
        cp = pltpu.make_async_copy(src, dst, isem.at[k])
        cp.start()
        return cp

    first = [fetch(cot_in, cot, 0), fetch(nm_in, gub, 1), fetch(tok_in, tok, 2), fetch(branch_in, branch, 3)]

    def cols(ref, k):
        return ref.at[:, pl.ds(pl.multiple_of(zs(k) * COLS, 128), COLS)]

    def zs(k):
        return jnp.where(k == 0, 0, jnp.where(k == 1, 3, k - 1))

    def load_first(t, k):
        return pltpu.make_async_copy(cols(g.at[t], k), w1.at[lax.rem(k, 2)], w1_sem.at[lax.rem(k, 2)])

    def d_store(t, k):
        return pltpu.make_async_copy(dbuf, cols(d.at[t], k), dsem)

    load_first(1, jnp.int32(0)).start()
    net.greet()
    flow = Scatter(
        net, lambda v: d2 if v < 4 else d.at[2 - v // 4], sums, stage, out_sem, rc, far_in, near_in, line_in, side_in, acc, ctmp, ftmp,
        csend, crecv, own_sem, ctmp_sem, fsend, frecv, ftmp_sem, nsend, nrecv, lsend, lrecv, srecv,
    )
    for v in range(4):
        flow.begin(v)
    shift_attn, scale_attn, gate_attn, shift_mlp, scale_mlp, gate_mlp = [vectors[i : i + 1] for i in range(6)]
    terms[...] = jnp.zeros_like(terms)
    bias[...] = jnp.zeros_like(bias)
    for h in range(16):
        bias[h : h + 1, COLS:] = peak[h]
    gn[...] = jnp.zeros_like(gn)
    br[...] = jnp.zeros_like(br)
    first[0].wait()

    def gated(r):
        gb[r] = (gate_mlp * cot[r].astype(f32)).astype(bf)

    by_rows(64, gated)
    first[1].wait()
    xt[...] = gub[...].T

    def mlp(w2, gd):
        def loads(k):
            i = lax.rem(k, 2)
            return (
                load_first(1, k),
                pltpu.make_async_copy(cols(g.at[2], k), w2.at[i], w2_sem.at[i]),
                pltpu.make_async_copy(act_in.at[zs(k)], act.at[i], act_sem.at[i]),
                pltpu.make_async_copy(gd_in.at[zs(k)], gd.at[i], gd_sem.at[i]),
            )

        for cp in loads(jnp.int32(0))[1:]:
            cp.start()
        flow.do((Scatter.fetch, 0), (Scatter.core, 0), (Scatter.fetch, 1), (Scatter.core, 1), (Scatter.fetch, 2))

        def hidden(k, _):
            i = lax.rem(k, 2)
            for cp in loads(k):
                cp.wait()

            @pl.when(k < 3)
            def _():
                for cp in loads(k + 1):
                    cp.start()

            gub[...] = (dg(gb[...], w2[i], 1, 0) * gd[i]).astype(bf)
            bias[pl.ds(4 + zs(k), 1), :COLS] = column_sum(gub[...])
            br[...] += dg(act[i], w2[i], 1, 1)
            pl.when(k > 0)(lambda: d_store(1, k - 1).wait())
            flow.at(2 * k, HIDDEN)
            dbuf[...] = dg(xt[...], gub[...], 1, 0).astype(bf)
            d_store(1, k).start()
            gn[...] += dg(gub[...], w1[i], 1, 1)
            flow.at(2 * k + 1, HIDDEN)
            return 0

        lax.fori_loop(0, 4, hidden, 0)

    pl.run_scoped(mlp, V((2, COLS, COLS), bf), V((2, TOK, COLS), f32))
    load_first(0, jnp.int32(0)).start()
    d_store(1, jnp.int32(3)).wait()
    flow.do((Scatter.begin, 7), (Scatter.core, 5), (Scatter.bring, 3), (Scatter.far, 3))
    first[2].wait()
    first[3].wait()

    def second_norm(r):
        after = tok[r].astype(f32) + gate_attn * branch[r]
        n, s = normalize(after)
        mlp_out = br[r] + down_bias[...]
        gub[r] = (after + gate_mlp * mlp_out).astype(bf)
        go = cot[r].astype(f32)
        terms[5:6] += column_sum(go * mlp_out)
        gr = gn[r]
        terms[3:4] += column_sum(gr)
        terms[4:5] += column_sum(gr * n)
        e = gr * (1.0 + scale_mlp)
        ga = go + s * (e - jnp.mean(e, axis=-1, keepdims=True) - n * jnp.mean(e * n, axis=-1, keepdims=True))
        br[r] = ga
        terms[2:3] += column_sum(ga * branch[r])
        bias[9:10, :COLS] += column_sum(gb[r])
        low = (gate_attn * ga).astype(bf)
        bias[8:9, :COLS] += column_sum(low)
        gb[r] = low

    by_rows(64, second_norm)
    block_back = Back(net, gub, block_rows, bsend.at[0], brecv.at[0])
    flow.do((Scatter.near, 2), (Scatter.line0, 2), (Scatter.fetch, 6))
    flow.block_back = block_back
    flow.do((Scatter.core, 6),)
    load = fetch(x_in, cot, 0)
    gt[...] = gb[...].T
    gn[...] = jnp.zeros_like(gn)
    load.wait()
    xt[...] = cot[...].T

    def attention(kvo, att, qh, kh, vh, gh, dqh, dkh, dvh, dkm, dvm, mate_out):
        pack = cot

        def loads(k):
            i = lax.rem(k, 2)
            return (
                load_first(0, k),
                pltpu.make_async_copy(qkv_in.at[zs(k)], act.at[i], act_sem.at[i]),
                pltpu.make_async_copy(kvo_in.at[zs(k)], kvo, kvsem.at[0, i]),
                pltpu.make_async_copy(att_in.at[zs(k)], att.at[i], kvsem.at[1, i]),
            )

        for cp in loads(jnp.int32(0))[1:]:
            cp.start()

        def to_mate(k):
            return remote(mate_out, mate_in.at[lax.rem(k, 2)], msend, mrecv.at[k], net.cn)

        def complete(k):
            i = lax.rem(k, 2)
            to_mate(k).wait_send()
            landed(mate_in.at[i], mrecv.at[k])
            both = (branch[:, : 2 * HS] + mate_in[i, :, : 2 * HS].astype(f32)).astype(bf)
            pack[:, HS:] = jnp.concatenate([both, jnp.zeros((TOK, HS), bf)], axis=1)
            bias[pl.ds(zs(k), 1), :COLS] = column_sum(pack[...])
            gn[...] += dg(pack[...], w1[i], 1, 1)
            d1 = dg(xt[...], pack[:, :896], 1, 0)
            d2_ = dg(gt[...], att[i], 1, 0)
            dbuf[:, :AT0] = d1[:, :AT0].astype(bf)
            dbuf[:, AT0:896] = (d1[:, AT0:] + d2_[:, :128]).astype(bf)
            dbuf[:, 896:] = d2_[:, 128:].astype(bf)
            d_store(0, k).start()

        def chunk(k, _):
            i = lax.rem(k, 2)
            for cp in loads(k):
                cp.wait()
            ga = dg(gb[...], w1[i, :, AT0:], 1, 0).astype(bf)
            for j in range(4):
                a = j * HEAD_DIM
                gh[j] = ga[:, ATW - HS + a : ATW - HS + a + HEAD_DIM]
                qh[j] = act[i, :, a : a + HEAD_DIM]
                kh[j, :TOK] = act[i, :, HS + a : HS + a + HEAD_DIM]
                vh[j, :TOK] = act[i, :, 2 * HS + a : 2 * HS + a + HEAD_DIM]
                kh[j, TOK:] = kvo[:, HS - KV0 + a : HS - KV0 + a + HEAD_DIM]
                vh[j, TOK:] = kvo[:, 2 * HS - KV0 + a : 2 * HS - KV0 + a + HEAD_DIM]

            def head(j, _):
                kk, q, gg = kh[j], qh[j], gh[j]
                p = jnp.exp2(dg(kk, q, 1, 1) * (C * LOG2E) - lse[zs(k) * 4 + j])
                t = p * dg(vh[j], gg, 1, 1)
                inner = jnp.sum(t, axis=0, keepdims=True)
                ds = (t - p * inner).astype(bf)
                dv = dg(p.astype(bf), gg, 1, 0)
                dvh[j], dvm[j] = dv[:TOK], dv[TOK:].astype(bf)
                dk = dg(ds, q, 1, 0) * C
                dkh[j], dkm[j] = dk[:TOK], dk[TOK:].astype(bf)
                dqh[j] = (dg(kk, ds, 0, 0) * C).T.astype(bf)
                pl.when(jnp.logical_and(j == 1, k > 0))(lambda: complete(k - 1))

                @pl.when(jnp.logical_and(j == 1, k < 3))
                def _():
                    for cp in loads(k + 1):
                        cp.start()

                pl.when(jnp.logical_and(j == 2, k > 0))(lambda: d_store(0, k - 1).wait())
                flow.at(4 * k + j, HEADS)
                return 0

            lax.fori_loop(0, 4, head, 0)
            mate_out[...] = jnp.concatenate(
                [dkm[j] for j in range(4)] + [dvm[j] for j in range(4)] + [jnp.zeros((TOK, KVW - 2 * HS), bf)], axis=1,
            )
            to_mate(k).start()
            branch[:, : 2 * HS] = jnp.concatenate([dkh[j] for j in range(4)] + [dvh[j] for j in range(4)], axis=1)
            pack[:, :HS] = jnp.concatenate([dqh[j] for j in range(4)], axis=1)
            return 0

        lax.fori_loop(0, 4, chunk, 0)
        flow.do((Scatter.core, 10), (Scatter.bring, 9))
        complete(jnp.int32(3))
        flow.do((Scatter.far, 9), (Scatter.near, 8), (Scatter.line0, 8), (Scatter.last, 4), (Scatter.line2, 6), (Scatter.line2, 7))

    T = (4, TOK, HEAD_DIM)
    T2 = (4, 2 * TOK, HEAD_DIM)
    pl.run_scoped(
        attention, V((TOK, KVW), bf), V((2, TOK, ATW), bf), V(T, bf), V(T2, bf), V(T2, bf), V(T, bf), V(T, bf), V(T, f32), V(T, f32),
        V(T, bf), V(T, bf), V((TOK, KVW), bf),
    )

    def first_norm(r):
        n, s = normalize(tok[r].astype(f32))
        gr = gn[r]
        terms[0:1] += column_sum(gr)
        terms[1:2] += column_sum(gr * n)
        e = gr * (1.0 + scale_attn)
        gr = s * (e - jnp.mean(e, axis=-1, keepdims=True) - n * jnp.mean(e * n, axis=-1, keepdims=True))
        tok[r] = (br[r] + gr).astype(bf)

    by_rows(64, first_norm)
    token_back = Back(net, tok, token_rows, bsend.at[1], brecv.at[1])
    flow.token_back = token_back

    small = []

    def exchange(k, src, dst, dev):
        cp = remote(src, dst, small_send.at[k], small_recv.at[k], dev)
        cp.start()
        small.append(cp)

    def combine(k):
        bias[:, :COLS] += bias_in[k, :, :COLS]
        bias[:, COLS:] = jnp.maximum(bias[:, COLS:], bias_in[k, :, COLS:])

    peers = ((net.xn, 2 * y + 1 - x), (net.yn, 2 - 2 * y + x), (net.dn, 3 - plane))
    exchange(0, terms, terms_in, net.cn)
    four[0] = bias[...]
    exchange(1, four.at[0], bias_in.at[0], net.cn)
    d_store(0, jnp.int32(3)).wait()
    flow.begin(11)
    landed(terms_in, small_recv.at[0])
    image[plane, z] = (terms[...] + terms_in[...]).astype(bf).astype(f32)
    for k in range(3):
        exchange(2 + k, image.at[plane, z], image.at[plane, z], net.along_z(k + 1))
    landed(bias_in.at[0], small_recv.at[1])
    combine(0)
    four[1] = bias[...]
    for k in range(3):
        exchange(5 + k, four.at[1], bias_in.at[1 + k], net.along_z(k + 1))
    flow.do((Scatter.fetch, 11), (Scatter.near, 9), (Scatter.line0, 9), (Scatter.core, 11), (Scatter.bring, 10), (Scatter.far, 10), (Scatter.toks, 0), (Scatter.toks, 1))
    for k in range(3):
        landed(image.at[plane, lax.rem(z + 3 - k, 4)], small_recv.at[2 + k])
    for k, (dev, _) in enumerate(peers):
        exchange(8 + k, image.at[plane], image.at[plane], dev)
    flow.do((Scatter.bring, 11), (Scatter.far, 11), (Scatter.near, 10), (Scatter.line0, 10), (Scatter.line1, 8), (Scatter.toks, 2))
    for k, (_, p) in enumerate(peers):
        landed(image.at[p], small_recv.at[8 + k])
    every = [jnp.concatenate([image[p, q, i : i + 1] for p in range(4) for q in range(4)], axis=0) for i in range(6)]
    half = COLS // 2
    options = (
        (every[0], every[1][:, :half]), (every[1][:, half:], every[2]),
        (every[3], every[4][:, :half]), (every[4][:, half:], every[5]),
    )
    grad = sum(jnp.where(z == k, jnp.concatenate(o, axis=1), 0.0) for k, o in enumerate(options))
    low = grad.astype(bf)
    pgl[0] = dg(low, ada[...], 1, 1)
    for k in range(3):
        exchange(14 + k, pgl.at[0], pgl_in.at[k], net.along_z(k + 1))
    flow.do((Scatter.toks, 3), (Scatter.near, 11), (Scatter.line0, 11), (Scatter.toks, 4))
    ada_bias_grad[...] = column_sum(grad)
    ada_grad[...] = dg(lift_rows[...].astype(bf), low, 0, 0)
    for k in range(3):
        landed(bias_in.at[1 + k], small_recv.at[5 + k])
        combine(1 + k)
    four[2] = bias[...]
    for k, (dev, _) in enumerate(peers):
        exchange(11 + k, four.at[2], bias_in.at[4 + k], dev)
    flow.do((Scatter.line1, 9), (Scatter.toks, 5), (Scatter.line2, 8), (Scatter.line1, 10), (Scatter.toks, 6))
    for k in range(3):
        landed(pgl_in.at[k], small_recv.at[14 + k])
    lifted[plane, c] = pgl[0] + pgl_in[0] + pgl_in[1] + pgl_in[2]
    exchange(17, lifted.at[plane, c], lifted.at[plane, c], net.cn)
    flow.do((Scatter.line1, 11), (Scatter.line2, 9), (Scatter.toks, 7))
    landed(lifted.at[plane, 1 - c], small_recv.at[17])
    for k, (dev, _) in enumerate(peers):
        exchange(18 + k, lifted.at[plane], lifted.at[plane], dev)
    for k in range(3):
        landed(bias_in.at[4 + k], small_recv.at[11 + k])
        combine(4 + k)
    totals[...] = bias[...]
    flow.do((Scatter.last, 5), (Scatter.last, 6), (Scatter.last, 7), (Scatter.last, 8), (Scatter.line2, 10), (Scatter.last, 9), (Scatter.line2, 11), (Scatter.last, 10), (Scatter.last, 11))
    for k, (_, p) in enumerate(peers):
        landed(lifted.at[p], small_recv.at[18 + k])
    block_back.arrivals()
    token_back.arrivals()
    flow.finish()
    for cp in small:
        cp.wait_send()
    block_back.sent()
    token_back.sent()


def backward(*args):
    B = (ROWS, COLS)
    wide, rows = (TOK, COLS), (2, 256, COLS)
    pair = D((2,))
    return pl.pallas_call(
        backward_kernel,
        name="backward",
        out_shape=(
            S((3,) + B, f32), S(rows, bf), S(rows, bf), S((2, 8 * ROWS, 4 * COLS), bf), S((12, 2, 2) + B, bf), S((12, 2) + B, bf),
            S((ROWS, ADA), f32), S((1, ADA), f32), S((4, 2, 16, ROWS), f32), S((16, COLS + 128), f32),
        ),
        in_specs=[HB] * 8 + [VM, VM] + [HB] * 4 + [VM] * 4,
        out_specs=(HB,) * 6 + (VM,) * 4,
        scratch_shapes=[
            V(wide, bf), V(wide, bf), V(wide, f32), V(wide, f32), V(wide, f32), V(wide, bf), V(wide, bf), V((COLS, TOK), bf), V((COLS, TOK), bf),
            V((2, COLS, COLS), bf), V((2, TOK, COLS), bf), V((COLS, COLS), bf),
            V((12,) + B, bf), V((12,) + B, bf), V((3,) + B, bf), V((4, 2, 2) + B, bf), V((2, 2) + B, bf), V((2,) + B, bf), V((2, TOK, KVW), bf),
            V(B, f32), V((16, COLS + 128), f32), V((7, 16, COLS + 128), f32), V((8, COLS), f32), V((8, COLS), f32), V((4, 4, 8, COLS), f32),
            V((1, 16, ROWS), f32), V((3, 16, ROWS), f32), V((3, 16, COLS + 128), f32),
            D, D((12, 2, 2)), D((12, 2, 2)), D((2, 2)), D((2, 2)), D((12, 2)), D((12, 2)), pair, D((12,)), D((12,)), D((12,)), D((12,)), D((3,)),
            D((2, 2)), D((2, 2)), D((4,)), pair, pair, pair, pair, D, D, D((4,)), D((2, 2)), D((21,)), D((21,)),
        ],
        compiler_params=pltpu.CompilerParams(collective_id=2, has_side_effects=True, vmem_limit_bytes=62 * 2**20),
    )(*args)


def modulate_images(values, shift, scale):
    average = jnp.mean(values, axis=-1, keepdims=True)
    centred = values - average
    spread = jnp.mean(centred * centred, axis=-1, keepdims=True)
    return centred * lax.rsqrt(spread + epsilon) * (1.0 + scale[:, None, :]) + shift[:, None, :]


def product(left, right):
    return jnp.dot(left, right, preferred_element_type=jnp.float32)


def inner_rows(left, right):
    return lax.dot_general(
        left, right, (((0,), (0,)), ((), ())), preferred_element_type=jnp.float32
    )


def against(left, right):
    return lax.dot_general(
        left, right, (((1,), (1,)), ((), ())), preferred_element_type=jnp.float32
    )


def spread_rows(values):
    return lax.all_gather(values, "tensor", axis=1, tiled=True)


def fold_rows(values):
    return lax.psum_scatter(values, "tensor", scatter_dimension=1, tiled=True)


def spread_grads(values):
    return lax.all_gather(values, "tensor", axis=1, tiled=True)


def fold_grads(values):
    return lax.psum_scatter(values, "tensor", scatter_dimension=1, tiled=True)


def local(
    tokens,
    conditioning,
    cotangent,
    query_weight,
    key_weight,
    value_weight,
    out_weight,
    up_weight,
    down_weight,
    ada_weight,
    query_bias,
    value_bias,
    out_bias,
    up_bias,
    down_bias,
    ada_bias,
    threshold,
):
    images = tokens.shape[0]
    model_width = tokens.shape[2]
    gathered = (
        lax.all_gather(query_weight, "dp", axis=0, tiled=True),
        lax.all_gather(key_weight, "dp", axis=0, tiled=True),
        lax.all_gather(value_weight, "dp", axis=0, tiled=True),
        lax.all_gather(out_weight, "dp", axis=1, tiled=True),
        lax.all_gather(up_weight, "dp", axis=0, tiled=True),
        lax.all_gather(down_weight, "dp", axis=1, tiled=True),
        lax.all_gather(ada_weight, "dp", axis=0, tiled=True),
    )
    full_query, full_key, full_value, full_out, full_up, full_down, full_ada = gathered
    lifted_low = jax.nn.silu(conditioning).astype(jnp.bfloat16)
    own_columns = product(lifted_low, full_ada) + ada_bias
    modulation = lax.all_gather(own_columns, "tensor", axis=1, tiled=True)
    pieces = [
        modulation[:, piece_index * model_width : (piece_index + 1) * model_width]
        for piece_index in range(6)
    ]
    shift_attn, scale_attn, gate_attn, shift_mlp, scale_mlp, gate_mlp = pieces
    inputs = tokens.astype(jnp.float32)
    normed_attn = spread_rows(modulate_images(inputs, shift_attn, scale_attn).astype(jnp.bfloat16))
    length = normed_attn.shape[1]
    row_count = images * length
    flat_attn = normed_attn.reshape(row_count, model_width)
    local_width = full_query.shape[1]
    heads_here = local_width // HEAD_DIM
    queries = (product(flat_attn, full_query) + query_bias).astype(jnp.bfloat16)
    key_rows = product(flat_attn, full_key).astype(jnp.bfloat16)
    value_rows = (product(flat_attn, full_value) + value_bias).astype(jnp.bfloat16)
    block_rows = min(512, length)
    head_scale = HEAD_DIM ** (-0.5)

    def by_head(matrix):
        return matrix.reshape(images, length, heads_here, HEAD_DIM)

    def attend_image(bundle):
        queries_img, keys_img, values_img = bundle
        outputs, totals, highest = ([], [], [])
        for offset in range(0, length, block_rows):
            logits = (
                jnp.einsum(
                    "qhe,khe->hqk",
                    queries_img[offset : offset + block_rows],
                    keys_img,
                    preferred_element_type=jnp.float32,
                )
                * head_scale
            )
            row_top = jnp.max(logits, axis=2, keepdims=True)
            raised = jnp.exp(logits - row_top)
            summed = jnp.sum(raised, axis=2, keepdims=True)
            shares = (raised / summed).astype(jnp.bfloat16)
            outputs.append(
                jnp.einsum(
                    "hqk,khe->qhe", shares, values_img, preferred_element_type=jnp.float32
                ).astype(jnp.bfloat16)
            )
            totals.append(row_top[:, :, 0] + jnp.log(summed[:, :, 0]))
            highest.append(jnp.max(row_top[:, :, 0], axis=1))
        return (
            jnp.concatenate(outputs, 0),
            jnp.concatenate(totals, 1),
            jnp.max(jnp.stack(highest), axis=0),
        )

    attended, log_totals, image_peaks = lax.map(
        attend_image, (by_head(queries), by_head(key_rows), by_head(value_rows))
    )
    flat_attended = attended.reshape(row_count, local_width)
    branch_attn = (
        fold_rows(product(flat_attended, full_out).reshape(images, length, model_width)) + out_bias
    )
    after_attn = inputs + gate_attn[:, None, :] * branch_attn
    normed_mlp = spread_rows(modulate_images(after_attn, shift_mlp, scale_mlp).astype(jnp.bfloat16))
    flat_mlp = normed_mlp.reshape(row_count, model_width)
    upward = product(flat_mlp, full_up) + up_bias
    active = jax.nn.gelu(upward, approximate=True).astype(jnp.bfloat16)
    branch_mlp = (
        fold_rows(product(active, full_down).reshape(images, length, model_width)) + down_bias
    )
    block_out = (after_attn + gate_mlp[:, None, :] * branch_mlp).astype(jnp.bfloat16)
    peaks = lax.pmax(jnp.max(image_peaks, axis=0), "dp")
    again = (
        lax.all_gather(query_weight, "dp", axis=0, tiled=True),
        lax.all_gather(key_weight, "dp", axis=0, tiled=True),
        lax.all_gather(value_weight, "dp", axis=0, tiled=True),
        lax.all_gather(out_weight, "dp", axis=1, tiled=True),
        lax.all_gather(up_weight, "dp", axis=0, tiled=True),
        lax.all_gather(down_weight, "dp", axis=1, tiled=True),
        lax.all_gather(ada_weight, "dp", axis=0, tiled=True),
    )
    back_query, back_key, back_value, back_out, back_up, back_down, back_ada = again
    grad_out = cotangent.astype(jnp.float32)
    grad_branch_mlp = (gate_mlp[:, None, :] * grad_out).astype(jnp.bfloat16)
    grad_gate_mlp = jnp.sum(grad_out * branch_mlp, axis=1)
    flat_grad_mlp = spread_grads(grad_branch_mlp).reshape(row_count, model_width)
    grad_down_bias = jnp.sum(flat_grad_mlp, axis=0, dtype=jnp.float32)
    grad_down_weight = inner_rows(active, flat_grad_mlp)
    grad_active = against(flat_grad_mlp, back_down)
    _, gelu_pull = jax.vjp(partial(jax.nn.gelu, approximate=True), upward)
    grad_upward = gelu_pull(grad_active)[0].astype(jnp.bfloat16)
    grad_up_bias = jnp.sum(grad_upward, axis=0, dtype=jnp.float32)
    grad_up_weight = inner_rows(flat_mlp, grad_upward)
    grad_normed_mlp = fold_grads(against(grad_upward, back_up).reshape(images, length, model_width))
    _, mlp_pull = jax.vjp(modulate_images, after_attn, shift_mlp, scale_mlp)
    grad_after, grad_shift_mlp, grad_scale_mlp = mlp_pull(grad_normed_mlp)
    grad_after = grad_out + grad_after
    grad_branch_attn = (gate_attn[:, None, :] * grad_after).astype(jnp.bfloat16)
    grad_gate_attn = jnp.sum(grad_after * branch_attn, axis=1)
    flat_grad_attn = spread_grads(grad_branch_attn).reshape(row_count, model_width)
    grad_out_bias = jnp.sum(flat_grad_attn, axis=0, dtype=jnp.float32)
    grad_out_weight = inner_rows(flat_attended, flat_grad_attn)
    grad_attended = against(flat_grad_attn, back_out).astype(jnp.bfloat16)

    def attend_back(bundle):
        queries_img, keys_img, values_img, grads_img, totals_img = bundle
        query_parts = []
        grad_keys_img = jnp.zeros(keys_img.shape, jnp.float32)
        grad_values_img = jnp.zeros(values_img.shape, jnp.float32)
        for offset in range(0, length, block_rows):
            query_block = queries_img[offset : offset + block_rows]
            grad_block = grads_img[offset : offset + block_rows]
            logits = (
                jnp.einsum(
                    "qhe,khe->hqk", query_block, keys_img, preferred_element_type=jnp.float32
                )
                * head_scale
            )
            shares = jnp.exp(logits - totals_img[:, offset : offset + block_rows, None])
            grad_shares = jnp.einsum(
                "qhe,khe->hqk", grad_block, values_img, preferred_element_type=jnp.float32
            )
            row_inner = jnp.sum(shares * grad_shares, axis=2, keepdims=True)
            grad_logits = (shares * (grad_shares - row_inner)).astype(jnp.bfloat16)
            query_parts.append(
                (
                    jnp.einsum(
                        "hqk,khe->qhe", grad_logits, keys_img, preferred_element_type=jnp.float32
                    )
                    * head_scale
                ).astype(jnp.bfloat16)
            )
            grad_keys_img = (
                grad_keys_img
                + jnp.einsum(
                    "hqk,qhe->khe", grad_logits, query_block, preferred_element_type=jnp.float32
                )
                * head_scale
            )
            grad_values_img = grad_values_img + jnp.einsum(
                "hqk,qhe->khe",
                shares.astype(jnp.bfloat16),
                grad_block,
                preferred_element_type=jnp.float32,
            )
        return (
            jnp.concatenate(query_parts, 0),
            grad_keys_img.astype(jnp.bfloat16),
            grad_values_img.astype(jnp.bfloat16),
        )

    grad_queries, grad_keys, grad_values = lax.map(
        attend_back,
        (
            by_head(queries),
            by_head(key_rows),
            by_head(value_rows),
            by_head(grad_attended),
            log_totals,
        ),
    )
    grad_queries = grad_queries.reshape(row_count, local_width)
    grad_keys = grad_keys.reshape(row_count, local_width)
    grad_values = grad_values.reshape(row_count, local_width)
    grad_query_bias = jnp.sum(grad_queries, axis=0, dtype=jnp.float32)
    grad_value_bias = jnp.sum(grad_values, axis=0, dtype=jnp.float32)
    grad_query_weight = inner_rows(flat_attn, grad_queries)
    grad_key_weight = inner_rows(flat_attn, grad_keys)
    grad_value_weight = inner_rows(flat_attn, grad_values)
    partial_normed = (
        against(grad_queries, back_query)
        + against(grad_keys, back_key)
        + against(grad_values, back_value)
    )
    grad_normed_attn = fold_grads(partial_normed.reshape(images, length, model_width))
    _, attn_pull = jax.vjp(modulate_images, inputs, shift_attn, scale_attn)
    grad_inputs, grad_shift_attn, grad_scale_attn = attn_pull(grad_normed_attn)
    grad_tokens = grad_after + grad_inputs
    modulation_terms = jnp.concatenate(
        [
            grad_shift_attn,
            grad_scale_attn,
            grad_gate_attn,
            grad_shift_mlp,
            grad_scale_mlp,
            grad_gate_mlp,
        ],
        axis=1,
    )
    grad_modulation = lax.psum_scatter(
        modulation_terms, "tensor", scatter_dimension=1, tiled=True
    ).astype(jnp.bfloat16)
    grad_ada_bias = jnp.sum(grad_modulation, axis=0, dtype=jnp.float32)
    grad_ada_weight = inner_rows(lifted_low, grad_modulation)
    grad_lifted = lax.psum(against(grad_modulation, back_ada), "tensor")
    _, silu_pull = jax.vjp(jax.nn.silu, conditioning)
    grad_conditioning = silu_pull(grad_lifted)[0]
    weight_grads = (
        lax.psum_scatter(grad_query_weight, "dp", scatter_dimension=0, tiled=True),
        lax.psum_scatter(grad_key_weight, "dp", scatter_dimension=0, tiled=True),
        lax.psum_scatter(grad_value_weight, "dp", scatter_dimension=0, tiled=True),
        lax.psum_scatter(grad_out_weight, "dp", scatter_dimension=1, tiled=True),
        lax.psum_scatter(grad_up_weight, "dp", scatter_dimension=0, tiled=True),
        lax.psum_scatter(grad_down_weight, "dp", scatter_dimension=1, tiled=True),
        lax.psum_scatter(grad_ada_weight, "dp", scatter_dimension=0, tiled=True),
    )
    bias_grads = lax.psum(
        (
            grad_query_bias,
            grad_value_bias,
            grad_out_bias,
            grad_up_bias,
            grad_down_bias,
            grad_ada_bias,
        ),
        "dp",
    )
    limit = threshold[0]
    factor = jnp.sqrt(limit / jnp.maximum(peaks, limit))
    column_factor = jnp.repeat(factor, HEAD_DIM)
    query_clipped = (query_weight.astype(jnp.float32) * column_factor).astype(jnp.bfloat16)
    key_clipped = (key_weight.astype(jnp.float32) * column_factor).astype(jnp.bfloat16)
    query_bias_clipped = query_bias * column_factor
    return (
        block_out,
        grad_tokens,
        grad_conditioning,
        weight_grads[0],
        weight_grads[1],
        weight_grads[2],
        weight_grads[3],
        weight_grads[4],
        weight_grads[5],
        weight_grads[6],
        bias_grads[0],
        bias_grads[1],
        bias_grads[2],
        bias_grads[3],
        bias_grads[4],
        bias_grads[5],
        query_clipped,
        key_clipped,
        query_bias_clipped,
    )


def one_image_per_chip(
    tokens, conditioning, cotangent, query_weight, key_weight, value_weight, out_weight, up_weight,
    down_weight, ada_weight, query_bias, value_bias, out_bias, up_bias, down_bias, ada_bias, threshold,
):
    y, x, c, z = (lax.axis_index(a) for a in AXES)
    batch = 4 * y + 2 * x + c
    first = jnp.concatenate([query_weight, key_weight, value_weight, out_weight.T], axis=1)
    shard = jnp.stack([first, up_weight, down_weight.T])
    lift_own = jnp.pad(jax.nn.silu(conditioning).astype(bf).astype(f32), ((0, 6), (0, 0)))
    z_bias = jnp.concatenate([query_bias, value_bias, up_bias])[None]
    (
        full, own_tokens, own_cotangent, lifted_rows, vectors, biases, normed_attn, qkv, mate_kv, attended, totals,
        peak, branch_attn, normed_mlp, active, slope, grad_down,
    ) = forward(shard, tokens, cotangent, lift_own, ada_weight, ada_bias[None], z_bias, out_bias[None])
    sums, block_rows, token_rows, _, _, _, grad_ada_weight, grad_ada_bias, lifted, totals = backward(
        full, own_tokens, own_cotangent, normed_attn, normed_mlp, qkv, mate_kv, attended, totals, peak, branch_attn,
        active, slope, grad_down, vectors, lifted_rows, ada_weight, down_bias[None],
    )
    own_lifted = lax.dynamic_slice(lifted.reshape(8, 16, ROWS), (0, 2 * batch, 0), (8, 2, ROWS))
    own_lifted = jnp.swapaxes(own_lifted, 0, 1).reshape(2, 8 * ROWS)
    _, silu_pull = jax.vjp(jax.nn.silu, conditioning)
    grad_conditioning = silu_pull(own_lifted)[0]
    first_bias = lax.dynamic_slice(totals, (z, 0), (1, COLS))[0]
    grad_query_bias = first_bias[:HS]
    grad_value_bias = first_bias[2 * HS : 3 * HS]
    grad_up_bias = lax.dynamic_slice(totals, (4 + z, 0), (1, COLS))[0]
    grad_out_bias = totals[8, :COLS]
    grad_down_bias = totals[9, :COLS]
    grad_ada_bias = grad_ada_bias[0]
    limit = threshold[0]
    peaks = lax.dynamic_slice(totals[:, COLS], (4 * z,), (4,))
    factor = jnp.sqrt(limit / jnp.maximum(peaks, limit))
    column_factor = jnp.repeat(factor, HEAD_DIM)
    query_clipped = (query_weight.astype(f32) * column_factor).astype(bf)
    key_clipped = (key_weight.astype(f32) * column_factor).astype(bf)
    return (
        block_rows,
        token_rows.astype(f32),
        grad_conditioning,
        sums[0, :, :HS],
        sums[0, :, HS : 2 * HS],
        sums[0, :, 2 * HS : 3 * HS],
        sums[0, :, 3 * HS :].T,
        sums[1],
        sums[2].T,
        grad_ada_weight,
        grad_query_bias,
        grad_value_bias,
        grad_out_bias,
        grad_up_bias,
        grad_down_bias,
        grad_ada_bias,
        query_clipped,
        key_clipped,
        query_bias * column_factor,
    )


def solution(mesh):
    if dict(mesh.shape) == {"dp": 8, "tensor": 4}:
        mesh = Mesh(mesh.devices.reshape(2, 2, 2, 4), AXES)
        split, heads, body = ("y", "x", "core"), "z", one_image_per_chip
    else:
        split, heads, body = "dp", "tensor", local
    weight, turned, bias = P(split, heads), P(heads, split), P(heads)
    rows = P(split, heads, None)
    in_specs = (
        rows, P(split, None), rows, weight, weight, weight, turned, weight, turned, weight,
        bias, bias, P(), bias, P(), bias, P(),
    )
    out_specs = (
        rows, rows, P(split, None), weight, weight, weight, turned, weight, turned, weight,
        bias, bias, P(), bias, P(), bias, weight, weight, bias,
    )
    return jax.shard_map(body, mesh=mesh, in_specs=in_specs, out_specs=out_specs, check_vma=False)
```
